32 devices in a mesh: rep: 16 (over z, y, x), fsdp: 2 (over core).
Axes of the slice: x: 2, y: 2, z: 4, core: 2. Of those that a mesh axis runs over, the one named last changes fastest.
Arguments:
- tokens: bfloat16 [32, 1024, 768], P('rep', 'fsdp'), may hold values from -6 to 6
- lengths: int32 [32, 8], P('rep'), may hold values from 1 to 1017, as said below
- w_qkv: bfloat16 [768, 2304], P('fsdp'), may hold values from -0.21875 to 0.21875
- w_out: bfloat16 [768, 768], P('fsdp'), may hold values from -1.75 to 1.75
- w_gate: bfloat16 [768, 3072], P('fsdp'), may hold values from -0.21875 to 0.21875
- w_up: bfloat16 [768, 3072], P('fsdp'), may hold values from -0.21875 to 0.21875
- w_down: bfloat16 [3072, 768], P('fsdp'), may hold values from -0.109375 to 0.109375
- norm1_gain: bfloat16 [768], P('fsdp'), may hold values from 0.5 to 1.5
- norm1_bias: bfloat16 [768], P('fsdp'), may hold values from -2 to 2
- norm2_gain: bfloat16 [768], P('fsdp'), may hold values from 0.5 to 1.5
- norm2_bias: bfloat16 [768], P('fsdp'), may hold values from -2 to 2
- cotangent: bfloat16 [32, 1024, 768], P('rep', 'fsdp'), may hold values from -6 to 6
Outputs:
- activations: bfloat16 [32, 1024, 768], P('rep', 'fsdp')
- input_grad: float32 [32, 1024, 768], P('rep', 'fsdp')
- qkv_grad: float32 [768, 2304], P('fsdp')
- out_grad: float32 [768, 768], P('fsdp')
- gate_grad: float32 [768, 3072], P('fsdp')
- up_grad: float32 [768, 3072], P('fsdp')
- down_grad: float32 [3072, 768], P('fsdp')
- gain_one_grad: float32 [768], P('fsdp')
- bias_one_grad: float32 [768], P('fsdp')
- gain_two_grad: float32 [768], P('fsdp')
- bias_two_grad: float32 [768], P('fsdp')
The draws below stay inside these ranges and needn't reach their ends.
Inputs may be any that keep to these rules, and one draw needn't show every extreme that they name: Each row of 8 lengths sums to 1024; in each row the document that holds position 512 begins before position 256 and ends after position 768.
All inputs are finite; a program needn't handle non-finite values.
Results may differ from the reference program's by a relative error of at most 0.014.
Values may be sent and summed in bfloat16 or wider, within the bound.
A program may use at most 256 MiB of HBM per device.

```python
import jax
import jax.numpy as jnp
from jax import lax

D = 768
HEADS = 12
HEAD_DIM = 64
FF = 3072
DOCS = 8
LEN = 1024
SEQS = 32


def draw_lengths(key, part):
    key = jax.random.fold_in(key, 7)
    row_key_base, pick_key = jax.random.split(key)
    widest_row = jax.random.randint(pick_key, (), 0, SEQS).astype(jnp.int32)
    lower_count = (DOCS - 1) // 2
    upper_count = DOCS - 1 - lower_count
    packed_cuts = jnp.concatenate([jnp.arange(1, lower_count + 1, dtype=jnp.int32), jnp.arange(LEN - upper_count, LEN, dtype=jnp.int32)])

    def one_row(row_key, row_number):
        lower = jnp.arange(1, LEN // 4, dtype=jnp.int32)
        upper = jnp.arange(3 * LEN // 4 + 1, LEN, dtype=jnp.int32)
        candidates = jnp.concatenate([lower, upper])
        picked = jax.random.permutation(row_key, candidates)[:DOCS - 1]
        cuts = jnp.sort(picked).astype(jnp.int32)
        cuts = jnp.where(row_number == widest_row, packed_cuts, cuts).astype(jnp.int32)
        bounds = jnp.concatenate([jnp.zeros((1,), jnp.int32), cuts, jnp.full((1,), LEN, jnp.int32)])
        return (bounds[1:] - bounds[:-1]).astype(jnp.int32)
    row_keys = jax.random.split(row_key_base, SEQS)
    return jax.vmap(one_row)(row_keys, jnp.arange(SEQS, dtype=jnp.int32))


def levels(key, dims, cuts, low, top_value):
    def one(axis_at, blocks):
        heights = jax.random.uniform(jax.random.fold_in(jax.random.fold_in(key, 6), axis_at), (blocks,), jnp.float32, low / len(cuts), top_value / len(cuts))
        return jnp.repeat(jnp.exp(heights), dims[axis_at] // blocks).reshape((-1,) + (1,) * (len(dims) - axis_at - 1))

    gain = one(*cuts[0])
    for cut in cuts[1:]:
        gain = gain * one(*cut)
    return gain


def noise(own_key, shape, scale, most, cuts=(), held_as=jnp.bfloat16):
    entries = jax.random.normal(own_key, shape, jnp.float32) * scale
    if len(cuts) > 0:
        entries = levels(own_key, shape, cuts, -0.22, 0.18) * entries
    return jnp.clip(entries, min=-most, max=most).astype(held_as)


def setup_inputs(seed: int = 0) -> dict:
    keys = jax.random.split(jax.random.key(seed), 13)
    tokens = noise(keys[0], (SEQS, LEN, D), 1.0, 6.0, ((0, 16), (1, 2)))
    lengths = draw_lengths(jax.random.fold_in(keys[12], 71), 0)
    w_qkv = noise(keys[2], (D, 3 * D), D ** -0.5, 0.21875, ((0, 2),))
    w_out = noise(keys[3], (D, D), (D // 64) ** -0.5, 1.75, ((0, 2),))
    w_gate = noise(keys[4], (D, FF), D ** -0.5, 0.21875, ((0, 2),))
    w_up = noise(keys[5], (D, FF), D ** -0.5, 0.21875, ((0, 2),))
    w_down = noise(keys[6], (FF, D), FF ** -0.5, 0.109375, ((0, 2),))
    norm1_gain = jnp.clip(1.0 + 0.1 * jax.random.normal(keys[7], (D,), jnp.float32), 0.5, 1.5).astype(jnp.bfloat16)
    norm1_bias = noise(keys[8], (D,), 0.3, 2.0, ((0, 2),))
    norm2_gain = jnp.clip(1.0 + 0.1 * jax.random.normal(keys[9], (D,), jnp.float32), 0.5, 1.5).astype(jnp.bfloat16)
    norm2_bias = noise(keys[10], (D,), 0.3, 2.0, ((0, 2),))
    cotangent = noise(keys[11], (SEQS, LEN, D), 1.0, 6.0, ((0, 16), (1, 2)))
    return {"tokens": tokens, "lengths": lengths, "w_qkv": w_qkv, "w_out": w_out, "w_gate": w_gate, "w_up": w_up, "w_down": w_down, "norm1_gain": norm1_gain, "norm1_bias": norm1_bias, "norm2_gain": norm2_gain, "norm2_bias": norm2_bias, "cotangent": cotangent}


@jax.custom_vjp
def low(v):
    return lax.optimization_barrier(v.astype(jnp.bfloat16)).astype(jnp.float32)

@jax.custom_vjp
def low_back(v):
    return v

def low_keep(v):
    return (low(v), None)

def low_pass(kept, grad):
    return (grad,)

def back_keep(v):
    return (v, None)

def back_low(kept, grad):
    return (low(grad),)
low.defvjp(low_keep, low_pass)
low_back.defvjp(back_keep, back_low)
EPSILON = 1e-05

def matmul(left_side, right_side):
    return jnp.dot(left_side, right_side, precision=lax.Precision.HIGHEST, preferred_element_type=jnp.float32)

def doc_tables(doc_lengths, seq_len):
    doc_ends = jnp.cumsum(doc_lengths).astype(jnp.int32)
    doc_starts = (doc_ends - doc_lengths).astype(jnp.int32)
    places = jnp.arange(seq_len, dtype=jnp.int32)
    segment = lax.optimization_barrier(jnp.sum((places[:, None] >= doc_ends[None, :]).astype(jnp.int32), axis=1)).astype(jnp.int32)
    member = segment[:, None] == jnp.arange(doc_lengths.shape[0], dtype=jnp.int32)[None, :]
    begins = lax.optimization_barrier(jnp.sum(jnp.where(member, doc_starts[None, :], 0), axis=1)).astype(jnp.int32)
    return (segment, (places - begins).astype(jnp.int32))

def rope_tables(positions):
    half_dim = HEAD_DIM // 2
    frequencies = 1000.0 ** (-2.0 * jnp.arange(half_dim, dtype=jnp.float32) / HEAD_DIM)
    angles = positions.astype(jnp.float32)[:, None] * frequencies[None, :]
    return (jnp.cos(angles), jnp.sin(angles))

def rotate(values, cosine_table, sine_table):
    row_count = values.shape[0]
    split_heads = values.reshape(row_count, HEADS, HEAD_DIM)
    first_half = split_heads[..., :HEAD_DIM // 2]
    second_half = split_heads[..., HEAD_DIM // 2:]
    cosine_rows = cosine_table[:, None, :]
    sine_rows = sine_table[:, None, :]
    turned = jnp.concatenate([first_half * cosine_rows - second_half * sine_rows, second_half * cosine_rows + first_half * sine_rows], axis=-1)
    return turned.reshape(row_count, HEADS * HEAD_DIM)

def layer_norm(values, gain_vec, bias_vec):
    centre = values - lax.optimization_barrier(jnp.mean(values, axis=-1, keepdims=True))
    inv_std = lax.rsqrt(lax.optimization_barrier(jnp.mean(centre * centre, axis=-1, keepdims=True)) + EPSILON)
    return centre * inv_std * gain_vec + bias_vec

def block(stream, parameters, segment, cosine_table, sine_table):
    w_qkv, w_out, w_gate, w_up, w_down, gain_one, bias_one, gain_two, bias_two = parameters
    model_width = HEADS * HEAD_DIM
    row_count = stream.shape[0]
    projected = low_back(matmul(stream, w_qkv))
    queries = low(rotate(projected[:, :model_width], cosine_table, sine_table))
    key_rows = low(rotate(projected[:, model_width:2 * model_width], cosine_table, sine_table))
    value_rows = low(projected[:, 2 * model_width:])
    query_heads = queries.reshape(row_count, HEADS, HEAD_DIM)
    key_heads = key_rows.reshape(row_count, HEADS, HEAD_DIM)
    value_heads = value_rows.reshape(row_count, HEADS, HEAD_DIM)
    raw_scores = low_back(jnp.einsum('qhd,khd->hqk', query_heads, key_heads, precision=lax.Precision.HIGHEST))
    same_doc = segment[:, None] == segment[None, :]
    scores = jnp.where(same_doc[None], raw_scores * HEAD_DIM ** (-0.5), -1e+30)
    row_max = lax.optimization_barrier(jnp.max(scores, axis=-1, keepdims=True))
    exp_scores = jnp.exp(scores - row_max)
    attn_probs = low(exp_scores / lax.optimization_barrier(jnp.sum(exp_scores, axis=-1, keepdims=True)))
    context = jnp.einsum('hqk,khd->qhd', attn_probs, value_heads, precision=lax.Precision.HIGHEST)
    context = low(low_back(context.reshape(row_count, model_width)))
    attended = low_back(matmul(context, w_out))
    normed = layer_norm(stream + attended, gain_one, bias_one)
    normed_low = low(normed)
    gate_act = low_back(matmul(normed_low, w_gate))
    up_act = low_back(matmul(normed_low, w_up))
    hidden = low(jax.nn.silu(gate_act) * up_act)
    mixed = low_back(matmul(hidden, w_down))
    return layer_norm(normed + mixed, gain_two, bias_two)

def reference(tokens, lengths, w_qkv, w_out, w_gate, w_up, w_down, norm1_gain, norm1_bias, norm2_gain, norm2_bias, cotangent):
    parameters = tuple((operand.astype(jnp.float32) for operand in (w_qkv, w_out, w_gate, w_up, w_down, norm1_gain, norm1_bias, norm2_gain, norm2_bias)))

    def one_sequence(totals, entry):
        stream, doc_lengths, grad_out = entry
        segment, positions = doc_tables(doc_lengths, LEN)
        cosine_table, sine_table = rope_tables(positions)

        def forward(values, weights):
            return block(values, weights, segment, cosine_table, sine_table)
        result, pull = jax.vjp(forward, stream.astype(jnp.float32), parameters)
        grad_in, grads = pull(grad_out.astype(jnp.float32))
        totals = tuple((total + term for total, term in zip(totals, grads)))
        return (totals, (result.astype(jnp.bfloat16), grad_in))
    zeros = tuple((jnp.zeros_like(operand) for operand in parameters))
    totals, (outputs, input_grad) = lax.scan(one_sequence, zeros, (tokens, lengths, cotangent))
    return (outputs, input_grad, totals[0], totals[1], totals[2], totals[3], totals[4], totals[5], totals[6], totals[7], totals[8])
```

```python
import jax
import jax.numpy as jnp
from jax import lax
from jax.experimental import pallas as pl
from jax.experimental.pallas import tpu as pltpu
from jax.sharding import PartitionSpec as P

HEADS = 12
HEAD_DIM = 64


EPSILON = 1e-05


def doc_tables(doc_lengths, seq_len):
    doc_ends = jnp.cumsum(doc_lengths)
    doc_starts = doc_ends - doc_lengths
    places = jnp.arange(seq_len, dtype=jnp.int32)
    segment = jnp.sum((places[:, None] >= doc_ends[None, :]).astype(jnp.int32), axis=1)
    member = segment[:, None] == jnp.arange(doc_lengths.shape[0], dtype=jnp.int32)[None, :]
    begins = jnp.sum(jnp.where(member, doc_starts[None, :], 0), axis=1)
    return (segment, places - begins)


def rope_tables(positions):
    half_dim = HEAD_DIM // 2
    frequencies = 1000.0 ** (-2.0 * jnp.arange(half_dim, dtype=jnp.float32) / HEAD_DIM)
    angles = positions.astype(jnp.float32)[:, None] * frequencies[None, :]
    return (jnp.cos(angles), jnp.sin(angles))


def rotate(values, cosine_table, sine_table):
    row_count = values.shape[0]
    split_heads = values.reshape(row_count, HEADS, HEAD_DIM)
    first_half = split_heads[..., : HEAD_DIM // 2]
    second_half = split_heads[..., HEAD_DIM // 2 :]
    cosine_rows = cosine_table[:, None, :]
    sine_rows = sine_table[:, None, :]
    turned = jnp.concatenate(
        [
            first_half * cosine_rows - second_half * sine_rows,
            second_half * cosine_rows + first_half * sine_rows,
        ],
        axis=-1,
    )
    return turned.reshape(row_count, HEADS * HEAD_DIM)


def norm_forward(values, gain_vec, bias_vec):
    centre = values - jnp.mean(values, axis=-1, keepdims=True)
    inv_std = lax.rsqrt(jnp.mean(centre * centre, axis=-1, keepdims=True) + EPSILON)
    unit_rows = centre * inv_std
    return (unit_rows * gain_vec + bias_vec, unit_rows, inv_std)


def norm_back(grad_norm, unit_rows, inv_std):
    return inv_std * (
        grad_norm
        - jnp.mean(grad_norm, axis=-1, keepdims=True)
        - unit_rows * jnp.mean(grad_norm * unit_rows, axis=-1, keepdims=True)
    )


def heads_of(values):
    return values.reshape(values.shape[0], HEADS, HEAD_DIM)


def product(left_side, right_side):
    return jnp.dot(left_side, right_side, preferred_element_type=jnp.float32)


def product_left_t(left_side, right_side):
    return lax.dot_general(
        left_side, right_side, (((0,), (0,)), ((), ())), preferred_element_type=jnp.float32
    )


def product_right_t(left_side, right_side):
    return lax.dot_general(
        left_side, right_side, (((1,), (1,)), ((), ())), preferred_element_type=jnp.float32
    )


def masked_scores(query_heads, key_heads, same_doc, score_scale):
    raw_scores = jnp.einsum(
        "qhd,khd->hqk", query_heads, key_heads, preferred_element_type=jnp.float32
    )
    return jnp.where(same_doc[None], raw_scores * score_scale, -1e30)


CHUNKS = 16
PARTS = 3
PART_ROWS = 128
UNITS = 16
STEPS = 4
MESH = pl.DeviceIdType.MESH
BF16 = jnp.bfloat16
F32 = jnp.float32


def bit_of(value, weight):
    return lax.rem(lax.div(value, weight), 2)


def orders(chunk):
    rep = lax.axis_index("rep")
    odd = lax.rem(chunk, 2)
    first, second = 1 + odd, 2 - odd
    bits = {1: bit_of(rep, 1), 2: bit_of(rep, 2), 4: bit_of(rep, 4), 8: bit_of(rep, 8)}
    first_bit = bits[1] * (1 - odd) + bits[2] * odd
    second_bit = bits[2] * (1 - odd) + bits[1] * odd
    return (
        ((1, bits[1]), (2, bits[2]), (4, bits[4]), (8, bits[8])),
        ((2, bits[2]), (1, bits[1]), (4, bits[4]), (8, bits[8])),
        ((4, bits[4]), (first, first_bit), (second, second_bit), (8, bits[8])),
    )


def partner_of(weight, bit):
    return (lax.axis_index("rep") + weight * (1 - 2 * bit), lax.axis_index("fsdp"))


def other_core():
    return (lax.axis_index("rep"), 1 - lax.axis_index("fsdp"))


def region(ref, chunk, part, order, level, flip):
    rows = PART_ROWS >> min(level, STEPS - 1)
    start = part * PART_ROWS
    for step in range(level):
        bit = order[step][1]
        if flip and step == level - 1:
            bit = 1 - bit
        if step < STEPS - 1:
            start = start + bit * (PART_ROWS >> (step + 1))
        else:
            column = bit * (ref.shape[2] // 2)
    start = pl.multiple_of(start, 16)
    if level < STEPS:
        return (chunk, pl.ds(start, rows), slice(None))
    half = ref.shape[2] // 2
    return (chunk, pl.ds(start, rows), pl.ds(pl.multiple_of(column, 128), half))


def landing(ref, chunk, part, step):
    start = part * PART_ROWS + PART_ROWS - (PART_ROWS >> step)
    if step < STEPS - 1:
        return (chunk, pl.ds(start, PART_ROWS >> (step + 1)), slice(None))
    return (chunk, pl.ds(start, PART_ROWS >> step), pl.ds(0, ref.shape[2] // 2))


def halving_copy(refs, chunk, part, order, step):
    grads, halves, _, send_sems, recv_sems = refs
    return pltpu.make_async_remote_copy(
        src_ref=grads.at[region(grads, chunk, part, order, step + 1, True)],
        dst_ref=halves.at[landing(halves, chunk, part, step)],
        send_sem=send_sems.at[chunk, part, step],
        recv_sem=recv_sems.at[chunk, part, step],
        device_id=partner_of(*order[step]),
        device_id_type=MESH,
    )


def halving_add(refs, chunk, part, order, step):
    grads, halves = refs[:2]
    kept = region(grads, chunk, part, order, step + 1, False)
    theirs = halves[landing(halves, chunk, part, step)]
    grads[kept] = (grads[kept].astype(F32) + theirs.astype(F32)).astype(BF16)


def settle_copy(refs, chunk, part, order):
    grads, _, out, send_sems, _ = refs
    mine = region(grads, chunk, part, order, STEPS, False)
    return pltpu.make_async_copy(grads.at[mine], out.at[mine], send_sems.at[chunk, part, 2 * STEPS])


def doubling_copy(refs, chunk, part, order, step):
    _, _, out, send_sems, recv_sems = refs
    there = out.at[region(out, chunk, part, order, step + 1, False)]
    return pltpu.make_async_remote_copy(
        src_ref=there,
        dst_ref=there,
        send_sem=send_sems.at[chunk, part, STEPS + step],
        recv_sem=recv_sems.at[chunk, part, STEPS + step],
        device_id=partner_of(*order[step]),
        device_id_type=MESH,
    )


def rep_stage(refs, chunk, stage):
    for part, order in enumerate(orders(chunk)):
        if 1 <= stage <= STEPS:
            halving_copy(refs, chunk, part, order, stage - 1).wait()
            halving_add(refs, chunk, part, order, stage - 1)
        if stage > STEPS:
            doubling_copy(refs, chunk, part, order, 2 * STEPS - stage).wait()
        if stage < STEPS:
            halving_copy(refs, chunk, part, order, stage).start()
        elif stage < 2 * STEPS:
            if stage == STEPS:
                settle = settle_copy(refs, chunk, part, order)
                settle.start()
                settle.wait()
            doubling_copy(refs, chunk, part, order, 2 * STEPS - 1 - stage).start()


def greet():
    rep = lax.axis_index("rep")
    barrier = pltpu.get_barrier_semaphore()
    pl.semaphore_signal(barrier, inc=1, device_id=other_core(), device_id_type=MESH)
    for weight in (1, 2, 4, 8):
        there = partner_of(weight, bit_of(rep, weight))
        pl.semaphore_signal(barrier, inc=1, device_id=there, device_id_type=MESH)
    pl.semaphore_wait(barrier, 5)


def vector_copy(vectors, send_sems, recv_sems, step):
    rep = lax.axis_index("rep")
    if step == 0:
        there = other_core()
    else:
        weight = 1 << (step - 1)
        there = partner_of(weight, bit_of(rep, weight))
    return pltpu.make_async_remote_copy(
        src_ref=vectors.at[2 * step],
        dst_ref=vectors.at[2 * step + 1],
        send_sem=send_sems.at[step],
        recv_sem=recv_sems.at[step],
        device_id=there,
        device_id_type=MESH,
    )


VECTOR_STEPS = 5


def vector_stage(vectors, send_sems, recv_sems, stage):
    if stage > 0:
        vector_copy(vectors, send_sems, recv_sems, stage - 1).wait()
        vectors[2 * stage] = vectors[2 * stage - 2] + vectors[2 * stage - 1]
    if stage < VECTOR_STEPS:
        vector_copy(vectors, send_sems, recv_sems, stage).start()


def reduce_kernel(
    own, other, vec, out, vec_out, grads, halves, from_core, vectors,
    send_sems, recv_sems, core_send, core_recv, vec_send, vec_recv,
):
    refs = (grads, halves, out, send_sems, recv_sems)
    greet()
    vectors[0] = vec[...]

    def core_copy(chunk):
        return pltpu.make_async_remote_copy(
            src_ref=other.at[chunk],
            dst_ref=from_core.at[chunk],
            send_sem=core_send.at[chunk],
            recv_sem=core_recv.at[chunk],
            device_id=other_core(),
            device_id_type=MESH,
        )

    last = 2 * STEPS + 1

    def tick(t, carry):
        for stage in range(last, -1, -1):
            chunk = t - stage

            @pl.when((chunk >= 0) & (chunk < CHUNKS))
            def _():
                if stage == 0:
                    core_copy(chunk).start()
                if stage == 1:
                    core_copy(chunk).wait()
                    grads[chunk] = (own[chunk].astype(F32) + from_core[chunk].astype(F32)).astype(BF16)
                if stage >= 1:
                    rep_stage(refs, chunk, stage - 1)

        for stage in range(VECTOR_STEPS + 1):
            @pl.when(t == stage)
            def _():
                vector_stage(vectors, vec_send, vec_recv, stage)

        return carry

    lax.fori_loop(0, CHUNKS + last, tick, 0)
    vec_out[...] = vectors[2 * VECTOR_STEPS]


def all_reduce(own, other, vec):
    copies = pltpu.SemaphoreType.DMA
    return pl.pallas_call(
        reduce_kernel,
        out_shape=(jax.ShapeDtypeStruct(own.shape, BF16), jax.ShapeDtypeStruct(vec.shape, F32)),
        in_specs=[
            pl.BlockSpec(memory_space=pltpu.VMEM),
            pl.BlockSpec(memory_space=pl.ANY),
            pl.BlockSpec(memory_space=pltpu.VMEM),
        ],
        out_specs=(pl.BlockSpec(memory_space=pl.ANY), pl.BlockSpec(memory_space=pltpu.VMEM)),
        scratch_shapes=[
            pltpu.VMEM(own.shape, BF16),
            pltpu.VMEM(own.shape, BF16),
            pltpu.VMEM(own.shape, BF16),
            pltpu.VMEM((2 * VECTOR_STEPS + 1,) + vec.shape, F32),
            copies((CHUNKS, PARTS, 2 * STEPS + 1)),
            copies((CHUNKS, PARTS, 2 * STEPS)),
            copies((CHUNKS,)),
            copies((CHUNKS,)),
            copies((VECTOR_STEPS,)),
            copies((VECTOR_STEPS,)),
        ],
        compiler_params=pltpu.CompilerParams(collective_id=0, has_side_effects=True, vmem_limit_bytes=60 << 20),
    )(own, other, vec)


def to_sequence(block):
    return lax.all_to_all(block, "fsdp", split_axis=0, concat_axis=1, tiled=True)[0]


def to_positions(rows):
    return lax.all_to_all(rows[None], "fsdp", split_axis=1, concat_axis=0, tiled=True)


def row_halves(grad, core):
    rows, cols = grad.shape
    pieces = grad.reshape(2, rows // 768, 384, cols // 768, 768)
    pieces = jnp.moveaxis(pieces, 3, 1).reshape(2, -1, 384, 768).astype(BF16)
    return pieces


def shards(
    tokens,
    lengths,
    w_qkv,
    w_out,
    w_gate,
    w_up,
    w_down,
    norm1_gain,
    norm1_bias,
    norm2_gain,
    norm2_bias,
    cotangent,
):
    core = lax.axis_index("fsdp")
    stream = to_sequence(tokens)
    grad_out = to_sequence(cotangent).astype(F32)
    doc_lengths = lax.dynamic_index_in_dim(lengths, core, 0, keepdims=False)
    seq_len, model_width = stream.shape
    score_scale = HEAD_DIM ** (-0.5)

    def whole(block):
        return lax.all_gather(block, "fsdp", axis=0, tiled=True)

    w_qkv, w_out, w_gate, w_up, w_down = map(whole, (w_qkv, w_out, w_gate, w_up, w_down))
    vectors = whole(jnp.stack([norm1_gain, norm1_bias, norm2_gain, norm2_bias], axis=1)).astype(F32)
    gain_one, bias_one, gain_two, bias_two = (vectors[:, n] for n in range(4))
    stream_wide = stream.astype(F32)
    segment, positions = doc_tables(doc_lengths, seq_len)
    cosine_table, sine_table = rope_tables(positions)
    projected = product(stream, w_qkv)
    queries = rotate(projected[:, :model_width], cosine_table, sine_table).astype(BF16)
    key_rows = rotate(projected[:, model_width : 2 * model_width], cosine_table, sine_table).astype(BF16)
    value_rows = projected[:, 2 * model_width :].astype(BF16)
    same_doc = segment[:, None] == segment[None, :]
    scores = masked_scores(heads_of(queries), heads_of(key_rows), same_doc, score_scale)
    row_max = jnp.max(scores, axis=-1, keepdims=True)
    exp_scores = jnp.exp(scores - row_max)
    row_total = jnp.sum(exp_scores, axis=-1, keepdims=True)
    log_total = row_max + jnp.log(row_total)
    attn_low = (exp_scores / row_total).astype(BF16)
    context = jnp.einsum("hqk,khd->qhd", attn_low, heads_of(value_rows), preferred_element_type=F32)
    context = context.reshape(seq_len, model_width).astype(BF16)
    first_sum = stream_wide + product(context, w_out)
    normed, unit_one, inv_one = norm_forward(first_sum, gain_one, bias_one)
    normed_low = normed.astype(BF16)
    gate_act = product(normed_low, w_gate)
    up_act = product(normed_low, w_up)
    gate_sig = jax.nn.sigmoid(gate_act)
    gate_silu = gate_act * gate_sig
    hidden = (gate_silu * up_act).astype(BF16)
    second_sum = normed + product(hidden, w_down)
    result, unit_two, inv_two = norm_forward(second_sum, gain_two, bias_two)

    bias_two_grad = jnp.sum(grad_out, axis=0)
    gain_two_grad = jnp.sum(grad_out * unit_two, axis=0)
    grad_second = norm_back(grad_out * gain_two, unit_two, inv_two)
    grad_mixed = grad_second.astype(BF16)
    down_grad = product_left_t(hidden, grad_mixed)
    grad_hidden = product_right_t(grad_mixed, w_down)
    grad_gate_act = (grad_hidden * up_act * gate_sig * (1.0 + gate_act * (1.0 - gate_sig))).astype(BF16)
    grad_up_act = (grad_hidden * gate_silu).astype(BF16)
    gate_grad = product_left_t(normed_low, grad_gate_act)
    up_grad = product_left_t(normed_low, grad_up_act)
    grad_normed = grad_second + product_right_t(grad_gate_act, w_gate) + product_right_t(grad_up_act, w_up)
    bias_one_grad = jnp.sum(grad_normed, axis=0)
    gain_one_grad = jnp.sum(grad_normed * unit_one, axis=0)
    grad_first = norm_back(grad_normed * gain_one, unit_one, inv_one)
    grad_attended = grad_first.astype(BF16)
    out_grad = product_left_t(context, grad_attended)
    grad_context = product_right_t(grad_attended, w_out).astype(BF16)
    scores_again = masked_scores(heads_of(queries), heads_of(key_rows), same_doc, score_scale)
    attn_probs = jnp.exp(scores_again - log_total)
    context_heads = heads_of(grad_context)
    grad_probs = jnp.einsum("qhd,khd->hqk", context_heads, heads_of(value_rows), preferred_element_type=F32)
    grad_scores = (
        score_scale * attn_probs * (grad_probs - jnp.sum(attn_probs * grad_probs, axis=-1, keepdims=True))
    ).astype(BF16)
    grad_queries = jnp.einsum("hqk,khd->qhd", grad_scores, heads_of(key_rows), preferred_element_type=F32)
    grad_keys = jnp.einsum("hqk,qhd->khd", grad_scores, heads_of(queries), preferred_element_type=F32)
    grad_values = jnp.einsum("hqk,qhd->khd", attn_probs.astype(BF16), context_heads, preferred_element_type=F32)
    grad_projected = jnp.concatenate(
        [
            rotate(grad_queries.reshape(seq_len, model_width), cosine_table, -sine_table),
            rotate(grad_keys.reshape(seq_len, model_width), cosine_table, -sine_table),
            grad_values.reshape(seq_len, model_width),
        ],
        axis=1,
    ).astype(BF16)
    qkv_grad = product_left_t(stream, grad_projected)
    input_grad = grad_first + product_right_t(grad_projected, w_qkv)

    halves = [row_halves(grad, core) for grad in (down_grad, gate_grad, up_grad, out_grad, qkv_grad)]
    both = jnp.concatenate(halves, axis=1)
    own = lax.dynamic_index_in_dim(both, core, 0, keepdims=False)
    other = lax.dynamic_index_in_dim(both, 1 - core, 0, keepdims=False)
    zero = jnp.zeros_like(bias_one_grad)
    vec = jnp.stack([gain_one_grad, bias_one_grad, gain_two_grad, bias_two_grad, zero, zero, zero, zero])
    summed, vec_sum = all_reduce(own, other, vec)
    groups = lax.axis_size("rep") // UNITS
    if groups > 1:
        alike = [[UNITS * g + n for g in range(groups)] for n in range(UNITS)]
        summed = lax.psum(summed, "rep", axis_index_groups=alike)
        vec_sum = lax.psum(vec_sum, "rep", axis_index_groups=alike)
    summed = summed.astype(F32)

    def wide(first, count):
        return jnp.moveaxis(summed[first : first + count], 0, 1).reshape(384, -1)

    vec_own = lax.dynamic_slice_in_dim(vec_sum, core * 384, 384, axis=1)
    return (
        to_positions(result.astype(BF16)),
        to_positions(input_grad),
        wide(13, 3),
        wide(12, 1),
        wide(4, 4),
        wide(8, 4),
        summed[:4].reshape(-1, model_width),
        vec_own[0],
        vec_own[1],
        vec_own[2],
        vec_own[3],
    )


def solution(mesh):
    placed = (
        P("rep", "fsdp", None),
        P("rep", None),
        P("fsdp", None),
        P("fsdp", None),
        P("fsdp", None),
        P("fsdp", None),
        P("fsdp", None),
        P("fsdp"),
        P("fsdp"),
        P("fsdp"),
        P("fsdp"),
        P("rep", "fsdp", None),
    )
    return jax.shard_map(
        shards,
        mesh=mesh,
        in_specs=placed,
        out_specs=(
            P("rep", "fsdp", None),
            P("rep", "fsdp", None),
            P("fsdp", None),
            P("fsdp", None),
            P("fsdp", None),
            P("fsdp", None),
            P("fsdp", None),
            P("fsdp"),
            P("fsdp"),
            P("fsdp"),
            P("fsdp"),
        ),
        check_vma=False,
    )
```

```python
import jax
import jax.numpy as jnp
from jax import lax
from jax.experimental import pallas as pl
from jax.experimental.pallas import tpu as pltpu
from jax.sharding import PartitionSpec as P

HEADS = 12
HEAD_DIM = 64


EPSILON = 1e-05


def doc_tables(doc_lengths, seq_len):
    doc_ends = jnp.cumsum(doc_lengths)
    doc_starts = doc_ends - doc_lengths
    places = jnp.arange(seq_len, dtype=jnp.int32)
    segment = jnp.sum((places[:, None] >= doc_ends[None, :]).astype(jnp.int32), axis=1)
    member = segment[:, None] == jnp.arange(doc_lengths.shape[0], dtype=jnp.int32)[None, :]
    begins = jnp.sum(jnp.where(member, doc_starts[None, :], 0), axis=1)
    return (segment, places - begins)


def rope_tables(positions):
    half_dim = HEAD_DIM // 2
    frequencies = 1000.0 ** (-2.0 * jnp.arange(half_dim, dtype=jnp.float32) / HEAD_DIM)
    angles = positions.astype(jnp.float32)[:, None] * frequencies[None, :]
    return (jnp.cos(angles), jnp.sin(angles))


CHUNKS = 16
PARTS = 3
PART_ROWS = 128
UNITS = 16
STEPS = 4
MESH = pl.DeviceIdType.MESH
BF16 = jnp.bfloat16
F32 = jnp.float32


def bit_of(value, weight):
    return lax.rem(lax.div(value, weight), 2)


def orders(chunk):
    rep = lax.axis_index("rep")
    odd = lax.rem(chunk, 2)
    first, second = 1 + odd, 2 - odd
    bits = {1: bit_of(rep, 1), 2: bit_of(rep, 2), 4: bit_of(rep, 4), 8: bit_of(rep, 8)}
    first_bit = bits[1] * (1 - odd) + bits[2] * odd
    second_bit = bits[2] * (1 - odd) + bits[1] * odd
    return (
        ((1, bits[1]), (2, bits[2]), (4, bits[4]), (8, bits[8])),
        ((2, bits[2]), (1, bits[1]), (4, bits[4]), (8, bits[8])),
        ((4, bits[4]), (first, first_bit), (second, second_bit), (8, bits[8])),
    )


def partner_of(weight, bit):
    return (lax.axis_index("rep") + weight * (1 - 2 * bit), lax.axis_index("fsdp"))


def other_core():
    return (lax.axis_index("rep"), 1 - lax.axis_index("fsdp"))


def region(ref, chunk, part, order, level, flip):
    rows = PART_ROWS >> min(level, STEPS - 1)
    start = part * PART_ROWS
    for step in range(level):
        bit = order[step][1]
        if flip and step == level - 1:
            bit = 1 - bit
        if step < STEPS - 1:
            start = start + bit * (PART_ROWS >> (step + 1))
        else:
            column = bit * (ref.shape[2] // 2)
    start = pl.multiple_of(start, 16)
    if level < STEPS:
        return (chunk, pl.ds(start, rows), slice(None))
    half = ref.shape[2] // 2
    return (chunk, pl.ds(start, rows), pl.ds(pl.multiple_of(column, 128), half))


def landing(ref, chunk, part, step):
    start = part * PART_ROWS + PART_ROWS - (PART_ROWS >> step)
    chunk = lax.rem(chunk, ref.shape[0])
    if step < STEPS - 1:
        return (chunk, pl.ds(start, PART_ROWS >> (step + 1)), slice(None))
    return (chunk, pl.ds(start, PART_ROWS >> step), pl.ds(0, ref.shape[2] // 2))


def halving_copy(refs, chunk, part, order, step):
    grads, halves, _, send_sems, recv_sems = refs
    return pltpu.make_async_remote_copy(
        src_ref=grads.at[region(grads, chunk, part, order, step + 1, True)],
        dst_ref=halves.at[landing(halves, chunk, part, step)],
        send_sem=send_sems.at[chunk, part, step],
        recv_sem=recv_sems.at[chunk, part, step],
        device_id=partner_of(*order[step]),
        device_id_type=MESH,
    )


def halving_add(refs, chunk, part, order, step):
    grads, halves = refs[:2]
    kept = region(grads, chunk, part, order, step + 1, False)
    theirs = halves[landing(halves, chunk, part, step)]
    grads[kept] = (grads[kept].astype(F32) + theirs.astype(F32)).astype(BF16)


def settle_copy(refs, chunk, part, order):
    grads, _, out, send_sems, _ = refs
    mine = region(grads, chunk, part, order, STEPS, False)
    return pltpu.make_async_copy(grads.at[mine], out.at[mine], send_sems.at[chunk, part, 2 * STEPS])


def doubling_copy(refs, chunk, part, order, step):
    _, _, out, send_sems, recv_sems = refs
    there = out.at[region(out, chunk, part, order, step + 1, False)]
    return pltpu.make_async_remote_copy(
        src_ref=there,
        dst_ref=there,
        send_sem=send_sems.at[chunk, part, STEPS + step],
        recv_sem=recv_sems.at[chunk, part, STEPS + step],
        device_id=partner_of(*order[step]),
        device_id_type=MESH,
    )


def rep_stage(refs, chunk, stage):
    for part, order in enumerate(orders(chunk)):
        if 1 <= stage <= STEPS:
            halving_copy(refs, chunk, part, order, stage - 1).wait()
            halving_add(refs, chunk, part, order, stage - 1)
        if stage > STEPS:
            doubling_copy(refs, chunk, part, order, 2 * STEPS - stage).wait()
        if stage < STEPS:
            halving_copy(refs, chunk, part, order, stage).start()
        elif stage < 2 * STEPS:
            if stage == STEPS:
                settle = settle_copy(refs, chunk, part, order)
                settle.start()
                settle.wait()
            doubling_copy(refs, chunk, part, order, 2 * STEPS - 1 - stage).start()


def greet():
    rep = lax.axis_index("rep")
    barrier = pltpu.get_barrier_semaphore()
    pl.semaphore_signal(barrier, inc=1, device_id=other_core(), device_id_type=MESH)
    for weight in (1, 2, 4, 8):
        there = partner_of(weight, bit_of(rep, weight))
        pl.semaphore_signal(barrier, inc=1, device_id=there, device_id_type=MESH)
    pl.semaphore_wait(barrier, 5)


def vector_copy(vectors, send_sems, recv_sems, step):
    rep = lax.axis_index("rep")
    if step == 0:
        there = other_core()
    else:
        weight = 1 << (step - 1)
        there = partner_of(weight, bit_of(rep, weight))
    return pltpu.make_async_remote_copy(
        src_ref=vectors.at[2 * step],
        dst_ref=vectors.at[2 * step + 1],
        send_sem=send_sems.at[step],
        recv_sem=recv_sems.at[step],
        device_id=there,
        device_id_type=MESH,
    )


VECTOR_STEPS = 5


def vector_stage(vectors, send_sems, recv_sems, stage):
    if stage > 0:
        vector_copy(vectors, send_sems, recv_sems, stage - 1).wait()
        vectors[2 * stage] = vectors[2 * stage - 2] + vectors[2 * stage - 1]
    if stage < VECTOR_STEPS:
        vector_copy(vectors, send_sems, recv_sems, stage).start()


SEQ_ROWS = 512
NEG = -1e30
FEATURES = 128
SPLIT_LANE = 8


def nn(left, right):
    return jnp.dot(left, right, preferred_element_type=F32)


def nt(left, right):
    return lax.dot_general(left, right, (((1,), (1,)), ((), ())), preferred_element_type=F32)


def tn(left, right):
    return lax.dot_general(left, right, (((0,), (0,)), ((), ())), preferred_element_type=F32)


def aligned(start, size, multiple=None):
    return pl.ds(pl.multiple_of(start, multiple or size), size)


def lanes():
    return lax.broadcasted_iota(jnp.int32, (1, 128), 1)


def head_mask(values, first):
    low = lanes() < HEAD_DIM
    zero = jnp.zeros_like(values)
    return jnp.where(low, values, zero) if first else jnp.where(low, zero, values)


def turn(values, cosines, sines):
    first = lax.rem(lanes(), HEAD_DIM) < HEAD_DIM // 2
    swapped = jnp.where(first, pltpu.roll(values, 96, 1), pltpu.roll(values, 32, 1))
    return values * cosines + swapped * sines


def split_lanes(base, values):
    high = values.astype(BF16).astype(F32)
    middle = (values - high).astype(BF16).astype(F32)
    low = values - high - middle
    lane = lanes()
    out = jnp.where(lane == SPLIT_LANE, high, base)
    out = jnp.where(lane == SPLIT_LANE + 1, middle, out)
    return jnp.where(lane == SPLIT_LANE + 2, low, out).astype(BF16)


def row_mean(values):
    return jnp.mean(values, axis=1, keepdims=True)


def forward_kernel(
    tokens, cotangent, w_qkv, w_out, w_gate, w_up, w_down, norms, query_marks, key_marks, cosines, sines,
    q_out, k_out, v_out, context_out, features_out, low_out, unit_out, inv_out, slope_gate_out, slope_up_out,
    hidden_out, grad_second_out, mixed_out, activations_out, vec_out,
    norms_out, wq_out, wo_out, wg_out, wu_out, wd_out,
    x, g, wq, wo, wg, wu, wd, nv, qs, ks, vs, ctx, total, low, key_aug, value_aug, pieces, acts, seconds,
    send_sems, recv_sems, own_sems, save_sems, act_sems,
):
    rep = lax.axis_index("rep")
    core = lax.axis_index("fsdp")
    there = (rep, 1 - core)
    seq, width = x.shape
    half = seq // 2

    barrier = pltpu.get_barrier_semaphore()
    pl.semaphore_signal(barrier, inc=1, device_id=there, device_id_type=MESH)
    pl.semaphore_wait(barrier, 1)

    def rows_of(ref, block):
        return ref.at[aligned(core * block, block)]

    exchanges = (
        (tokens.at[core], tokens.at[1 - core], rows_of(x, half)),
        (w_qkv, w_qkv, rows_of(wq, w_qkv.shape[0])),
        (w_out, w_out, rows_of(wo, w_out.shape[0])),
        (norms, norms, nv.at[core]),
        (w_gate, w_gate, rows_of(wg, w_gate.shape[0])),
        (w_up, w_up, rows_of(wu, w_up.shape[0])),
        (w_down, w_down, rows_of(wd, w_down.shape[0])),
        (cotangent.at[core], cotangent.at[1 - core], rows_of(g, half)),
    )

    def copies(number):
        mine, theirs, place = exchanges[number]
        return (
            pltpu.make_async_copy(mine, place, own_sems.at[number]),
            pltpu.make_async_remote_copy(
                src_ref=theirs,
                dst_ref=place,
                send_sem=send_sems.at[number],
                recv_sem=recv_sems.at[number],
                device_id=there,
                device_id_type=MESH,
            ),
        )

    for number in range(len(exchanges)):
        for copy in copies(number):
            copy.start()

    def arrived(number):
        for copy in copies(number):
            copy.wait()

    def save(source, target, number):
        copy = pltpu.make_async_copy(source, target, save_sems.at[number])
        copy.start()
        return copy

    arrived(0)
    arrived(1)
    tile = 512
    for n, out in enumerate((qs, ks, vs)):
        for r in range(seq // tile):
            rows = pl.ds(r * tile, tile)
            product_rows = nn(x[rows, :], wq[:, pl.ds(n * width, width)])
            if n == 2:
                out[rows, :] = product_rows.astype(BF16)
                continue
            for pair in range(width // 128):
                cols = slice(pair * 128, pair * 128 + 128)
                turned = turn(product_rows[:, cols], cosines[rows, :], sines[rows, :]).astype(BF16)
                if n == 0:
                    turned = turned * jnp.asarray(HEAD_DIM ** (-0.5), BF16)
                out[rows, cols] = turned
    saves = {0: save(qs, q_out, 0), 1: save(ks, k_out, 1), 2: save(vs, v_out, 2)}

    saves[7] = save(wq, wq_out, 7)

    block = 256
    steps = [(a, r) for r in range(seq // block) for a in range(2)]

    def pair_step(pair, carry):
        cols = aligned(pair * 128, 128)
        key_aug[:, :128] = ks[:, cols]
        key_aug[:, 128:] = key_marks[...]
        for a in range(2):
            value_aug[a, :, :128] = head_mask(vs[:, cols], a == 0)
            value_aug[a, :, 128:] = jnp.ones((seq, 128), BF16)

        def scores_of(a, r):
            rows = pl.ds(r * block, block)
            query = jnp.concatenate([head_mask(qs[rows, cols], a == 0), query_marks[rows, :]], axis=1)
            return nt(query, key_aug[...])

        scores = scores_of(*steps[0])
        parts = [None, None]
        for number, (a, r) in enumerate(steps):
            rows = pl.ds(r * block, block)
            upcoming = scores_of(*steps[number + 1]) if number + 1 < len(steps) else None
            row_max = jnp.max(scores, axis=1, keepdims=True)
            probs = jnp.exp(scores - row_max).astype(BF16)
            summed = nn(probs, value_aug[a])
            row_total = summed[:, 128:]
            parts[a] = summed[:, :128] / row_total
            lse = row_max + jnp.log(row_total)
            features_out[2 * pair + a, rows, :] = split_lanes(query_marks[rows, :].astype(F32), -lse)
            if a == 1:
                ctx[rows, cols] = (parts[0] + parts[1]).astype(BF16)
            scores = upcoming
        return carry

    lax.fori_loop(0, HEADS // 2, pair_step, 0)
    saves[3] = save(ctx, context_out, 3)

    arrived(2)
    arrived(3)

    def vector(n):
        return jnp.concatenate([nv[0, n : n + 1, :], nv[1, n : n + 1, :]], axis=1)

    for r in range(seq // block):
        rows = pl.ds(r * block, block)
        first_sum = x[rows, :].astype(F32) + nn(ctx[rows, :], wo[...])
        centre = first_sum - row_mean(first_sum)
        inv = lax.rsqrt(row_mean(centre * centre) + EPSILON)
        unit = centre * inv
        normed = unit * vector(0) + vector(1)
        seconds[rows, :] = unit
        inv_out[rows, :] = jnp.broadcast_to(inv, (block, 128))
        total[rows, :] = normed
        low[rows, :] = normed.astype(BF16)
    saves[4] = save(seconds, unit_out, 4)
    saves[5] = save(low, low_out, 5)
    saves[8] = save(wo, wo_out, 8)

    arrived(4)
    arrived(5)
    arrived(6)
    for number, (source, target) in enumerate(((wg, wg_out), (wu, wu_out), (wd, wd_out))):
        saves[9 + number] = save(source, target, 9 + number)
    columns = pieces.shape[3]
    row_tiles = seq // tile
    count = row_tiles * (wg.shape[1] // columns)
    outs = (slope_gate_out, slope_up_out, hidden_out)

    def piece_copy(number, n):
        slot = lax.rem(number, 2)
        rows = aligned(lax.rem(number, row_tiles) * tile, tile)
        cols = aligned(lax.div(number, row_tiles) * columns, columns)
        return pltpu.make_async_copy(pieces.at[slot, n], outs[n].at[rows, cols], act_sems.at[slot, n])

    def feed_step(number, carry):
        slot = lax.rem(number, 2)
        rows = aligned(lax.rem(number, row_tiles) * tile, tile)
        cols = aligned(lax.div(number, row_tiles) * columns, columns)

        @pl.when(number >= 2)
        def _():
            for n in range(3):
                piece_copy(number - 2, n).wait()

        gate = nn(low[rows, :], wg[:, cols])
        up = nn(low[rows, :], wu[:, cols])
        gate_sig = 0.5 + 0.5 * jnp.tanh(0.5 * gate)
        gate_silu = gate * gate_sig
        pieces[slot, 0] = (up * gate_sig * (1.0 + gate * (1.0 - gate_sig))).astype(BF16)
        pieces[slot, 1] = gate_silu.astype(BF16)
        hidden = (gate_silu * up).astype(BF16)
        pieces[slot, 2] = hidden
        for n in range(3):
            piece_copy(number, n).start()
        total[rows, :] += nn(hidden, wd[cols, :])
        return carry

    lax.fori_loop(0, count, feed_step, 0)

    arrived(7)
    saves[2].wait()
    saves[4].wait()
    gain_two, bias_two = vector(2), vector(3)
    bias_sum = jnp.zeros((1, width), F32)
    gain_sum = jnp.zeros((1, width), F32)
    for r in range(seq // block):
        rows = pl.ds(r * block, block)
        second_sum = total[rows, :]
        centre = second_sum - row_mean(second_sum)
        inv = lax.rsqrt(row_mean(centre * centre) + EPSILON)
        unit = centre * inv
        acts[rows, :] = (unit * gain_two + bias_two).astype(BF16)
        grad_out = g[rows, :].astype(F32)
        bias_sum += jnp.sum(grad_out, axis=0, keepdims=True)
        gain_sum += jnp.sum(grad_out * unit, axis=0, keepdims=True)
        scaled = grad_out * gain_two
        grad_second = inv * (scaled - row_mean(scaled) - unit * row_mean(scaled * unit))
        seconds[rows, :] = grad_second
        vs[rows, :] = grad_second.astype(BF16)
    norms_out[...] = nv[...]
    vec_out[...] = jnp.zeros_like(vec_out)
    vec_out[2:3, :] = gain_sum
    vec_out[3:4, :] = bias_sum
    saves[4] = save(seconds, grad_second_out, 4)
    saves[2] = save(vs, mixed_out, 2)

    mine = pltpu.make_async_copy(rows_of(acts, half), activations_out.at[core], save_sems.at[6])
    mine.start()
    theirs = pltpu.make_async_remote_copy(
        src_ref=acts.at[aligned((1 - core) * half, half)],
        dst_ref=activations_out.at[core],
        send_sem=send_sems.at[len(exchanges)],
        recv_sem=recv_sems.at[len(exchanges)],
        device_id=there,
        device_id_type=MESH,
    )
    theirs.start()
    for copy in saves.values():
        copy.wait()
    for number in range(2):
        for n in range(3):
            piece_copy(count - 2 + number, n).wait()
    mine.wait()
    theirs.wait()


def forward(tokens, cotangent, weights, norms, query_marks, key_marks, cosines, sines):
    w_qkv, w_out, w_gate, w_up, w_down = weights
    seq, width = 2 * tokens.shape[1], tokens.shape[2]
    hidden_width = w_gate.shape[1]
    dma = pltpu.SemaphoreType.DMA
    vmem = pl.BlockSpec(memory_space=pltpu.VMEM)
    hbm = pl.BlockSpec(memory_space=pl.ANY)

    def shape(*dims, dtype=BF16):
        return jax.ShapeDtypeStruct(dims, dtype)

    def full(shard):
        return pltpu.VMEM((2 * shard.shape[0], shard.shape[1]), BF16)

    rows = shape(seq, width)
    wide = shape(seq, hidden_width)
    return pl.pallas_call(
        forward_kernel,
        out_shape=(
            rows, rows, rows, rows, shape(HEADS, seq, FEATURES), rows, shape(seq, width, dtype=F32),
            shape(seq, 128, dtype=F32), wide, wide, wide, shape(seq, width, dtype=F32), rows,
            shape(*tokens.shape), shape(8, width, dtype=F32), shape(2, *norms.shape, dtype=F32),
        )
        + tuple(shape(2 * shard.shape[0], shard.shape[1]) for shard in weights),
        in_specs=[hbm] * 8 + [vmem] * 4,
        out_specs=(hbm, hbm, hbm, hbm, vmem, hbm, hbm, vmem, hbm, hbm, hbm, hbm, hbm, hbm, vmem, vmem) + (hbm,) * 5,
        scratch_shapes=[
            pltpu.VMEM((seq, width), BF16),
            pltpu.VMEM((seq, width), BF16),
            full(w_qkv), full(w_out), full(w_gate), full(w_up), full(w_down),
            pltpu.VMEM((2,) + norms.shape, F32),
            pltpu.VMEM((seq, width), BF16),
            pltpu.VMEM((seq, width), BF16),
            pltpu.VMEM((seq, width), BF16),
            pltpu.VMEM((seq, width), BF16),
            pltpu.VMEM((seq, width), F32),
            pltpu.VMEM((seq, width), BF16),
            pltpu.VMEM((seq, 256), BF16),
            pltpu.VMEM((2, seq, 256), BF16),
            pltpu.VMEM((2, 3, 512, 768), BF16),
            pltpu.VMEM((seq, width), BF16),
            pltpu.VMEM((seq, width), F32),
            dma((9,)), dma((9,)), dma((8,)), dma((12,)), dma((2, 3)),
        ],
        compiler_params=pltpu.CompilerParams(collective_id=1, has_side_effects=True, vmem_limit_bytes=62 << 20),
    )(tokens, cotangent, w_qkv, w_out, w_gate, w_up, w_down, norms, query_marks, key_marks, cosines, sines)


RING = 4
HALVES_RING = 8


def backward_kernel(
    tokens, context, low, mixed, hidden, slope_gate, slope_up, grad_second, unit, inv, norms, q_in, k_in, v_in,
    features, key_marks, cosines, sines, vec, wq, wo, wg, wu, wd,
    out, input_grad_out, vec_out,
    grads, halves, from_core, to_core, vectors, arena, total, key_aug, value_aug, delta_aug, dkey, dvalue, wide,
    send_sems, recv_sems, core_send, core_recv, vec_send, vec_recv, load_sems, input_sems,
):
    rep = lax.axis_index("rep")
    core = lax.axis_index("fsdp")
    seq, width = total.shape
    shard = width // 2
    refs = (grads, halves, out, send_sems, recv_sems)
    greet()

    def load(slot, source, target=None):
        return pltpu.make_async_copy(source, arena.at[slot] if target is None else target, load_sems.at[slot])

    def square(slot):
        return arena.at[slot, pl.ds(0, width), :]

    def sided(slot, source, first, second):
        return (
            pltpu.make_async_copy(
                source.at[:, aligned(first, shard, 128)], arena.at[slot, :, pl.ds(0, shard)], load_sems.at[slot]
            ),
            pltpu.make_async_copy(
                source.at[:, aligned(second, shard, 128)], arena.at[slot, :, pl.ds(shard, shard)], input_sems.at[slot]
            ),
        )

    def begin(loads):
        for one in loads if isinstance(loads, tuple) else (loads,):
            one.start()

    def finish(loads):
        for one in loads if isinstance(loads, tuple) else (loads,):
            one.wait()

    def core_copy(chunk):
        slot = lax.rem(chunk, RING)
        return pltpu.make_async_remote_copy(
            src_ref=to_core.at[slot],
            dst_ref=from_core.at[slot],
            send_sem=core_send.at[slot],
            recv_sem=core_recv.at[slot],
            device_id=other_core(),
            device_id_type=MESH,
        )

    def emit(chunk, left, right):
        slot = lax.rem(chunk, RING)

        @pl.when(chunk >= RING)
        def _():
            core_copy(chunk - RING).wait_send()

        to_core[slot] = tn(arena[left, :, shard:], arena[right]).astype(BF16)
        core_copy(chunk).start()
        grads[chunk] = tn(arena[left, :, :shard], arena[right]).astype(BF16)

    def absorb(chunk):
        core_copy(chunk).wait_recv()
        slot = lax.rem(chunk, RING)
        grads[chunk] = (grads[chunk].astype(F32) + from_core[slot].astype(F32)).astype(BF16)

    def slot_work(k):
        for stage in range(2 * STEPS, -1, -1):
            entered = k - stage

            @pl.when((entered >= 0) & (entered <= CHUNKS) & (entered != CHUNKS - 3))
            def _():
                rep_stage(refs, entered - lax.div(entered, CHUNKS - 3), stage)

    MIXED, LOW, SLOPE_GATE, SLOPE_UP, HIDDEN, GATE, UP, WD, WG, WU = range(10)
    blocks = wg.shape[1] // width

    def block_loads(j):
        cols = aligned(j * width, width)
        return {
            SLOPE_GATE: load(SLOPE_GATE, slope_gate.at[:, cols]),
            SLOPE_UP: load(SLOPE_UP, slope_up.at[:, cols]),
            WD: load(WD, wd.at[cols, :], square(WD)),
            WG: load(WG, wg.at[:, cols], square(WG)),
            WU: load(WU, wu.at[:, cols], square(WU)),
            HIDDEN: sided(
                HIDDEN,
                hidden,
                core * (wd.shape[0] // 2) + j * shard,
                (1 - core) * (wd.shape[0] // 2) + j * shard,
            ),
        }

    first_loads = block_loads(0)
    mixed_load = load(MIXED, mixed)
    low_load = sided(LOW, low, core * shard, (1 - core) * shard)
    second_load = load(10, grad_second, total)
    for one in (mixed_load, first_loads[WD], first_loads[SLOPE_GATE], first_loads[SLOPE_UP], first_loads[HIDDEN],
                low_load, first_loads[WG], first_loads[WU], second_load):
        begin(one)
    vectors[0] = vec[...]
    finish(mixed_load)

    tile = 512

    def feed_step(j, carry):
        loads = block_loads(j)
        upcoming = block_loads(j + 1)

        def renew(*slots):
            @pl.when(j + 1 < blocks)
            def _():
                for slot in slots:
                    begin(upcoming[slot])

        for slot in (WD, SLOPE_GATE, SLOPE_UP):
            finish(loads[slot])
        for r in range(seq // tile):
            rows = pl.ds(r * tile, tile)
            grad_hidden = nt(arena[MIXED, rows, :], arena[WD, :width, :])
            arena[GATE, rows, :] = (grad_hidden * arena[SLOPE_GATE, rows, :].astype(F32)).astype(BF16)
            arena[UP, rows, :] = (grad_hidden * arena[SLOPE_UP, rows, :].astype(F32)).astype(BF16)
        renew(WD, SLOPE_GATE, SLOPE_UP)
        finish(loads[HIDDEN])
        emit(3 * j, HIDDEN, MIXED)
        renew(HIDDEN)

        @pl.when(j > 0)
        def _():
            absorb(3 * j - 1)
            slot_work(2 * j - 1)

        @pl.when(j == 0)
        def _():
            finish(low_load)
            finish(second_load)

        emit(3 * j + 1, LOW, GATE)
        finish(loads[WG])
        for r in range(seq // tile):
            rows = pl.ds(r * tile, tile)
            total[rows, :] += nt(arena[GATE, rows, :], arena[WG, :width, :])
        renew(WG)
        absorb(3 * j)
        slot_work(2 * j)
        emit(3 * j + 2, LOW, UP)
        finish(loads[WU])
        for r in range(seq // tile):
            rows = pl.ds(r * tile, tile)
            total[rows, :] += nt(arena[UP, rows, :], arena[WU, :width, :])
        renew(WU)
        absorb(3 * j + 1)
        return carry

    lax.fori_loop(0, blocks, feed_step, 0)

    CONTEXT, SIDED_CONTEXT, WO, ATTENDED, GRAD_CONTEXT, Q, K, V, DQ, DK, DV, TOKENS, WQ = range(13)
    chunk = 3 * blocks
    loads = {
        CONTEXT: load(CONTEXT, context),
        SIDED_CONTEXT: sided(SIDED_CONTEXT, context, core * shard, (1 - core) * shard),
        WO: load(WO, wo, square(WO)),
        Q: load(Q, q_in),
        K: load(K, k_in),
        V: load(V, v_in),
        TOKENS: sided(TOKENS, tokens, core * shard, (1 - core) * shard),
        WQ: load(WQ, wq.at[:, pl.ds(0, width)], square(WQ)),
    }
    for slot in (SIDED_CONTEXT, WO, CONTEXT, Q, K, V, TOKENS, WQ):
        begin(loads[slot])
    absorb(chunk - 1)
    gain_one = jnp.concatenate([norms[0, 0:1, :], norms[1, 0:1, :]], axis=1)
    bias_sum = jnp.zeros((1, width), F32)
    gain_sum = jnp.zeros((1, width), F32)
    block = 256
    for r in range(seq // block):
        rows = pl.ds(r * block, block)
        grad_normed = total[rows, :]
        unit_rows = unit[rows, :]
        bias_sum += jnp.sum(grad_normed, axis=0, keepdims=True)
        gain_sum += jnp.sum(grad_normed * unit_rows, axis=0, keepdims=True)
        scaled = grad_normed * gain_one
        grad_first = inv[rows, 0:1] * (scaled - row_mean(scaled) - unit_rows * row_mean(scaled * unit_rows))
        total[rows, :] = grad_first
        arena[ATTENDED, rows, :] = grad_first.astype(BF16)
    vectors[0, 0:1, :] = gain_sum
    vectors[0, 1:2, :] = bias_sum
    finish(loads[SIDED_CONTEXT])
    emit(chunk, SIDED_CONTEXT, ATTENDED)
    finish(loads[WO])
    for r in range(seq // tile):
        rows = pl.ds(r * tile, tile)
        arena[GRAD_CONTEXT, rows, :] = nt(arena[ATTENDED, rows, :], arena[WO, :width, :]).astype(BF16)
    absorb(chunk)
    first_slot = 2 * blocks - 1
    slot_work(first_slot)
    for slot in (CONTEXT, Q, K, V):
        finish(loads[slot])

    steps = [(a, r) for r in range(seq // block) for a in range(2)]
    ones = jnp.where((lanes() >= SPLIT_LANE) & (lanes() < SPLIT_LANE + 3), 1.0, 0.0)

    def pair_step(pair, carry):
        cols = aligned(pair * 128, 128)
        key_aug[:, :128] = arena[K, :, cols]
        key_aug[:, 128:] = (key_marks[...].astype(F32) + ones).astype(BF16)
        value_aug[:, :128] = arena[V, :, cols]
        value_aug[:, 128:] = jnp.broadcast_to(ones, (seq, 128)).astype(BF16)
        delta = arena[GRAD_CONTEXT, :, cols].astype(F32) * arena[CONTEXT, :, cols].astype(F32)
        for a in range(2):
            row_delta = jnp.sum(head_mask(delta, a == 0), axis=1, keepdims=True)
            delta_aug[a, :, :128] = head_mask(arena[GRAD_CONTEXT, :, cols], a == 0)
            delta_aug[a, :, 128:] = split_lanes(jnp.zeros((seq, 128), F32), -row_delta)

        def products_of(a, r):
            rows = pl.ds(r * block, block)
            query = jnp.concatenate([head_mask(arena[Q, rows, cols], a == 0), features[2 * pair + a, rows, :]], axis=1)
            return nt(query, key_aug[...]), nt(delta_aug[a, rows, :], value_aug[...])

        upcoming = products_of(*steps[0])
        for number, (a, r) in enumerate(steps):
            rows = pl.ds(r * block, block)
            scores, grad_probs = upcoming
            upcoming = products_of(*steps[number + 1]) if number + 1 < len(steps) else None
            probs = jnp.exp(scores)
            grad_scores = (probs * grad_probs).astype(BF16)
            probs = probs.astype(BF16)
            dquery = nn(grad_scores, head_mask(key_aug[:, :128], a == 0))
            dkey_term = tn(grad_scores, head_mask(arena[Q, rows, cols], a == 0))
            dvalue_term = tn(probs, delta_aug[a, rows, :128])
            if number == 0:
                dkey[...] = dkey_term
                dvalue[...] = dvalue_term
            else:
                dkey[...] += dkey_term
                dvalue[...] += dvalue_term
            if a == 0:
                wide[...] = dquery
            else:
                dquery = (wide[...] + dquery) * (HEAD_DIM ** (-0.5))
                arena[DQ, rows, cols] = turn(dquery, cosines[rows, :], -sines[rows, :]).astype(BF16)
        arena[DK, :, cols] = turn(dkey[...], cosines[...], -sines[...]).astype(BF16)
        arena[DV, :, cols] = dvalue[...].astype(BF16)
        slot_work(first_slot + 1 + pair)
        for stage in range(VECTOR_STEPS + 1):

            @pl.when(pair == stage)
            def _():
                vector_stage(vectors, vec_send, vec_recv, stage)

        return carry

    lax.fori_loop(0, HEADS // 2, pair_step, 0)
    k = first_slot + 1 + HEADS // 2

    finish(loads[TOKENS])
    following = load(WQ, wq.at[:, pl.ds(0, width)], square(WQ))
    for n, slot in enumerate((DQ, DK, DV)):
        emit(chunk + 1 + n, TOKENS, slot)
        finish(following)
        for r in range(seq // tile):
            rows = pl.ds(r * tile, tile)
            total[rows, :] += nt(arena[slot, rows, :], arena[WQ, :width, :])
        if n < 2:
            following = load(WQ, wq.at[:, pl.ds((n + 1) * width, width)], square(WQ))
            following.start()
        absorb(chunk + 1 + n)
        slot_work(k + n)

    half = seq // 2
    mine = pltpu.make_async_copy(total.at[aligned(core * half, half)], input_grad_out.at[core], load_sems.at[13])
    theirs = pltpu.make_async_remote_copy(
        src_ref=total.at[aligned((1 - core) * half, half)],
        dst_ref=input_grad_out.at[core],
        send_sem=core_send.at[RING],
        recv_sem=core_recv.at[RING],
        device_id=other_core(),
        device_id_type=MESH,
    )
    mine.start()
    theirs.start()
    vec_out[...] = vectors[2 * VECTOR_STEPS]

    def drain(k, carry):
        slot_work(k)
        return carry

    lax.fori_loop(k + 3, CHUNKS + 2 * STEPS + 1, drain, 0)
    mine.wait()
    theirs.wait()
    for number in range(RING):
        core_copy(CHUNKS - RING + number).wait_send()


def backward(tokens, saved, norms, key_marks, cosines, sines, vec, weights, outs):
    context, low, mixed, hidden, slope_gate, slope_up, grad_second, unit, inv, q, k, v, features = saved
    seq, width = tokens.shape
    dma = pltpu.SemaphoreType.DMA
    vmem = pl.BlockSpec(memory_space=pltpu.VMEM)
    hbm = pl.BlockSpec(memory_space=pl.ANY)
    chunks = (CHUNKS, width // 2, width)
    return pl.pallas_call(
        backward_kernel,
        out_shape=(
            jax.ShapeDtypeStruct(chunks, BF16),
            jax.ShapeDtypeStruct(outs, F32),
            jax.ShapeDtypeStruct(vec.shape, F32),
        ),
        in_specs=[hbm] * 8 + [vmem] * 3 + [hbm] * 3 + [vmem] * 5 + [hbm] * 5,
        out_specs=(hbm, hbm, vmem),
        scratch_shapes=[
            pltpu.VMEM(chunks, BF16),
            pltpu.VMEM((HALVES_RING,) + chunks[1:], BF16),
            pltpu.VMEM((RING,) + chunks[1:], BF16),
            pltpu.VMEM((RING,) + chunks[1:], BF16),
            pltpu.VMEM((2 * VECTOR_STEPS + 1,) + vec.shape, F32),
            pltpu.VMEM((13, seq, width), BF16),
            pltpu.VMEM((seq, width), F32),
            pltpu.VMEM((seq, 256), BF16),
            pltpu.VMEM((seq, 256), BF16),
            pltpu.VMEM((2, seq, 256), BF16),
            pltpu.VMEM((seq, 128), F32),
            pltpu.VMEM((seq, 128), F32),
            pltpu.VMEM((256, 128), F32),
            dma((CHUNKS, PARTS, 2 * STEPS + 1)),
            dma((CHUNKS, PARTS, 2 * STEPS)),
            dma((RING + 1,)),
            dma((RING + 1,)),
            dma((VECTOR_STEPS,)),
            dma((VECTOR_STEPS,)),
            dma((14,)),
            dma((14,)),
        ],
        compiler_params=pltpu.CompilerParams(collective_id=0, has_side_effects=True, vmem_limit_bytes=62 << 20),
    )(tokens, context, low, mixed, hidden, slope_gate, slope_up, grad_second, unit, inv, norms, q, k, v,
      features, key_marks, cosines, sines, vec, *weights)


def widen_kernel(summed, qkv, out, gate, up, down):
    step = pl.program_id(0)
    values = summed[0].astype(F32)
    turn_of = lax.rem(step, 3)
    fed = step < CHUNKS - 4
    for ref, now in (
        (down, fed & (turn_of == 0)),
        (gate, fed & (turn_of == 1)),
        (up, fed & (turn_of == 2)),
        (out, step == CHUNKS - 4),
        (qkv, step > CHUNKS - 4),
    ):

        @pl.when(now)
        def _():
            ref[...] = values


def widen(summed):
    rows, cols = summed.shape[1:]
    fed = CHUNKS - 4

    def shape(high, across):
        return jax.ShapeDtypeStruct((rows * high, cols * across), F32)

    def spec(place):
        return pl.BlockSpec((rows, cols), place)

    def turn_of(step):
        return lax.div(jnp.minimum(step, fed - 1), 3)

    return pl.pallas_call(
        widen_kernel,
        grid=(CHUNKS,),
        out_shape=(shape(1, 3), shape(1, 1), shape(1, 4), shape(1, 4), shape(4, 1)),
        in_specs=[pl.BlockSpec((1, rows, cols), lambda step: (step, 0, 0))],
        out_specs=(
            spec(lambda step: (0, jnp.maximum(step - fed - 1, 0))),
            spec(lambda step: (0, 0)),
            spec(lambda step: (0, turn_of(step))),
            spec(lambda step: (0, turn_of(step))),
            spec(lambda step: (turn_of(step), 0)),
        ),
    )(summed)


def shards(
    tokens,
    lengths,
    w_qkv,
    w_out,
    w_gate,
    w_up,
    w_down,
    norm1_gain,
    norm1_bias,
    norm2_gain,
    norm2_bias,
    cotangent,
):
    core = lax.axis_index("fsdp")
    shard = norm1_gain.shape[0]
    seq_len = 2 * tokens.shape[1]
    doc_lengths = lax.dynamic_index_in_dim(lengths, core, 0, keepdims=False)
    segment, positions = doc_tables(doc_lengths, seq_len)
    cosine_table, sine_table = rope_tables(positions)
    cosines = jnp.concatenate([cosine_table] * 4, axis=1)
    sines = jnp.concatenate([-sine_table, sine_table] * 2, axis=1)
    columns = jnp.arange(FEATURES, dtype=jnp.int32)[None, :]
    same = segment[:, None] == columns
    query_marks = same.astype(BF16)
    key_marks = jnp.where(same | (columns >= SPLIT_LANE), 0.0, NEG).astype(BF16)
    zero = jnp.zeros_like(norm1_gain)
    norms = jnp.stack([norm1_gain, norm1_bias, norm2_gain, norm2_bias, zero, zero, zero, zero]).astype(F32)

    weights = (w_qkv, w_out, w_gate, w_up, w_down)
    (q, k, v, context, features, low, unit, inv, slope_gate, slope_up, hidden, grad_second, mixed, activations,
     vec, norms, *weights) = forward(tokens, cotangent, weights, norms, query_marks, key_marks, cosines, sines)
    stream = lax.all_to_all(tokens, "fsdp", split_axis=0, concat_axis=1, tiled=True)[0]
    saved = (context, low, mixed, hidden, slope_gate, slope_up, grad_second, unit, inv, q, k, v, features)
    summed, input_grad, vec_sum = backward(
        stream, saved, norms, key_marks, cosines, sines, vec, weights, tokens.shape
    )
    groups = lax.axis_size("rep") // UNITS
    if groups > 1:
        alike = [[UNITS * g + n for g in range(groups)] for n in range(UNITS)]
        summed = lax.psum(summed, "rep", axis_index_groups=alike)
        vec_sum = lax.psum(vec_sum, "rep", axis_index_groups=alike)
    vec_own = lax.dynamic_slice_in_dim(vec_sum, core * shard, shard, axis=1)
    return (activations, input_grad, *widen(summed), vec_own[0], vec_own[1], vec_own[2], vec_own[3])


def solution(mesh):
    placed = (
        P("rep", "fsdp", None),
        P("rep", None),
        P("fsdp", None),
        P("fsdp", None),
        P("fsdp", None),
        P("fsdp", None),
        P("fsdp", None),
        P("fsdp"),
        P("fsdp"),
        P("fsdp"),
        P("fsdp"),
        P("rep", "fsdp", None),
    )
    return jax.shard_map(
        shards,
        mesh=mesh,
        in_specs=placed,
        out_specs=(
            P("rep", "fsdp", None),
            P("rep", "fsdp", None),
            P("fsdp", None),
            P("fsdp", None),
            P("fsdp", None),
            P("fsdp", None),
            P("fsdp", None),
            P("fsdp"),
            P("fsdp"),
            P("fsdp"),
            P("fsdp"),
        ),
        check_vma=False,
    )
```

```python
import functools

import jax
import jax.numpy as jnp
from jax import lax
from jax.experimental import pallas as pl
from jax.experimental.pallas import tpu as pltpu
from jax.sharding import PartitionSpec as P

HEADS = 12
HEAD_DIM = 64


EPSILON = 1e-05


def doc_tables(doc_lengths, seq_len):
    doc_ends = jnp.cumsum(doc_lengths)
    doc_starts = doc_ends - doc_lengths
    places = jnp.arange(seq_len, dtype=jnp.int32)
    segment = jnp.sum((places[:, None] >= doc_ends[None, :]).astype(jnp.int32), axis=1)
    member = segment[:, None] == jnp.arange(doc_lengths.shape[0], dtype=jnp.int32)[None, :]
    begins = jnp.sum(jnp.where(member, doc_starts[None, :], 0), axis=1)
    return (segment, places - begins)


def rope_tables(positions):
    half_dim = HEAD_DIM // 2
    frequencies = 1000.0 ** (-2.0 * jnp.arange(half_dim, dtype=jnp.float32) / HEAD_DIM)
    angles = positions.astype(jnp.float32)[:, None] * frequencies[None, :]
    return (jnp.cos(angles), jnp.sin(angles))


CHUNKS = 16
PARTS = 3
PART_ROWS = 128
UNITS = 16
STEPS = 4
MESH = pl.DeviceIdType.MESH
BF16 = jnp.bfloat16
F32 = jnp.float32


def bit_of(value, weight):
    return lax.rem(lax.div(value, weight), 2)


def orders(chunk):
    rep = lax.axis_index("rep")
    odd = lax.rem(jnp.asarray(chunk, jnp.int32), 2)
    first, second = 1 + odd, 2 - odd
    bits = {1: bit_of(rep, 1), 2: bit_of(rep, 2), 4: bit_of(rep, 4), 8: bit_of(rep, 8)}
    first_bit = bits[1] * (1 - odd) + bits[2] * odd
    second_bit = bits[2] * (1 - odd) + bits[1] * odd
    return (
        ((1, bits[1]), (2, bits[2]), (4, bits[4]), (8, bits[8])),
        ((2, bits[2]), (1, bits[1]), (4, bits[4]), (8, bits[8])),
        ((4, bits[4]), (first, first_bit), (second, second_bit), (8, bits[8])),
    )


def partner_of(weight, bit):
    return (lax.axis_index("rep") + weight * (1 - 2 * bit), lax.axis_index("fsdp"))


def other_core():
    return (lax.axis_index("rep"), 1 - lax.axis_index("fsdp"))


def region(ref, chunk, part, order, level, flip):
    rows = PART_ROWS >> min(level, STEPS - 1)
    start = part * PART_ROWS
    for step in range(level):
        bit = order[step][1]
        if flip and step == level - 1:
            bit = 1 - bit
        if step < STEPS - 1:
            start = start + bit * (PART_ROWS >> (step + 1))
        else:
            column = bit * (ref.shape[2] // 2)
    start = pl.multiple_of(start, 16)
    if level < STEPS:
        return (chunk, pl.ds(start, rows), slice(None))
    half = ref.shape[2] // 2
    return (chunk, pl.ds(start, rows), pl.ds(pl.multiple_of(column, 128), half))


def landing(ref, chunk, part, step):
    start = part * PART_ROWS + PART_ROWS - (PART_ROWS >> step)
    chunk = lax.rem(jnp.asarray(chunk, jnp.int32), ref.shape[0])
    if step < STEPS - 1:
        return (chunk, pl.ds(start, PART_ROWS >> (step + 1)), slice(None))
    return (chunk, pl.ds(start, PART_ROWS >> step), pl.ds(0, ref.shape[2] // 2))


def halving_copy(refs, chunk, part, order, step):
    grads, halves, _, send_sems, recv_sems = refs
    return pltpu.make_async_remote_copy(
        src_ref=grads.at[region(grads, chunk, part, order, step + 1, True)],
        dst_ref=halves.at[landing(halves, chunk, part, step)],
        send_sem=send_sems.at[chunk, part, step],
        recv_sem=recv_sems.at[chunk, part, step],
        device_id=partner_of(*order[step]),
        device_id_type=MESH,
    )


def halving_add(refs, chunk, part, order, step):
    grads, halves = refs[:2]
    kept = region(grads, chunk, part, order, step + 1, False)
    theirs = halves[landing(halves, chunk, part, step)]
    grads[kept] = (grads[kept].astype(F32) + theirs.astype(F32)).astype(BF16)


def settle_copy(refs, chunk, part, order):
    grads, _, out, send_sems, _ = refs
    mine = region(grads, chunk, part, order, STEPS, False)
    return pltpu.make_async_copy(grads.at[mine], out.at[mine], send_sems.at[chunk, part, 2 * STEPS])


def doubling_copy(refs, chunk, part, order, step):
    grads, _, out, send_sems, recv_sems = refs
    mine = region(out, chunk, part, order, step + 1, False)
    return pltpu.make_async_remote_copy(
        src_ref=(grads if step == STEPS - 1 else out).at[mine],
        dst_ref=out.at[mine],
        send_sem=send_sems.at[chunk, part, STEPS + step],
        recv_sem=recv_sems.at[chunk, part, STEPS + step],
        device_id=partner_of(*order[step]),
        device_id_type=MESH,
    )


def halve(refs, chunk, stage):
    for part, order in enumerate(orders(chunk)):
        if stage > 0:
            halving_copy(refs, chunk, part, order, stage - 1).wait()
            halving_add(refs, chunk, part, order, stage - 1)
        if stage < STEPS:
            halving_copy(refs, chunk, part, order, stage).start()
        else:
            settle_copy(refs, chunk, part, order).start()


def double(refs, chunk, stage):
    for part, order in enumerate(orders(chunk)):
        if stage > 0:
            doubling_copy(refs, chunk, part, order, STEPS - stage).wait()
        if stage == 1:
            settle_copy(refs, chunk, part, order).wait()
        if stage < STEPS:
            doubling_copy(refs, chunk, part, order, STEPS - 1 - stage).start()


def greet():
    rep = lax.axis_index("rep")
    barrier = pltpu.get_barrier_semaphore()
    pl.semaphore_signal(barrier, inc=1, device_id=other_core(), device_id_type=MESH)
    for weight in (1, 2, 4, 8):
        there = partner_of(weight, bit_of(rep, weight))
        pl.semaphore_signal(barrier, inc=1, device_id=there, device_id_type=MESH)
    pl.semaphore_wait(barrier, 5)


def vector_copy(vectors, send_sems, recv_sems, step):
    rep = lax.axis_index("rep")
    if step == 0:
        there = other_core()
    else:
        weight = 1 << (step - 1)
        there = partner_of(weight, bit_of(rep, weight))
    return pltpu.make_async_remote_copy(
        src_ref=vectors.at[2 * step],
        dst_ref=vectors.at[2 * step + 1],
        send_sem=send_sems.at[step],
        recv_sem=recv_sems.at[step],
        device_id=there,
        device_id_type=MESH,
    )


VECTOR_STEPS = 5


def vector_stage(vectors, send_sems, recv_sems, stage):
    if stage > 0:
        vector_copy(vectors, send_sems, recv_sems, stage - 1).wait()
        vectors[2 * stage] = vectors[2 * stage - 2] + vectors[2 * stage - 1]
    if stage < VECTOR_STEPS:
        vector_copy(vectors, send_sems, recv_sems, stage).start()


SEQ_ROWS = 512
NEG = -1e30
FEATURES = 128
SPLIT_LANE = 8


def nn(left, right):
    return jnp.dot(left, right, preferred_element_type=F32)


def nt(left, right):
    return lax.dot_general(left, right, (((1,), (1,)), ((), ())), preferred_element_type=F32)


def tn(left, right):
    return lax.dot_general(left, right, (((0,), (0,)), ((), ())), preferred_element_type=F32)


def aligned(start, size, multiple=None):
    return pl.ds(pl.multiple_of(start, multiple or size), size)


def lanes():
    return lax.broadcasted_iota(jnp.int32, (1, 128), 1)


def head_mask(values, first):
    low = lanes() < HEAD_DIM
    zero = jnp.zeros_like(values)
    return jnp.where(low, values, zero) if first else jnp.where(low, zero, values)


def turn(values, cosines, sines):
    first = lax.rem(lanes(), HEAD_DIM) < HEAD_DIM // 2
    swapped = jnp.where(first, pltpu.roll(values, 96, 1), pltpu.roll(values, 32, 1))
    return values * cosines + swapped * sines


def split_lanes(base, values):
    high = values.astype(BF16).astype(F32)
    middle = (values - high).astype(BF16).astype(F32)
    low = values - high - middle
    lane = lanes()
    out = jnp.where(lane == SPLIT_LANE, high, base)
    out = jnp.where(lane == SPLIT_LANE + 1, middle, out)
    return jnp.where(lane == SPLIT_LANE + 2, low, out).astype(BF16)


def row_mean(values):
    return jnp.mean(values, axis=1, keepdims=True)


def forward_kernel(
    tokens, cotangent, w_qkv, w_out, w_gate, w_up, w_down, norms, query_marks, key_marks, cosines, sines,
    q_out, k_out, v_out, context_out, features_out, low_out, unit_out, inv_out, slope_gate_out, slope_up_out,
    hidden_out, grad_second_out, mixed_out, activations_out, vec_out,
    norms_out, x_out, wq_out, wo_out, wg_out, wu_out, wd_out,
    x, g, wq, wo, wg, wu, wd, nv, qs, ks, vs, ctx, total, low, key_aug, value_aug, pieces, acts, seconds,
    send_sems, recv_sems, own_sems, save_sems, act_sems,
):
    rep = lax.axis_index("rep")
    core = lax.axis_index("fsdp")
    there = (rep, 1 - core)
    seq, width = x.shape
    half = seq // 2

    barrier = pltpu.get_barrier_semaphore()
    pl.semaphore_signal(barrier, inc=1, device_id=there, device_id_type=MESH)
    pl.semaphore_wait(barrier, 1)

    def rows_of(ref, block):
        return ref.at[aligned(core * block, block)]

    exchanges = (
        (tokens.at[core], tokens.at[1 - core], rows_of(x, half)),
        (w_qkv, w_qkv, rows_of(wq, w_qkv.shape[0])),
        (w_out, w_out, rows_of(wo, w_out.shape[0])),
        (norms, norms, nv.at[core]),
        (w_gate, w_gate, rows_of(wg, w_gate.shape[0])),
        (w_up, w_up, rows_of(wu, w_up.shape[0])),
        (w_down, w_down, rows_of(wd, w_down.shape[0])),
        (cotangent.at[core], cotangent.at[1 - core], rows_of(g, half)),
    )

    def copies(number):
        mine, theirs, place = exchanges[number]
        return (
            pltpu.make_async_copy(mine, place, own_sems.at[number]),
            pltpu.make_async_remote_copy(
                src_ref=theirs,
                dst_ref=place,
                send_sem=send_sems.at[number],
                recv_sem=recv_sems.at[number],
                device_id=there,
                device_id_type=MESH,
            ),
        )

    for number in range(len(exchanges)):
        for copy in copies(number):
            copy.start()

    def arrived(number):
        for copy in copies(number):
            copy.wait()

    def save(source, target, number):
        copy = pltpu.make_async_copy(source, target, save_sems.at[number])
        copy.start()
        return copy

    arrived(0)
    arrived(1)
    tile = 512
    for n, out in enumerate((qs, ks, vs)):
        for r in range(seq // tile):
            rows = pl.ds(r * tile, tile)
            product_rows = nn(x[rows, :], wq[:, pl.ds(n * width, width)])
            if n == 2:
                out[rows, :] = product_rows.astype(BF16)
                continue
            for pair in range(width // 128):
                cols = slice(pair * 128, pair * 128 + 128)
                turned = turn(product_rows[:, cols], cosines[rows, :], sines[rows, :]).astype(BF16)
                if n == 0:
                    turned = turned * jnp.asarray(HEAD_DIM ** (-0.5), BF16)
                out[rows, cols] = turned
    saves = {12: save(x, x_out, 12), 0: save(qs, q_out, 0), 1: save(ks, k_out, 1), 2: save(vs, v_out, 2)}

    saves[7] = save(wq, wq_out, 7)

    block = 256
    steps = [(a, r) for r in range(seq // block) for a in range(2)]

    def pair_step(pair, carry):
        cols = aligned(pair * 128, 128)
        key_aug[:, :128] = ks[:, cols]
        key_aug[:, 128:] = key_marks[...]
        for a in range(2):
            value_aug[a, :, :128] = head_mask(vs[:, cols], a == 0)
            value_aug[a, :, 128:] = jnp.ones((seq, 128), BF16)

        def scores_of(a, r):
            rows = pl.ds(r * block, block)
            query = jnp.concatenate([head_mask(qs[rows, cols], a == 0), query_marks[rows, :]], axis=1)
            return nt(query, key_aug[...])

        scores = scores_of(*steps[0])
        parts = [None, None]
        for number, (a, r) in enumerate(steps):
            rows = pl.ds(r * block, block)
            upcoming = scores_of(*steps[number + 1]) if number + 1 < len(steps) else None
            row_max = jnp.max(scores, axis=1, keepdims=True)
            probs = jnp.exp(scores - row_max).astype(BF16)
            summed = nn(probs, value_aug[a])
            row_total = summed[:, 128:]
            parts[a] = summed[:, :128] / row_total
            lse = row_max + jnp.log(row_total)
            features_out[2 * pair + a, rows, :] = split_lanes(query_marks[rows, :].astype(F32), -lse)
            if a == 1:
                ctx[rows, cols] = (parts[0] + parts[1]).astype(BF16)
            scores = upcoming
        return carry

    lax.fori_loop(0, HEADS // 2, pair_step, 0)
    saves[3] = save(ctx, context_out, 3)

    arrived(2)
    arrived(3)

    def vector(n):
        return jnp.concatenate([nv[0, n : n + 1, :], nv[1, n : n + 1, :]], axis=1)

    for r in range(seq // block):
        rows = pl.ds(r * block, block)
        first_sum = x[rows, :].astype(F32) + nn(ctx[rows, :], wo[...])
        centre = first_sum - row_mean(first_sum)
        inv = lax.rsqrt(row_mean(centre * centre) + EPSILON)
        unit = centre * inv
        normed = unit * vector(0) + vector(1)
        seconds[rows, :] = unit
        inv_out[rows, :] = jnp.broadcast_to(inv, (block, 128))
        total[rows, :] = normed
        low[rows, :] = normed.astype(BF16)
    saves[4] = save(seconds, unit_out, 4)
    saves[5] = save(low, low_out, 5)
    saves[8] = save(wo, wo_out, 8)

    arrived(4)
    arrived(5)
    arrived(6)
    for number, (source, target) in enumerate(((wg, wg_out), (wu, wu_out), (wd, wd_out))):
        saves[9 + number] = save(source, target, 9 + number)
    columns = pieces.shape[3]
    row_tiles = seq // tile
    count = row_tiles * (wg.shape[1] // columns)
    outs = (slope_gate_out, slope_up_out, hidden_out)

    def piece_copy(number, n):
        slot = lax.rem(number, 2)
        rows = aligned(lax.rem(number, row_tiles) * tile, tile)
        cols = aligned(lax.div(number, row_tiles) * columns, columns)
        return pltpu.make_async_copy(pieces.at[slot, n], outs[n].at[rows, cols], act_sems.at[slot, n])

    def feed_step(number, carry):
        slot = lax.rem(number, 2)
        rows = aligned(lax.rem(number, row_tiles) * tile, tile)
        cols = aligned(lax.div(number, row_tiles) * columns, columns)

        @pl.when(number >= 2)
        def _():
            for n in range(3):
                piece_copy(number - 2, n).wait()

        gate = nn(low[rows, :], wg[:, cols])
        up = nn(low[rows, :], wu[:, cols])
        gate_sig = 0.5 + 0.5 * jnp.tanh(0.5 * gate)
        gate_silu = gate * gate_sig
        pieces[slot, 0] = (up * gate_sig * (1.0 + gate * (1.0 - gate_sig))).astype(BF16)
        pieces[slot, 1] = gate_silu.astype(BF16)
        hidden = (gate_silu * up).astype(BF16)
        pieces[slot, 2] = hidden
        for n in range(3):
            piece_copy(number, n).start()
        total[rows, :] += nn(hidden, wd[cols, :])
        return carry

    lax.fori_loop(0, count, feed_step, 0)

    arrived(7)
    saves[2].wait()
    saves[4].wait()
    gain_two, bias_two = vector(2), vector(3)
    bias_sum = jnp.zeros((1, width), F32)
    gain_sum = jnp.zeros((1, width), F32)
    for r in range(seq // block):
        rows = pl.ds(r * block, block)
        second_sum = total[rows, :]
        centre = second_sum - row_mean(second_sum)
        inv = lax.rsqrt(row_mean(centre * centre) + EPSILON)
        unit = centre * inv
        acts[rows, :] = (unit * gain_two + bias_two).astype(BF16)
        grad_out = g[rows, :].astype(F32)
        bias_sum += jnp.sum(grad_out, axis=0, keepdims=True)
        gain_sum += jnp.sum(grad_out * unit, axis=0, keepdims=True)
        scaled = grad_out * gain_two
        grad_second = inv * (scaled - row_mean(scaled) - unit * row_mean(scaled * unit))
        seconds[rows, :] = grad_second
        vs[rows, :] = grad_second.astype(BF16)
    norms_out[...] = nv[...]
    vec_out[...] = jnp.zeros_like(vec_out)
    vec_out[2:3, :] = gain_sum
    vec_out[3:4, :] = bias_sum
    saves[4] = save(seconds, grad_second_out, 4)
    saves[2] = save(vs, mixed_out, 2)

    mine = pltpu.make_async_copy(rows_of(acts, half), activations_out.at[core], save_sems.at[6])
    mine.start()
    theirs = pltpu.make_async_remote_copy(
        src_ref=acts.at[aligned((1 - core) * half, half)],
        dst_ref=activations_out.at[core],
        send_sem=send_sems.at[len(exchanges)],
        recv_sem=recv_sems.at[len(exchanges)],
        device_id=there,
        device_id_type=MESH,
    )
    theirs.start()
    for copy in saves.values():
        copy.wait()
    for number in range(2):
        for n in range(3):
            piece_copy(count - 2 + number, n).wait()
    mine.wait()
    theirs.wait()


def forward(tokens, cotangent, weights, norms, query_marks, key_marks, cosines, sines):
    w_qkv, w_out, w_gate, w_up, w_down = weights
    seq, width = 2 * tokens.shape[1], tokens.shape[2]
    hidden_width = w_gate.shape[1]
    dma = pltpu.SemaphoreType.DMA
    vmem = pl.BlockSpec(memory_space=pltpu.VMEM)
    hbm = pl.BlockSpec(memory_space=pl.ANY)

    def shape(*dims, dtype=BF16):
        return jax.ShapeDtypeStruct(dims, dtype)

    def full(shard):
        return pltpu.VMEM((2 * shard.shape[0], shard.shape[1]), BF16)

    rows = shape(seq, width)
    wide = shape(seq, hidden_width)
    return pl.pallas_call(
        forward_kernel,
        out_shape=(
            rows, rows, rows, rows, shape(HEADS, seq, FEATURES), rows, shape(seq, width, dtype=F32),
            shape(seq, 128, dtype=F32), wide, wide, wide, shape(seq, width, dtype=F32), rows,
            shape(*tokens.shape), shape(8, width, dtype=F32), shape(2, *norms.shape, dtype=F32), rows,
        )
        + tuple(shape(2 * shard.shape[0], shard.shape[1]) for shard in weights),
        in_specs=[hbm] * 8 + [vmem] * 4,
        out_specs=(hbm, hbm, hbm, hbm, vmem, hbm, hbm, vmem, hbm, hbm, hbm, hbm, hbm, hbm, vmem, vmem) + (hbm,) * 6,
        scratch_shapes=[
            pltpu.VMEM((seq, width), BF16),
            pltpu.VMEM((seq, width), BF16),
            full(w_qkv), full(w_out), full(w_gate), full(w_up), full(w_down),
            pltpu.VMEM((2,) + norms.shape, F32),
            pltpu.VMEM((seq, width), BF16),
            pltpu.VMEM((seq, width), BF16),
            pltpu.VMEM((seq, width), BF16),
            pltpu.VMEM((seq, width), BF16),
            pltpu.VMEM((seq, width), F32),
            pltpu.VMEM((seq, width), BF16),
            pltpu.VMEM((seq, 256), BF16),
            pltpu.VMEM((2, seq, 256), BF16),
            pltpu.VMEM((2, 3, 512, 768), BF16),
            pltpu.VMEM((seq, width), BF16),
            pltpu.VMEM((seq, width), F32),
            dma((9,)), dma((9,)), dma((8,)), dma((13,)), dma((2, 3)),
        ],
        compiler_params=pltpu.CompilerParams(collective_id=1, has_side_effects=True, vmem_limit_bytes=62 << 20),
    )(tokens, cotangent, w_qkv, w_out, w_gate, w_up, w_down, norms, query_marks, key_marks, cosines, sines)


RING = 4
HALVES_RING = 8
FIRST_ATTENTION = 13
FIRST_DOUBLING = 14
LATE_SLOT = 17
LATE_EVERY = 5
REMAINDER = (
    (halve, 14, 2),
    (double, 6, 4),
    (double, 8, 3),
    (halve, 13, 4),
    (double, 7, 4),
    (double, 9, 3),
    (double, 13, 0),
    (halve, 15, 1),
    (double, 10, 2),
    (double, 11, 2),
    (halve, 14, 3),
    (double, 12, 1),
    (double, 8, 4),
    (double, 9, 4),
    (halve, 15, 2),
    (double, 10, 3),
    (double, 13, 1),
    (halve, 15, 3),
    (halve, 14, 4),
    (double, 11, 3),
    (double, 12, 2),
    (double, 14, 0),
    (double, 10, 4),
    (double, 13, 2),
    (halve, 15, 4),
    (double, 15, 0),
    (double, 11, 4),
    (double, 12, 3),
    (double, 13, 3),
    (double, 14, 1),
    (double, 15, 1),
    (double, 12, 4),
    (double, 13, 4),
    (double, 14, 2),
    (double, 15, 2),
    (double, 14, 3),
    (double, 15, 3),
    (double, 14, 4),
    (double, 15, 4),
)


def backward_kernel(
    tokens, context, low, mixed, hidden, slope_gate, slope_up, grad_second, unit_in, inv, norms, q_in, k_in, v_in,
    features, key_marks, cosines, sines, vec, wq, wo, wg, wu, wd,
    out, input_grad_out, vec_out,
    grads, halves, from_core, to_core, vectors, arena, total, unit, marks, key_aug, value_aug, delta_aug, dkey, dvalue,
    send_sems, recv_sems, core_send, core_recv, vec_send, vec_recv, load_sems, input_sems, extra_sems, wq_sems,
    feature_sems,
):
    rep = lax.axis_index("rep")
    core = lax.axis_index("fsdp")
    seq, width = total.shape
    shard = width // 2
    refs = (grads, halves, out, send_sems, recv_sems)

    def load(slot, source, target=None):
        return pltpu.make_async_copy(source, arena.at[slot] if target is None else target, load_sems.at[slot])

    def square(slot):
        return arena.at[slot, pl.ds(0, width), :]

    def sided(slot, source, first, second):
        return (
            pltpu.make_async_copy(
                source.at[:, aligned(first, shard, 128)], arena.at[slot, :, pl.ds(0, shard)], load_sems.at[slot]
            ),
            pltpu.make_async_copy(
                source.at[:, aligned(second, shard, 128)], arena.at[slot, :, pl.ds(shard, shard)], input_sems.at[slot]
            ),
        )

    def begin(loads):
        for one in loads if isinstance(loads, tuple) else (loads,):
            one.start()

    def finish(loads):
        for one in loads if isinstance(loads, tuple) else (loads,):
            one.wait()

    def core_copy(chunk):
        slot = lax.rem(chunk, RING)
        return pltpu.make_async_remote_copy(
            src_ref=to_core.at[slot],
            dst_ref=from_core.at[slot],
            send_sem=core_send.at[slot],
            recv_sem=core_recv.at[slot],
            device_id=other_core(),
            device_id_type=MESH,
        )

    def emit(chunk, left, right):
        slot = lax.rem(chunk, RING)

        @pl.when(chunk >= RING)
        def _():
            core_copy(chunk - RING).wait_send()

        to_core[slot] = tn(arena[left, :, shard:], arena[right]).astype(BF16)
        core_copy(chunk).start()
        grads[chunk] = tn(arena[left, :, :shard], arena[right]).astype(BF16)

    def absorb(chunk):
        core_copy(chunk).wait_recv()
        slot = lax.rem(chunk, RING)
        grads[chunk] = (grads[chunk].astype(F32) + from_core[slot].astype(F32)).astype(BF16)

    def slot_work(slot, doubling):
        for stage in range(STEPS, -1, -1):
            if doubling:
                out_chunk = slot - FIRST_DOUBLING - 2 * stage

                @pl.when((out_chunk >= 0) & (out_chunk < fed + 1))
                def _():
                    double(refs, out_chunk, stage)

            chunk = slot - 1 - 3 * stage

            @pl.when((chunk >= 0) & (chunk < fed + 1))
            def _():
                halve(refs, chunk, stage)

            if doubling:
                late = slot - LATE_SLOT - 3 * stage

                @pl.when((late >= 0) & (lax.rem(late, LATE_EVERY) == 0))
                def _():
                    halve(refs, fed + 1 + lax.div(late, LATE_EVERY), stage)

    MIXED, LOW, SLOPE_GATE, SLOPE_UP, HIDDEN, GATE, UP, WD, WG, WU, SIDED_CONTEXT, WO, CONTEXT = range(13)
    ATTENDED, Q, K, V, GRAD_CONTEXT, PROJECTED, TOKENS, WQ = MIXED, SLOPE_GATE, SLOPE_UP, WD, HIDDEN, GATE, WG, WU
    blocks = wg.shape[1] // width
    fed = 3 * blocks

    def block_loads(j):
        cols = aligned(j * width, width)
        return {
            SLOPE_GATE: load(SLOPE_GATE, slope_gate.at[:, cols]),
            SLOPE_UP: load(SLOPE_UP, slope_up.at[:, cols]),
            WD: load(WD, wd.at[cols, :], square(WD)),
            WG: load(WG, wg.at[:, cols], square(WG)),
            WU: load(WU, wu.at[:, cols], square(WU)),
            HIDDEN: sided(
                HIDDEN,
                hidden,
                core * (wd.shape[0] // 2) + j * shard,
                (1 - core) * (wd.shape[0] // 2) + j * shard,
            ),
        }

    def wq_loads(turn_number):
        part = width // 3
        return tuple(
            pltpu.make_async_copy(
                wq.at[:, aligned(n * width + turn_number * part, part)],
                arena.at[WQ, pl.ds(0, width), pl.ds(n * part, part)],
                wq_sems.at[n],
            )
            for n in range(3)
        )

    def feature_load(pair):
        slot = lax.rem(pair, 2)
        return pltpu.make_async_copy(
            features.at[pl.ds(2 * pair, 2)], marks.at[slot], feature_sems.at[slot]
        )

    first_loads = block_loads(0)
    mixed_load = load(MIXED, mixed)
    low_load = sided(LOW, low, core * shard, (1 - core) * shard)
    second_load = pltpu.make_async_copy(grad_second, total, extra_sems.at[0])
    unit_load = pltpu.make_async_copy(unit_in, unit, extra_sems.at[1])
    context_load = load(CONTEXT, context)
    sided_load = sided(SIDED_CONTEXT, context, core * shard, (1 - core) * shard)
    wo_load = load(WO, wo, square(WO))
    late_loads = {
        Q: load(Q, q_in),
        K: load(K, k_in),
        V: load(V, v_in),
        TOKENS: sided(TOKENS, tokens, core * shard, (1 - core) * shard),
    }
    for one in (mixed_load, first_loads[WD], first_loads[SLOPE_GATE], first_loads[SLOPE_UP], first_loads[HIDDEN],
                low_load, first_loads[WG], second_load, first_loads[WU], sided_load, wo_load, unit_load, context_load,
                feature_load(0)):
        begin(one)
    vectors[0] = vec[...]
    greet()
    finish(mixed_load)

    tile = 512

    def feed_step(j, carry):
        loads = block_loads(j)
        upcoming = block_loads(j + 1)
        more = j + 1 < blocks

        def renew(*slots):
            @pl.when(more)
            def _():
                for slot in slots:
                    begin(upcoming[slot])

        def replace(*slots):
            @pl.when(jnp.logical_not(more))
            def _():
                for slot in slots:
                    begin(late_loads[slot])

        for slot in (WD, SLOPE_GATE, SLOPE_UP):
            finish(loads[slot])
        for r in range(seq // tile):
            rows = pl.ds(r * tile, tile)
            grad_hidden = nt(arena[MIXED, rows, :], arena[WD, :width, :])
            arena[GATE, rows, :] = (grad_hidden * arena[SLOPE_GATE, rows, :].astype(F32)).astype(BF16)
            arena[UP, rows, :] = (grad_hidden * arena[SLOPE_UP, rows, :].astype(F32)).astype(BF16)
        renew(WD, SLOPE_GATE, SLOPE_UP)
        replace(Q, K, V)
        finish(loads[HIDDEN])
        emit(3 * j, HIDDEN, MIXED)
        renew(HIDDEN)

        @pl.when(j > 0)
        def _():
            absorb(3 * j - 1)
            slot_work(3 * j, False)

        @pl.when(j == 0)
        def _():
            finish(low_load)
            finish(second_load)

        emit(3 * j + 1, LOW, GATE)
        finish(loads[WG])
        for r in range(seq // tile):
            rows = pl.ds(r * tile, tile)
            total[rows, :] += nt(arena[GATE, rows, :], arena[WG, :width, :])
        renew(WG)
        replace(TOKENS)
        absorb(3 * j)
        slot_work(3 * j + 1, False)
        emit(3 * j + 2, LOW, UP)
        finish(loads[WU])
        for r in range(seq // tile):
            rows = pl.ds(r * tile, tile)
            total[rows, :] += nt(arena[UP, rows, :], arena[WU, :width, :])
        renew(WU)
        absorb(3 * j + 1)
        slot_work(3 * j + 2, False)
        return carry

    lax.fori_loop(0, blocks, feed_step, 0)

    begin(wq_loads(0))
    finish(unit_load)
    gain_one = jnp.concatenate([norms[0, 0:1, :], norms[1, 0:1, :]], axis=1)
    bias_sum = jnp.zeros((1, width), F32)
    gain_sum = jnp.zeros((1, width), F32)
    block = 256
    for r in range(seq // block):
        rows = pl.ds(r * block, block)
        grad_normed = total[rows, :]
        unit_rows = unit[rows, :]
        bias_sum += jnp.sum(grad_normed, axis=0, keepdims=True)
        gain_sum += jnp.sum(grad_normed * unit_rows, axis=0, keepdims=True)
        scaled = grad_normed * gain_one
        grad_first = inv[rows, 0:1] * (scaled - row_mean(scaled) - unit_rows * row_mean(scaled * unit_rows))
        total[rows, :] = grad_first
        arena[ATTENDED, rows, :] = grad_first.astype(BF16)
    vectors[0, 0:1, :] = gain_sum
    vectors[0, 1:2, :] = bias_sum
    finish(sided_load)
    emit(fed, SIDED_CONTEXT, ATTENDED)
    finish(wo_load)
    absorb(fed - 1)
    slot_work(fed, False)
    for r in range(seq // tile):
        rows = pl.ds(r * tile, tile)
        arena[GRAD_CONTEXT, rows, :] = nt(arena[ATTENDED, rows, :], arena[WO, :width, :]).astype(BF16)
    absorb(fed)
    for one in (context_load, late_loads[Q], late_loads[K], late_loads[V], late_loads[TOKENS]):
        finish(one)

    steps = [(a, r) for r in range(2) for a in range(2)]
    ones = jnp.where((lanes() >= SPLIT_LANE) & (lanes() < SPLIT_LANE + 3), 1.0, 0.0)
    part = width // 3

    def half_step(turn_number, number, carry):
        pair = 2 * turn_number + lax.div(number, 2)
        half = lax.rem(number, 2)
        place = lax.div(number, 2) * 128
        cols = aligned(pair * 128, 128)
        mark_slot = lax.rem(pair, 2)

        @pl.when(half == 0)
        def _():
            feature_load(pair).wait()

            @pl.when(pair + 1 < HEADS // 2)
            def _():
                feature_load(pair + 1).start()

            key_aug[:, :128] = arena[K, :, cols]
            key_aug[:, 128:] = (key_marks[...].astype(F32) + ones).astype(BF16)
            value_aug[:, :128] = arena[V, :, cols]
            value_aug[:, 128:] = jnp.broadcast_to(ones, (seq, 128)).astype(BF16)
            delta = arena[GRAD_CONTEXT, :, cols].astype(F32) * arena[CONTEXT, :, cols].astype(F32)
            for a in range(2):
                row_delta = jnp.sum(head_mask(delta, a == 0), axis=1, keepdims=True)
                delta_aug[a, :, :128] = head_mask(arena[GRAD_CONTEXT, :, cols], a == 0)
                delta_aug[a, :, 128:] = split_lanes(jnp.zeros((seq, 128), F32), -row_delta)
            dkey[...] = jnp.zeros_like(dkey)
            dvalue[...] = jnp.zeros_like(dvalue)

        def rows_of(r):
            return aligned(half * (seq // 2) + r * block, block)

        def products_of(a, r):
            rows = rows_of(r)
            query = jnp.concatenate([head_mask(arena[Q, rows, cols], a == 0), marks[mark_slot, a, rows, :]], axis=1)
            return nt(query, key_aug[...]), nt(delta_aug[a, rows, :], value_aug[...])

        upcoming = products_of(*steps[0])
        dquery = [None, None]
        for n, (a, r) in enumerate(steps):
            rows = rows_of(r)
            scores, grad_probs = upcoming
            upcoming = products_of(*steps[n + 1]) if n + 1 < len(steps) else None
            probs = jnp.exp(scores)
            grad_scores = (probs * grad_probs).astype(BF16)
            probs = probs.astype(BF16)
            dquery[a] = nn(grad_scores, head_mask(key_aug[:, :128], a == 0))
            dkey[...] += tn(grad_scores, head_mask(arena[Q, rows, cols], a == 0))
            dvalue[...] += tn(probs, delta_aug[a, rows, :128])
            if a == 1:
                turned = turn((dquery[0] + dquery[1]) * (HEAD_DIM ** (-0.5)), cosines[rows, :], -sines[rows, :])
                arena[PROJECTED, rows, aligned(place, 128)] = turned.astype(BF16)

        @pl.when(half == 1)
        def _():
            turned = turn(dkey[...], cosines[...], -sines[...])
            arena[PROJECTED, :, aligned(part + place, 128)] = turned.astype(BF16)
            arena[PROJECTED, :, aligned(2 * part + place, 128)] = dvalue[...].astype(BF16)

        slot_work(FIRST_ATTENTION + LATE_EVERY * turn_number + number, True)
        for stage in range(VECTOR_STEPS + 1):

            @pl.when(4 * turn_number + number == stage)
            def _():
                vector_stage(vectors, vec_send, vec_recv, stage)

        return carry

    def turn_step(turn_number, carry):
        lax.fori_loop(0, 4, functools.partial(half_step, turn_number), 0)
        chunk = fed + 1 + turn_number
        emit(chunk, TOKENS, PROJECTED)
        finish(wq_loads(turn_number))
        for r in range(seq // tile):
            rows = pl.ds(r * tile, tile)
            total[rows, :] += nt(arena[PROJECTED, rows, :], arena[WQ, :width, :])

        @pl.when(turn_number < 2)
        def _():
            begin(wq_loads(turn_number + 1))

        absorb(chunk)
        slot_work(LATE_SLOT + LATE_EVERY * turn_number, True)
        return carry

    lax.fori_loop(0, 3, turn_step, 0)

    half = seq // 2
    mine = pltpu.make_async_copy(total.at[aligned(core * half, half)], input_grad_out.at[core], extra_sems.at[2])
    theirs = pltpu.make_async_remote_copy(
        src_ref=total.at[aligned((1 - core) * half, half)],
        dst_ref=input_grad_out.at[core],
        send_sem=core_send.at[RING],
        recv_sem=core_recv.at[RING],
        device_id=other_core(),
        device_id_type=MESH,
    )
    mine.start()
    theirs.start()
    vec_out[...] = vectors[2 * VECTOR_STEPS]
    for work, chunk, stage in REMAINDER:
        work(refs, chunk, stage)
    mine.wait()
    theirs.wait()
    for number in range(RING):
        core_copy(CHUNKS - RING + number).wait_send()


def backward(tokens, saved, norms, key_marks, cosines, sines, vec, weights, outs):
    context, low, mixed, hidden, slope_gate, slope_up, grad_second, unit, inv, q, k, v, features = saved
    seq, width = tokens.shape
    dma = pltpu.SemaphoreType.DMA
    vmem = pl.BlockSpec(memory_space=pltpu.VMEM)
    hbm = pl.BlockSpec(memory_space=pl.ANY)
    chunks = (CHUNKS, width // 2, width)
    return pl.pallas_call(
        backward_kernel,
        out_shape=(
            jax.ShapeDtypeStruct(chunks, BF16),
            jax.ShapeDtypeStruct(outs, F32),
            jax.ShapeDtypeStruct(vec.shape, F32),
        ),
        in_specs=[hbm] * 9 + [vmem] * 2 + [hbm] * 4 + [vmem] * 4 + [hbm] * 5,
        out_specs=(hbm, hbm, vmem),
        scratch_shapes=[
            pltpu.VMEM(chunks, BF16),
            pltpu.VMEM((HALVES_RING,) + chunks[1:], BF16),
            pltpu.VMEM((RING,) + chunks[1:], BF16),
            pltpu.VMEM((RING,) + chunks[1:], BF16),
            pltpu.VMEM((2 * VECTOR_STEPS + 1,) + vec.shape, F32),
            pltpu.VMEM((13, seq, width), BF16),
            pltpu.VMEM((seq, width), F32),
            pltpu.VMEM((seq, width), F32),
            pltpu.VMEM((2, 2, seq, FEATURES), BF16),
            pltpu.VMEM((seq, 256), BF16),
            pltpu.VMEM((seq, 256), BF16),
            pltpu.VMEM((2, seq, 256), BF16),
            pltpu.VMEM((seq, 128), F32),
            pltpu.VMEM((seq, 128), F32),
            dma((CHUNKS, PARTS, 2 * STEPS + 1)),
            dma((CHUNKS, PARTS, 2 * STEPS)),
            dma((RING + 1,)),
            dma((RING + 1,)),
            dma((VECTOR_STEPS,)),
            dma((VECTOR_STEPS,)),
            dma((13,)),
            dma((13,)),
            dma((3,)),
            dma((3,)),
            dma((2,)),
        ],
        compiler_params=pltpu.CompilerParams(collective_id=0, has_side_effects=True, vmem_limit_bytes=62 << 20),
    )(tokens, context, low, mixed, hidden, slope_gate, slope_up, grad_second, unit, inv, norms, q, k, v,
      features, key_marks, cosines, sines, vec, *weights)


def widen_kernel(summed, qkv, out, gate, up, down):
    step = pl.program_id(0)
    width = out.shape[1]
    part = width // 3
    fed = CHUNKS - 4
    values = summed[0].astype(F32)
    turn_of = lax.rem(step, 3)
    for ref, now in (
        (down, (step < fed) & (turn_of == 0)),
        (gate, (step < fed) & (turn_of == 1)),
        (up, (step < fed) & (turn_of == 2)),
        (out, step == fed),
    ):

        @pl.when(now)
        def _():
            ref[...] = values

    @pl.when(step > fed)
    def _():
        for n in range(3):
            qkv[:, aligned(n * width + (step - fed - 1) * part, part)] = values[:, n * part : (n + 1) * part]


def widen(summed):
    rows, cols = summed.shape[1:]
    fed = CHUNKS - 4

    def shape(high, across):
        return jax.ShapeDtypeStruct((rows * high, cols * across), F32)

    def spec(place, across=1):
        return pl.BlockSpec((rows, cols * across), place)

    def turn_of(step):
        return lax.div(jnp.minimum(step, fed - 1), 3)

    return pl.pallas_call(
        widen_kernel,
        grid=(CHUNKS,),
        out_shape=(shape(1, 3), shape(1, 1), shape(1, 4), shape(1, 4), shape(4, 1)),
        in_specs=[pl.BlockSpec((1, rows, cols), lambda step: (step, 0, 0))],
        out_specs=(
            spec(lambda step: (0, 0), 3),
            spec(lambda step: (0, 0)),
            spec(lambda step: (0, turn_of(step))),
            spec(lambda step: (0, turn_of(step))),
            spec(lambda step: (turn_of(step), 0)),
        ),
    )(summed)


def shards(
    tokens,
    lengths,
    w_qkv,
    w_out,
    w_gate,
    w_up,
    w_down,
    norm1_gain,
    norm1_bias,
    norm2_gain,
    norm2_bias,
    cotangent,
):
    core = lax.axis_index("fsdp")
    shard = norm1_gain.shape[0]
    seq_len = 2 * tokens.shape[1]
    doc_lengths = lax.dynamic_index_in_dim(lengths, core, 0, keepdims=False)
    segment, positions = doc_tables(doc_lengths, seq_len)
    cosine_table, sine_table = rope_tables(positions)
    cosines = jnp.concatenate([cosine_table] * 4, axis=1)
    sines = jnp.concatenate([-sine_table, sine_table] * 2, axis=1)
    columns = jnp.arange(FEATURES, dtype=jnp.int32)[None, :]
    same = segment[:, None] == columns
    query_marks = same.astype(BF16)
    key_marks = jnp.where(same | (columns >= SPLIT_LANE), 0.0, NEG).astype(BF16)
    zero = jnp.zeros_like(norm1_gain)
    norms = jnp.stack([norm1_gain, norm1_bias, norm2_gain, norm2_bias, zero, zero, zero, zero]).astype(F32)

    weights = (w_qkv, w_out, w_gate, w_up, w_down)
    (q, k, v, context, features, low, unit, inv, slope_gate, slope_up, hidden, grad_second, mixed, activations,
     vec, norms, stream, *weights) = forward(tokens, cotangent, weights, norms, query_marks, key_marks, cosines, sines)
    saved = (context, low, mixed, hidden, slope_gate, slope_up, grad_second, unit, inv, q, k, v, features)
    summed, input_grad, vec_sum = backward(
        stream, saved, norms, key_marks, cosines, sines, vec, weights, tokens.shape
    )
    groups = lax.axis_size("rep") // UNITS
    if groups > 1:
        alike = [[UNITS * g + n for g in range(groups)] for n in range(UNITS)]
        summed = lax.psum(summed, "rep", axis_index_groups=alike)
        vec_sum = lax.psum(vec_sum, "rep", axis_index_groups=alike)
    vec_own = lax.dynamic_slice_in_dim(vec_sum, core * shard, shard, axis=1)
    return (activations, input_grad, *widen(summed), vec_own[0], vec_own[1], vec_own[2], vec_own[3])


def solution(mesh):
    placed = (
        P("rep", "fsdp", None),
        P("rep", None),
        P("fsdp", None),
        P("fsdp", None),
        P("fsdp", None),
        P("fsdp", None),
        P("fsdp", None),
        P("fsdp"),
        P("fsdp"),
        P("fsdp"),
        P("fsdp"),
        P("rep", "fsdp", None),
    )
    return jax.shard_map(
        shards,
        mesh=mesh,
        in_specs=placed,
        out_specs=(
            P("rep", "fsdp", None),
            P("rep", "fsdp", None),
            P("fsdp", None),
            P("fsdp", None),
            P("fsdp", None),
            P("fsdp", None),
            P("fsdp", None),
            P("fsdp"),
            P("fsdp"),
            P("fsdp"),
            P("fsdp"),
        ),
        check_vma=False,
    )
```

```python
import functools

import jax
import jax.numpy as jnp
import numpy as np
from jax import lax
from jax.experimental import pallas as pl
from jax.experimental.pallas import tpu as pltpu
from jax.sharding import PartitionSpec as P

HEADS = 12
HEAD_DIM = 64


EPSILON = 1e-05


CHUNKS = 16
PARTS = 3
PART_ROWS = 128
UNITS = 16
STEPS = 4
HALVES_RING = 8
MESH = pl.DeviceIdType.MESH
BF16 = jnp.bfloat16
F32 = jnp.float32


def bit_of(value, weight):
    return lax.rem(lax.div(value, weight), 2)


def orders(chunk):
    rep = lax.axis_index("rep")
    odd = lax.rem(jnp.asarray(chunk, jnp.int32), 2)
    first, second = 1 + odd, 2 - odd
    bits = {1: bit_of(rep, 1), 2: bit_of(rep, 2), 4: bit_of(rep, 4), 8: bit_of(rep, 8)}
    first_bit = bits[1] * (1 - odd) + bits[2] * odd
    second_bit = bits[2] * (1 - odd) + bits[1] * odd
    return (
        ((1, bits[1]), (2, bits[2]), (4, bits[4]), (8, bits[8])),
        ((2, bits[2]), (1, bits[1]), (4, bits[4]), (8, bits[8])),
        ((4, bits[4]), (first, first_bit), (second, second_bit), (8, bits[8])),
    )


def partner_of(weight, bit):
    return (lax.axis_index("rep") + weight * (1 - 2 * bit), lax.axis_index("fsdp"))


def other_core():
    return (lax.axis_index("rep"), 1 - lax.axis_index("fsdp"))


def region(ref, chunk, part, order, level, flip):
    rows = PART_ROWS >> min(level, STEPS - 1)
    start = part * PART_ROWS
    for step in range(level):
        bit = order[step][1]
        if flip and step == level - 1:
            bit = 1 - bit
        if step < STEPS - 1:
            start = start + bit * (PART_ROWS >> (step + 1))
        else:
            column = bit * (ref.shape[2] // 2)
    start = pl.multiple_of(start, 16)
    if level < STEPS:
        return (chunk, pl.ds(start, rows), slice(None))
    half = ref.shape[2] // 2
    return (chunk, pl.ds(start, rows), pl.ds(pl.multiple_of(column, 128), half))


def ring_slot(chunk):
    return lax.rem(jnp.asarray(chunk, jnp.int32), HALVES_RING)


def landing(ref, chunk, part, step):
    start = part * PART_ROWS + PART_ROWS - (PART_ROWS >> step)
    chunk = ring_slot(chunk)
    if step < STEPS - 1:
        return (chunk, pl.ds(start, PART_ROWS >> (step + 1)), slice(None))
    return (chunk, pl.ds(start, PART_ROWS >> step), pl.ds(0, ref.shape[2] // 2))


def halving_copy(refs, chunk, part, order, step):
    grads, halves, _, send_sems, recv_sems = refs
    slot = ring_slot(chunk)
    return pltpu.make_async_remote_copy(
        src_ref=grads.at[region(grads, chunk, part, order, step + 1, True)],
        dst_ref=halves.at[landing(halves, chunk, part, step)],
        send_sem=send_sems.at[slot, step],
        recv_sem=recv_sems.at[slot, step],
        device_id=partner_of(*order[step]),
        device_id_type=MESH,
    )


def all_parts(ref, first, step):
    rows = PARTS * (PART_ROWS >> min(step + 1, STEPS - 1))
    columns = ref.shape[2] if step < STEPS - 1 else ref.shape[2] // 2
    return ref.at[first, pl.ds(0, rows), pl.ds(0, columns)]


def wait_parts(ref, first, step, send_sem, recv_sem):
    whole = all_parts(ref, first, step)
    pltpu.make_async_remote_copy(
        src_ref=whole,
        dst_ref=whole,
        send_sem=send_sem,
        recv_sem=recv_sem,
        device_id=other_core(),
        device_id_type=MESH,
    ).wait()


def halving_add(refs, chunk, part, order, step):
    grads, halves = refs[:2]
    kept = region(grads, chunk, part, order, step + 1, False)
    theirs = halves[landing(halves, chunk, part, step)]
    grads[kept] = (grads[kept].astype(F32) + theirs.astype(F32)).astype(BF16)


def settle_copy(refs, chunk, part, order):
    grads, _, out, send_sems, _ = refs
    mine = region(grads, chunk, part, order, STEPS, False)
    return pltpu.make_async_copy(grads.at[mine], out.at[mine], send_sems.at[ring_slot(chunk), 2 * STEPS])


def doubling_copy(refs, chunk, part, order, step):
    grads, _, out, send_sems, recv_sems = refs
    slot = ring_slot(chunk)
    mine = region(out, chunk, part, order, step + 1, False)
    return pltpu.make_async_remote_copy(
        src_ref=(grads if step == STEPS - 1 else out).at[mine],
        dst_ref=out.at[mine],
        send_sem=send_sems.at[slot, STEPS + step],
        recv_sem=recv_sems.at[slot, STEPS + step],
        device_id=partner_of(*order[step]),
        device_id_type=MESH,
    )


def halve(refs, chunk, stage):
    _, halves, _, send_sems, recv_sems = refs
    slot = ring_slot(chunk)
    if stage > 0:
        wait_parts(halves, slot, stage - 1, send_sems.at[slot, stage - 1], recv_sems.at[slot, stage - 1])
    for part, order in enumerate(orders(chunk)):
        if stage > 0:
            halving_add(refs, chunk, part, order, stage - 1)
        if stage < STEPS:
            halving_copy(refs, chunk, part, order, stage).start()
        else:
            settle_copy(refs, chunk, part, order).start()


def double(refs, chunk, stage):
    grads, _, out, send_sems, recv_sems = refs
    slot = ring_slot(chunk)
    if stage > 0:
        sems = send_sems.at[slot, 2 * STEPS - stage], recv_sems.at[slot, 2 * STEPS - stage]
        wait_parts(out, chunk, STEPS - stage, *sems)
    if stage == 1:
        sizes = [all_parts(ref, chunk, STEPS - 1) for ref in (grads, out)]
        pltpu.make_async_copy(*sizes, send_sems.at[slot, 2 * STEPS]).wait()
    if stage < STEPS:
        for part, order in enumerate(orders(chunk)):
            doubling_copy(refs, chunk, part, order, STEPS - 1 - stage).start()


def greet():
    rep = lax.axis_index("rep")
    barrier = pltpu.get_barrier_semaphore()
    pl.semaphore_signal(barrier, inc=1, device_id=other_core(), device_id_type=MESH)
    for weight in (1, 2, 4, 8):
        there = partner_of(weight, bit_of(rep, weight))
        pl.semaphore_signal(barrier, inc=1, device_id=there, device_id_type=MESH)
    pl.semaphore_wait(barrier, 5)


def vector_copy(vectors, send_sems, recv_sems, step):
    rep = lax.axis_index("rep")
    if step == 0:
        there = other_core()
    else:
        weight = 1 << (step - 1)
        there = partner_of(weight, bit_of(rep, weight))
    return pltpu.make_async_remote_copy(
        src_ref=vectors.at[2 * step],
        dst_ref=vectors.at[2 * step + 1],
        send_sem=send_sems.at[step],
        recv_sem=recv_sems.at[step],
        device_id=there,
        device_id_type=MESH,
    )


VECTOR_STEPS = 5


def vector_stage(vectors, send_sems, recv_sems, stage):
    if stage > 0:
        vector_copy(vectors, send_sems, recv_sems, stage - 1).wait()
        vectors[2 * stage] = vectors[2 * stage - 2] + vectors[2 * stage - 1]
    if stage < VECTOR_STEPS:
        vector_copy(vectors, send_sems, recv_sems, stage).start()


SEQ_ROWS = 512
NEG = -1e30
FEATURES = 128
SPLIT_LANE = 8


def nn(left, right):
    return jnp.dot(left, right, preferred_element_type=F32)


def nt(left, right):
    return lax.dot_general(left, right, (((1,), (1,)), ((), ())), preferred_element_type=F32)


def tn(left, right):
    return lax.dot_general(left, right, (((0,), (0,)), ((), ())), preferred_element_type=F32)


def aligned(start, size, multiple=None):
    return pl.ds(pl.multiple_of(start, multiple or size), size)


def lanes():
    return lax.broadcasted_iota(jnp.int32, (1, 128), 1)


def head_mask(values, first):
    low = lanes() < HEAD_DIM
    zero = jnp.zeros_like(values)
    return jnp.where(low, values, zero) if first else jnp.where(low, zero, values)


def turn(values, cosines, sines):
    first = lax.rem(lanes(), HEAD_DIM) < HEAD_DIM // 2
    swapped = jnp.where(first, pltpu.roll(values, 96, 1), pltpu.roll(values, 32, 1))
    return values * cosines + swapped * sines


def split_lanes(base, values):
    high = values.astype(BF16).astype(F32)
    middle = (values - high).astype(BF16).astype(F32)
    low = values - high - middle
    lane = lanes()
    out = jnp.where(lane == SPLIT_LANE, high, base)
    out = jnp.where(lane == SPLIT_LANE + 1, middle, out)
    return jnp.where(lane == SPLIT_LANE + 2, low, out).astype(BF16)


def row_mean(values):
    return jnp.mean(values, axis=1, keepdims=True)


def forward_kernel(
    tokens, cotangent, w_qkv, w_out, w_gate, w_up, w_down, norms, lengths, frequencies,
    q_out, k_out, v_out, context_out, features_out, low_out, unit_out, inv_out, slope_gate_out, slope_up_out,
    hidden_out, grad_second_out, mixed_out, activations_out, vec_out,
    norms_out, key_marks, cosines, sines, x_out, wq_out, wo_out, wg_out, wu_out, wd_out,
    x, g, wq, wo, wg, wu, wd, nv, qs, ks, vs, ctx, total, key_aug, value_aug, pieces, seconds,
    query_marks, marks, products, send_sems, recv_sems, own_sems, save_sems, act_sems, mark_sems,
):
    rep = lax.axis_index("rep")
    core = lax.axis_index("fsdp")
    there = (rep, 1 - core)
    seq, width = x.shape
    half = seq // 2

    barrier = pltpu.get_barrier_semaphore()
    pl.semaphore_signal(barrier, inc=1, device_id=there, device_id_type=MESH)
    pl.semaphore_wait(barrier, 1)

    def rows_of(ref, block):
        return ref.at[aligned(core * block, block)]

    exchanges = (
        (tokens.at[core], tokens.at[1 - core], rows_of(x, half)),
        (w_qkv, w_qkv, rows_of(wq, w_qkv.shape[0])),
        (w_out, w_out, rows_of(wo, w_out.shape[0])),
        (norms, norms, nv.at[core]),
        (w_gate, w_gate, rows_of(wg, w_gate.shape[0])),
        (w_up, w_up, rows_of(wu, w_up.shape[0])),
        (w_down, w_down, rows_of(wd, w_down.shape[0])),
        (cotangent.at[core], cotangent.at[1 - core], rows_of(g, half)),
    )

    def copies(number):
        mine, theirs, place = exchanges[number]
        return (
            pltpu.make_async_copy(mine, place, own_sems.at[number]),
            pltpu.make_async_remote_copy(
                src_ref=theirs,
                dst_ref=place,
                send_sem=send_sems.at[number],
                recv_sem=recv_sems.at[number],
                device_id=there,
                device_id_type=MESH,
            ),
        )

    for number in range(len(exchanges)):
        for copy in copies(number):
            copy.start()

    def arrived(number):
        for copy in copies(number):
            copy.wait()

    def save(source, target, number):
        copy = pltpu.make_async_copy(source, target, save_sems.at[number])
        copy.start()
        return copy

    places = lax.broadcasted_iota(jnp.int32, (seq, 128), 0)
    segment = jnp.zeros_like(places)
    begins = jnp.zeros_like(places)
    doc_end = jnp.int32(0)
    for doc in range(lengths.shape[1]):
        doc_end = doc_end + lengths[core, doc]
        past = places >= doc_end
        segment = segment + past.astype(jnp.int32)
        begins = jnp.where(past, doc_end, begins)
    same = segment == lanes()
    query_marks[...] = jnp.where(same, 1.0, 0.0).astype(BF16)
    key_marks[...] = jnp.where(same | (lanes() >= SPLIT_LANE), 0.0, NEG).astype(BF16)
    angles = (places - begins).astype(F32) * frequencies[0:1, :]
    cosines[...] = jnp.cos(angles)
    side = jnp.where(lax.rem(lanes(), HEAD_DIM) < HEAD_DIM // 2, -1.0, 1.0)
    sines[...] = jnp.sin(angles) * side

    arrived(0)
    arrived(1)
    tile = 512
    for n, out in enumerate((qs, ks, vs)):
        for r in range(seq // tile):
            rows = pl.ds(r * tile, tile)
            product_rows = nn(x[rows, :], wq[:, pl.ds(n * width, width)])
            if n == 2:
                out[rows, :] = product_rows.astype(BF16)
                continue
            for pair in range(width // 128):
                cols = slice(pair * 128, pair * 128 + 128)
                turned = turn(product_rows[:, cols], cosines[rows, :], sines[rows, :]).astype(BF16)
                if n == 0:
                    turned = turned * jnp.asarray(HEAD_DIM ** (-0.5), BF16)
                out[rows, cols] = turned
    saves = {12: save(x, x_out, 12), 0: save(qs, q_out, 0), 1: save(ks, k_out, 1), 2: save(vs, v_out, 2)}

    saves[7] = save(wq, wq_out, 7)

    block = 256
    steps = [(a, r) for r in range(seq // block) for a in range(2)]

    def mark_copy(pair):
        slot = lax.rem(pair, 2)
        return pltpu.make_async_copy(marks.at[slot], features_out.at[pl.ds(2 * pair, 2)], mark_sems.at[slot])

    weight_saves = [
        pltpu.make_async_copy(source, target, save_sems.at[8 + number])
        for number, (source, target) in enumerate(((wo, wo_out), (wg, wg_out), (wu, wu_out), (wd, wd_out)))
    ]

    def pair_step(pair, carry):
        for number, turn_number in enumerate((1, 2, 3, 4)):

            @pl.when(pair == turn_number)
            def _():
                arrived((2, 4, 5, 6)[number])
                weight_saves[number].start()

        cols = aligned(pair * 128, 128)
        mark_slot = lax.rem(pair, 2)

        @pl.when(pair >= 2)
        def _():
            mark_copy(pair - 2).wait()

        key_aug[:, :128] = ks[:, cols]
        key_aug[:, 128:] = key_marks[...]
        for a in range(2):
            value_aug[a, :, :128] = head_mask(vs[:, cols], a == 0)
            value_aug[a, :, 128:] = jnp.ones((seq, 128), BF16)

        def scores_of(a, r):
            rows = pl.ds(r * block, block)
            query = jnp.concatenate([head_mask(qs[rows, cols], a == 0), query_marks[rows, :]], axis=1)
            return nt(query, key_aug[...])

        scores = scores_of(*steps[0])
        parts = [None, None]
        for number, (a, r) in enumerate(steps):
            rows = pl.ds(r * block, block)
            upcoming = scores_of(*steps[number + 1]) if number + 1 < len(steps) else None
            row_max = jnp.max(scores, axis=1, keepdims=True)
            probs = jnp.exp(scores - row_max).astype(BF16)
            summed = nn(probs, value_aug[a])
            row_total = summed[:, 128:]
            parts[a] = summed[:, :128] / row_total
            lse = row_max + jnp.log(row_total)
            marks[mark_slot, a, rows, :] = split_lanes(query_marks[rows, :].astype(F32), -lse)
            if a == 1:
                ctx[rows, cols] = (parts[0] + parts[1]).astype(BF16)
            scores = upcoming
        mark_copy(pair).start()
        return carry

    lax.fori_loop(0, HEADS // 2, pair_step, 0)
    saves[3] = save(ctx, context_out, 3)

    low = qs
    saves[0].wait()
    arrived(3)

    def vector(n):
        return jnp.concatenate([nv[0, n : n + 1, :], nv[1, n : n + 1, :]], axis=1)

    for r in range(seq // block):
        rows = pl.ds(r * block, block)
        first_sum = x[rows, :].astype(F32) + nn(ctx[rows, :], wo[...])
        centre = first_sum - row_mean(first_sum)
        inv = lax.rsqrt(row_mean(centre * centre) + EPSILON)
        unit = centre * inv
        normed = unit * vector(0) + vector(1)
        seconds[rows, :] = unit
        inv_out[rows, :] = jnp.broadcast_to(inv, (block, 128))
        total[rows, :] = normed
        low[rows, :] = normed.astype(BF16)
    saves[4] = save(seconds, unit_out, 4)
    saves[5] = save(low, low_out, 5)

    columns = pieces.shape[3]
    row_tiles = seq // tile
    count = row_tiles * (wg.shape[1] // columns)
    outs = (slope_gate_out, slope_up_out, hidden_out)

    def piece_copy(number, n):
        slot = lax.rem(number, 2)
        rows = aligned(lax.rem(number, row_tiles) * tile, tile)
        cols = aligned(lax.div(number, row_tiles) * columns, columns)
        return pltpu.make_async_copy(pieces.at[slot, n], outs[n].at[rows, cols], act_sems.at[slot, n])

    def multiply(number, slot):
        rows = aligned(lax.rem(number, row_tiles) * tile, tile)
        cols = aligned(lax.div(number, row_tiles) * columns, columns)
        products[slot, 0] = nn(low[rows, :], wg[:, cols])
        products[slot, 1] = nn(low[rows, :], wu[:, cols])

    def take(number, slot):
        rows = aligned(lax.rem(number, row_tiles) * tile, tile)
        cols = aligned(lax.div(number, row_tiles) * columns, columns)
        gate = products[slot, 0]
        up = products[slot, 1]
        gate_sig = 0.5 + 0.5 * jnp.tanh(0.5 * gate)
        gate_silu = gate * gate_sig
        pieces[slot, 0] = (up * (gate_sig + gate_silu * (1.0 - gate_sig))).astype(BF16)
        pieces[slot, 1] = gate_silu.astype(BF16)
        hidden = (gate_silu * up).astype(BF16)
        pieces[slot, 2] = hidden
        for n in range(3):
            piece_copy(number, n).start()
        total[rows, :] += nn(hidden, wd[cols, :])

    def feed_step(turn_number, carry):
        number = 2 * turn_number

        @pl.when(turn_number > 0)
        def _():
            for n in range(3):
                piece_copy(number - 2, n).wait()
                piece_copy(number - 1, n).wait()

        multiply(number + 1, 1)
        take(number, 0)
        multiply(jnp.minimum(number + 2, count - 1), 0)
        take(number + 1, 1)
        return carry

    multiply(jnp.int32(0), 0)
    lax.fori_loop(0, count // 2, feed_step, 0)

    acts = ctx
    saves[3].wait()
    arrived(7)
    saves[2].wait()
    saves[4].wait()
    gain_two, bias_two = vector(2), vector(3)
    bias_sum = jnp.zeros((1, width), F32)
    gain_sum = jnp.zeros((1, width), F32)
    for r in range(seq // block):
        rows = pl.ds(r * block, block)
        second_sum = total[rows, :]
        centre = second_sum - row_mean(second_sum)
        inv = lax.rsqrt(row_mean(centre * centre) + EPSILON)
        unit = centre * inv
        acts[rows, :] = (unit * gain_two + bias_two).astype(BF16)
        grad_out = g[rows, :].astype(F32)
        bias_sum += jnp.sum(grad_out, axis=0, keepdims=True)
        gain_sum += jnp.sum(grad_out * unit, axis=0, keepdims=True)
        scaled = grad_out * gain_two
        grad_second = inv * (scaled - row_mean(scaled) - unit * row_mean(scaled * unit))
        seconds[rows, :] = grad_second
        vs[rows, :] = grad_second.astype(BF16)
    norms_out[...] = nv[...]
    vec_out[...] = jnp.zeros_like(vec_out)
    vec_out[2:3, :] = gain_sum
    vec_out[3:4, :] = bias_sum
    del saves[0], saves[3]
    saves[4] = save(seconds, grad_second_out, 4)
    saves[2] = save(vs, mixed_out, 2)

    mine = pltpu.make_async_copy(rows_of(acts, half), activations_out.at[core], save_sems.at[6])
    mine.start()
    theirs = pltpu.make_async_remote_copy(
        src_ref=acts.at[aligned((1 - core) * half, half)],
        dst_ref=activations_out.at[core],
        send_sem=send_sems.at[len(exchanges)],
        recv_sem=recv_sems.at[len(exchanges)],
        device_id=there,
        device_id_type=MESH,
    )
    theirs.start()
    for copy in list(saves.values()) + weight_saves:
        copy.wait()
    for pair in range(HEADS // 2 - 2, HEADS // 2):
        mark_copy(pair).wait()
    for number in range(2):
        for n in range(3):
            piece_copy(count - 2 + number, n).wait()
    mine.wait()
    theirs.wait()


def forward(tokens, cotangent, weights, norms, lengths):
    w_qkv, w_out, w_gate, w_up, w_down = weights
    seq, width = 2 * tokens.shape[1], tokens.shape[2]
    hidden_width = w_gate.shape[1]
    dma = pltpu.SemaphoreType.DMA
    vmem = pl.BlockSpec(memory_space=pltpu.VMEM)
    hbm = pl.BlockSpec(memory_space=pl.ANY)

    def shape(*dims, dtype=BF16):
        return jax.ShapeDtypeStruct(dims, dtype)

    lane = np.arange(128) % (HEAD_DIM // 2)
    frequencies = np.broadcast_to(1000.0 ** (-2.0 * lane / HEAD_DIM), (8, 128)).astype(np.float32)

    def full(shard):
        return pltpu.VMEM((2 * shard.shape[0], shard.shape[1]), BF16)

    rows = shape(seq, width)
    wide = shape(seq, hidden_width)
    return pl.pallas_call(
        forward_kernel,
        out_shape=(
            rows, rows, rows, rows, shape(HEADS, seq, FEATURES), rows, shape(seq, width, dtype=F32),
            shape(seq, 128, dtype=F32), wide, wide, wide, shape(seq, width, dtype=F32), rows,
            shape(*tokens.shape), shape(8, width, dtype=F32), shape(2, *norms.shape, dtype=F32),
            shape(seq, FEATURES), shape(seq, 128, dtype=F32), shape(seq, 128, dtype=F32), rows,
        )
        + tuple(shape(2 * shard.shape[0], shard.shape[1]) for shard in weights),
        in_specs=[hbm] * 8 + [pl.BlockSpec(memory_space=pltpu.SMEM), vmem],
        out_specs=(hbm, hbm, hbm, hbm, hbm, hbm, hbm, vmem, hbm, hbm, hbm, hbm, hbm, hbm, vmem, vmem)
        + (vmem,) * 3
        + (hbm,) * 6,
        scratch_shapes=[
            pltpu.VMEM((seq, width), BF16),
            pltpu.VMEM((seq, width), BF16),
            full(w_qkv), full(w_out), full(w_gate), full(w_up), full(w_down),
            pltpu.VMEM((2,) + norms.shape, F32),
            pltpu.VMEM((seq, width), BF16),
            pltpu.VMEM((seq, width), BF16),
            pltpu.VMEM((seq, width), BF16),
            pltpu.VMEM((seq, width), BF16),
            pltpu.VMEM((seq, width), F32),
            pltpu.VMEM((seq, 256), BF16),
            pltpu.VMEM((2, seq, 256), BF16),
            pltpu.VMEM((2, 3, 512, 768), BF16),
            pltpu.VMEM((seq, width), F32),
            pltpu.VMEM((seq, FEATURES), BF16),
            pltpu.VMEM((2, 2, seq, FEATURES), BF16),
            pltpu.VMEM((2, 2, 512, 768), F32),
            dma((9,)), dma((9,)), dma((8,)), dma((13,)), dma((2, 3)), dma((2,)),
        ],
        compiler_params=pltpu.CompilerParams(collective_id=1, has_side_effects=True, vmem_limit_bytes=63 << 20),
    )(tokens, cotangent, w_qkv, w_out, w_gate, w_up, w_down, norms, lengths, jnp.asarray(frequencies))


RING = 4
FIRST_ATTENTION = 13
FIRST_DOUBLING = 14
LATE_SLOT = 17
LATE_EVERY = 5
REMAINDER = (
    (halve, 14, 2),
    (double, 6, 4),
    (double, 8, 3),
    (halve, 13, 4),
    (double, 7, 4),
    (double, 9, 3),
    (double, 13, 0),
    (halve, 15, 1),
    (double, 10, 2),
    (double, 11, 2),
    (halve, 14, 3),
    (double, 12, 1),
    (double, 8, 4),
    (double, 9, 4),
    (halve, 15, 2),
    (double, 10, 3),
    (double, 13, 1),
    (halve, 15, 3),
    (halve, 14, 4),
    (double, 11, 3),
    (double, 12, 2),
    (double, 14, 0),
    (double, 10, 4),
    (double, 13, 2),
    (halve, 15, 4),
    (double, 15, 0),
    (double, 11, 4),
    (double, 12, 3),
    (double, 13, 3),
    (double, 14, 1),
    (double, 15, 1),
    (double, 12, 4),
    (double, 13, 4),
    (double, 14, 2),
    (double, 15, 2),
    (double, 14, 3),
    (double, 15, 3),
    (double, 14, 4),
    (double, 15, 4),
)


def backward_kernel(
    tokens, context, low, mixed, hidden, slope_gate, slope_up, grad_second, unit_in, inv, norms, q_in, k_in, v_in,
    features, key_marks, cosines, sines, vec, wq, wo, wg, wu, wd,
    out, input_grad_out, vec_out,
    grads, halves, from_core, to_core, vectors, arena, total, unit, marks, key_aug, value_aug, probs_kept, scores_kept, turned_rows, dquery, dkey, dvalue,
    send_sems, recv_sems, core_send, core_recv, vec_send, vec_recv, load_sems, input_sems, extra_sems, wq_sems,
    feature_sems, unit_sems,
):
    rep = lax.axis_index("rep")
    core = lax.axis_index("fsdp")
    seq, width = total.shape
    shard = width // 2
    refs = (grads, halves, out, send_sems, recv_sems)

    def load(slot, source, target=None):
        return pltpu.make_async_copy(source, arena.at[slot] if target is None else target, load_sems.at[slot])

    def square(slot):
        return arena.at[slot, pl.ds(0, width), :]

    def sided(slot, source, first, second):
        return (
            pltpu.make_async_copy(
                source.at[:, aligned(first, shard, 128)], arena.at[slot, :, pl.ds(0, shard)], load_sems.at[slot]
            ),
            pltpu.make_async_copy(
                source.at[:, aligned(second, shard, 128)], arena.at[slot, :, pl.ds(shard, shard)], input_sems.at[slot]
            ),
        )

    def begin(loads):
        for one in loads if isinstance(loads, tuple) else (loads,):
            one.start()

    def finish(loads):
        for one in loads if isinstance(loads, tuple) else (loads,):
            one.wait()

    def core_copy(chunk):
        slot = lax.rem(chunk, RING)
        return pltpu.make_async_remote_copy(
            src_ref=to_core.at[lax.rem(chunk, 2)],
            dst_ref=from_core.at[slot],
            send_sem=core_send.at[slot],
            recv_sem=core_recv.at[slot],
            device_id=other_core(),
            device_id_type=MESH,
        )

    def emit(chunk, left, right):
        slot = lax.rem(chunk, 2)

        @pl.when(chunk >= 2)
        def _():
            core_copy(chunk - 2).wait_send()

        to_core[slot] = tn(arena[left, :, shard:], arena[right]).astype(BF16)
        core_copy(chunk).start()
        grads[chunk] = tn(arena[left, :, :shard], arena[right]).astype(BF16)

    def absorb(chunk):
        core_copy(chunk).wait_recv()
        slot = lax.rem(chunk, RING)
        grads[chunk] = (grads[chunk].astype(F32) + from_core[slot].astype(F32)).astype(BF16)

    def slot_work(slot, doubling):
        for stage in range(STEPS, -1, -1):
            if doubling:
                out_chunk = slot - FIRST_DOUBLING - 2 * stage

                @pl.when((out_chunk >= 0) & (out_chunk < fed + 1))
                def _():
                    double(refs, out_chunk, stage)

            chunk = slot - 1 - 3 * stage

            @pl.when((chunk >= 0) & (chunk < fed + 1))
            def _():
                halve(refs, chunk, stage)

            if doubling:
                late = slot - LATE_SLOT - 3 * stage

                @pl.when((late >= 0) & (lax.rem(late, LATE_EVERY) == 0))
                def _():
                    halve(refs, fed + 1 + lax.div(late, LATE_EVERY), stage)

    MIXED, LOW, SLOPE_GATE, SLOPE_UP, HIDDEN, GATE, UP, WD, WG, WU, SIDED_CONTEXT, WO, CONTEXT = range(13)
    ATTENDED, Q, K, V, GRAD_CONTEXT, PROJECTED, TOKENS, WQ = MIXED, SLOPE_GATE, SLOPE_UP, WD, HIDDEN, GATE, WG, WU
    blocks = wg.shape[1] // width
    fed = 3 * blocks

    def block_loads(j):
        cols = aligned(j * width, width)
        return {
            SLOPE_GATE: load(SLOPE_GATE, slope_gate.at[:, cols]),
            SLOPE_UP: load(SLOPE_UP, slope_up.at[:, cols]),
            WD: load(WD, wd.at[cols, :], square(WD)),
            WG: load(WG, wg.at[:, cols], square(WG)),
            WU: load(WU, wu.at[:, cols], square(WU)),
            HIDDEN: sided(
                HIDDEN,
                hidden,
                core * (wd.shape[0] // 2) + j * shard,
                (1 - core) * (wd.shape[0] // 2) + j * shard,
            ),
        }

    def wq_loads(turn_number):
        part = width // 3
        return tuple(
            pltpu.make_async_copy(
                wq.at[:, aligned(n * width + turn_number * part, part)],
                arena.at[WQ, pl.ds(0, width), pl.ds(n * part, part)],
                wq_sems.at[n],
            )
            for n in range(3)
        )

    def feature_load(pair):
        slot = lax.rem(pair, 2)
        return pltpu.make_async_copy(
            features.at[pl.ds(2 * pair, 2)], marks.at[slot], feature_sems.at[slot]
        )

    first_loads = block_loads(0)
    mixed_load = load(MIXED, mixed)
    low_load = sided(LOW, low, core * shard, (1 - core) * shard)
    second_load = pltpu.make_async_copy(grad_second, total, extra_sems.at[0])
    block = 256

    def unit_load(r):
        return pltpu.make_async_copy(unit_in.at[pl.ds(r * block, block)], unit.at[r % 2], unit_sems.at[r % 2])

    context_load = load(CONTEXT, context)
    sided_load = sided(SIDED_CONTEXT, context, core * shard, (1 - core) * shard)
    wo_load = load(WO, wo, square(WO))
    late_loads = {
        Q: load(Q, q_in),
        K: load(K, k_in),
        V: load(V, v_in),
        TOKENS: sided(TOKENS, tokens, core * shard, (1 - core) * shard),
    }
    for one in (mixed_load, first_loads[WD], first_loads[SLOPE_GATE], first_loads[SLOPE_UP], first_loads[HIDDEN],
                low_load, first_loads[WG], second_load, first_loads[WU], sided_load, wo_load, unit_load(0), unit_load(1), context_load,
                feature_load(0)):
        begin(one)
    vectors[0] = vec[...]
    greet()
    finish(mixed_load)

    tile = 512

    def feed_step(j, carry):
        loads = block_loads(j)
        upcoming = block_loads(j + 1)
        more = j + 1 < blocks

        def renew(*slots):
            @pl.when(more)
            def _():
                for slot in slots:
                    begin(upcoming[slot])

        def replace(*slots):
            @pl.when(jnp.logical_not(more))
            def _():
                for slot in slots:
                    begin(late_loads[slot])

        for slot in (WD, SLOPE_GATE, SLOPE_UP):
            finish(loads[slot])
        for r in range(seq // tile):
            rows = pl.ds(r * tile, tile)
            grad_hidden = nt(arena[MIXED, rows, :], arena[WD, :width, :])
            arena[GATE, rows, :] = (grad_hidden * arena[SLOPE_GATE, rows, :].astype(F32)).astype(BF16)
            arena[UP, rows, :] = (grad_hidden * arena[SLOPE_UP, rows, :].astype(F32)).astype(BF16)
        renew(WD, SLOPE_GATE, SLOPE_UP)
        replace(Q, K, V)
        finish(loads[HIDDEN])
        emit(3 * j, HIDDEN, MIXED)
        renew(HIDDEN)

        @pl.when(j > 0)
        def _():
            absorb(3 * j - 1)
            slot_work(3 * j, False)

        @pl.when(j == 0)
        def _():
            finish(low_load)
            finish(second_load)

        emit(3 * j + 1, LOW, GATE)
        finish(loads[WG])
        for r in range(seq // tile):
            rows = pl.ds(r * tile, tile)
            total[rows, :] += nt(arena[GATE, rows, :], arena[WG, :width, :])
        renew(WG)
        replace(TOKENS)
        absorb(3 * j)
        slot_work(3 * j + 1, False)
        emit(3 * j + 2, LOW, UP)
        finish(loads[WU])
        for r in range(seq // tile):
            rows = pl.ds(r * tile, tile)
            total[rows, :] += nt(arena[UP, rows, :], arena[WU, :width, :])
        renew(WU)
        absorb(3 * j + 1)
        slot_work(3 * j + 2, False)
        return carry

    lax.fori_loop(0, blocks, feed_step, 0)

    begin(wq_loads(0))
    gain_one = jnp.concatenate([norms[0, 0:1, :], norms[1, 0:1, :]], axis=1)
    bias_sum = jnp.zeros((1, width), F32)
    gain_sum = jnp.zeros((1, width), F32)
    for r in range(seq // block):
        rows = pl.ds(r * block, block)
        grad_normed = total[rows, :]
        unit_load(r).wait()
        unit_rows = unit[r % 2]
        bias_sum += jnp.sum(grad_normed, axis=0, keepdims=True)
        gain_sum += jnp.sum(grad_normed * unit_rows, axis=0, keepdims=True)
        scaled = grad_normed * gain_one
        grad_first = inv[rows, 0:1] * (scaled - row_mean(scaled) - unit_rows * row_mean(scaled * unit_rows))
        total[rows, :] = grad_first
        arena[ATTENDED, rows, :] = grad_first.astype(BF16)
        if r + 2 < seq // block:
            unit_load(r + 2).start()
    vectors[0, 0:1, :] = gain_sum
    vectors[0, 1:2, :] = bias_sum
    finish(sided_load)
    emit(fed, SIDED_CONTEXT, ATTENDED)
    finish(wo_load)
    absorb(fed - 1)
    slot_work(fed, False)
    for r in range(seq // tile):
        rows = pl.ds(r * tile, tile)
        arena[GRAD_CONTEXT, rows, :] = nt(arena[ATTENDED, rows, :], arena[WO, :width, :]).astype(BF16)
    absorb(fed)
    for one in (context_load, late_loads[Q], late_loads[K], late_loads[V], late_loads[TOKENS]):
        finish(one)

    ones = jnp.where((lanes() >= SPLIT_LANE) & (lanes() < SPLIT_LANE + 3), 1.0, 0.0)
    part = width // 3
    block_count = seq // block

    def head_step(turn_number, number, carry):
        pair = 2 * turn_number + lax.div(number, 2)
        head = lax.rem(number, 2)
        place = lax.div(number, 2) * 128
        cols = aligned(pair * 128, 128)
        mark_slot = lax.rem(pair, 2)
        own_lanes = lax.div(lanes(), HEAD_DIM) == head

        def only(values):
            return jnp.where(own_lanes, values, jnp.zeros_like(values))

        @pl.when(head == 0)
        def _():
            feature_load(pair).wait()

            @pl.when(pair + 1 < HEADS // 2)
            def _():
                feature_load(pair + 1).start()

            key_aug[:, :128] = arena[K, :, cols]
            key_aug[:, 128:] = (key_marks[...].astype(F32) + ones).astype(BF16)
            value_aug[:, :128] = arena[V, :, cols]
            value_aug[:, 128:] = jnp.broadcast_to(ones, (seq, 128)).astype(BF16)
            turned_rows[0] = jnp.transpose(arena[Q, :, cols])
            turned_rows[1] = jnp.transpose(arena[GRAD_CONTEXT, :, cols])

        def products_of(r):
            rows = pl.ds(r * block, block)
            query = jnp.concatenate([only(arena[Q, rows, cols]), marks[mark_slot, head, rows, :]], axis=1)
            grads_here = only(arena[GRAD_CONTEXT, rows, cols])
            delta = jnp.sum(grads_here.astype(F32) * arena[CONTEXT, rows, cols].astype(F32), axis=1, keepdims=True)
            tail = split_lanes(jnp.zeros((block, 128), F32), -delta)
            return nt(query, key_aug[...]), nt(jnp.concatenate([grads_here, tail], axis=1), value_aug[...])

        key_only = only(key_aug[:, :128])
        upcoming = products_of(0)
        for r in range(block_count):
            rows = pl.ds(r * block, block)
            scores, grad_probs = upcoming
            upcoming = products_of(r + 1) if r + 1 < block_count else None
            probs = jnp.exp(scores)
            grad_scores = (probs * grad_probs).astype(BF16)
            probs_kept[rows, :] = probs.astype(BF16)
            scores_kept[rows, :] = grad_scores
            dquery_term = nn(grad_scores, key_only)

            dquery[rows, :] = jnp.where(head == 0, 0.0, dquery[rows, :]) + dquery_term

        own_rows = aligned(head * HEAD_DIM, HEAD_DIM)
        dkey[own_rows, :] = nn(turned_rows[0, own_rows, :], scores_kept[...])
        dvalue[own_rows, :] = nn(turned_rows[1, own_rows, :], probs_kept[...])

        @pl.when(head == 1)
        def _():
            turned = turn(dquery[...] * (HEAD_DIM ** (-0.5)), cosines[...], -sines[...])
            arena[PROJECTED, :, aligned(place, 128)] = turned.astype(BF16)
            turned = turn(jnp.transpose(dkey[...]), cosines[...], -sines[...])
            arena[PROJECTED, :, aligned(part + place, 128)] = turned.astype(BF16)
            arena[PROJECTED, :, aligned(2 * part + place, 128)] = jnp.transpose(dvalue[...]).astype(BF16)

        slot_work(FIRST_ATTENTION + LATE_EVERY * turn_number + number, True)
        for stage in range(VECTOR_STEPS + 1):

            @pl.when(4 * turn_number + number == stage)
            def _():
                vector_stage(vectors, vec_send, vec_recv, stage)

        return carry

    def turn_step(turn_number, carry):
        lax.fori_loop(0, 4, functools.partial(head_step, turn_number), 0)
        chunk = fed + 1 + turn_number
        emit(chunk, TOKENS, PROJECTED)
        finish(wq_loads(turn_number))
        for r in range(seq // tile):
            rows = pl.ds(r * tile, tile)
            total[rows, :] += nt(arena[PROJECTED, rows, :], arena[WQ, :width, :])

        @pl.when(turn_number < 2)
        def _():
            begin(wq_loads(turn_number + 1))

        absorb(chunk)
        slot_work(LATE_SLOT + LATE_EVERY * turn_number, True)
        return carry

    lax.fori_loop(0, 3, turn_step, 0)

    half = seq // 2
    mine = pltpu.make_async_copy(total.at[aligned(core * half, half)], input_grad_out.at[core], extra_sems.at[2])
    theirs = pltpu.make_async_remote_copy(
        src_ref=total.at[aligned((1 - core) * half, half)],
        dst_ref=input_grad_out.at[core],
        send_sem=core_send.at[RING],
        recv_sem=core_recv.at[RING],
        device_id=other_core(),
        device_id_type=MESH,
    )
    mine.start()
    theirs.start()
    vec_out[...] = vectors[2 * VECTOR_STEPS]
    for work, chunk, stage in REMAINDER:
        work(refs, chunk, stage)
    mine.wait()
    theirs.wait()
    for number in range(2):
        core_copy(CHUNKS - 2 + number).wait_send()


def backward(tokens, saved, norms, key_marks, cosines, sines, vec, weights, outs):
    context, low, mixed, hidden, slope_gate, slope_up, grad_second, unit, inv, q, k, v, features = saved
    seq, width = tokens.shape
    dma = pltpu.SemaphoreType.DMA
    vmem = pl.BlockSpec(memory_space=pltpu.VMEM)
    hbm = pl.BlockSpec(memory_space=pl.ANY)
    chunks = (CHUNKS, width // 2, width)
    return pl.pallas_call(
        backward_kernel,
        out_shape=(
            jax.ShapeDtypeStruct(chunks, BF16),
            jax.ShapeDtypeStruct(outs, F32),
            jax.ShapeDtypeStruct(vec.shape, F32),
        ),
        in_specs=[hbm] * 9 + [vmem] * 2 + [hbm] * 4 + [vmem] * 4 + [hbm] * 5,
        out_specs=(hbm, hbm, vmem),
        scratch_shapes=[
            pltpu.VMEM(chunks, BF16),
            pltpu.VMEM((HALVES_RING,) + chunks[1:], BF16),
            pltpu.VMEM((RING,) + chunks[1:], BF16),
            pltpu.VMEM((2,) + chunks[1:], BF16),
            pltpu.VMEM((2 * VECTOR_STEPS + 1,) + vec.shape, F32),
            pltpu.VMEM((13, seq, width), BF16),
            pltpu.VMEM((seq, width), F32),
            pltpu.VMEM((2, 256, width), F32),
            pltpu.VMEM((2, 2, seq, FEATURES), BF16),
            pltpu.VMEM((seq, 256), BF16),
            pltpu.VMEM((seq, 256), BF16),
            pltpu.VMEM((seq, seq), BF16),
            pltpu.VMEM((seq, seq), BF16),
            pltpu.VMEM((2, 128, seq), BF16),
            pltpu.VMEM((seq, 128), F32),
            pltpu.VMEM((128, seq), F32),
            pltpu.VMEM((128, seq), F32),
            dma((HALVES_RING, 2 * STEPS + 1)),
            dma((HALVES_RING, 2 * STEPS)),
            dma((RING + 1,)),
            dma((RING + 1,)),
            dma((VECTOR_STEPS,)),
            dma((VECTOR_STEPS,)),
            dma((13,)),
            dma((13,)),
            dma((3,)),
            dma((3,)),
            dma((2,)),
            dma((2,)),
        ],
        compiler_params=pltpu.CompilerParams(collective_id=0, has_side_effects=True, vmem_limit_bytes=63 << 20),
    )(tokens, context, low, mixed, hidden, slope_gate, slope_up, grad_second, unit, inv, norms, q, k, v,
      features, key_marks, cosines, sines, vec, *weights)


def finish_kernel(
    summed, vec, activations, input_grad,
    activations_out, input_grad_out, qkv, out, gate, up, down, gain_one, bias_one, gain_two, bias_two,
    narrow, wide, acts, inputs, in_sems, out_sems, pass_sems,
):
    rows, width = narrow.shape[1:]
    part = width // 3
    fed = CHUNKS - 4
    held = ((activations, acts, activations_out), (input_grad, inputs, input_grad_out))
    fetches = [pltpu.make_async_copy(source, place, pass_sems.at[n]) for n, (source, place, _) in enumerate(held)]
    passes = [pltpu.make_async_copy(place, target, pass_sems.at[n]) for n, (_, place, target) in enumerate(held)]
    loads = [pltpu.make_async_copy(summed.at[n], narrow.at[n], in_sems.at[n]) for n in range(CHUNKS)]
    for load in loads + fetches:
        load.start()
    core = lax.axis_index("fsdp")
    for n, ref in enumerate((gain_one, bias_one, gain_two, bias_two)):
        ref[...] = vec[n, aligned(core * rows, rows, 128)]
    stores = []
    for n in range(CHUNKS):
        loads[n].wait()
        wide[n] = narrow[n].astype(F32)
        turn_number = n // 3
        block = pl.ds(width * turn_number, width)
        if n < fed:
            target = (down.at[pl.ds(rows * turn_number, rows)], gate.at[:, block], up.at[:, block])[n % 3]
            parts = [(wide.at[n], target)]
        elif n == fed:
            parts = [(wide.at[n], out)]
        else:
            parts = [
                (wide.at[n, :, pl.ds(m * part, part)], qkv.at[:, pl.ds(m * width + (n - fed - 1) * part, part)])
                for m in range(3)
            ]
        for source, target in parts:
            stores.append(pltpu.make_async_copy(source, target, out_sems.at[len(stores)]))
            stores[-1].start()
    for fetch, store in zip(fetches, passes):
        fetch.wait()
        store.start()
    for store in stores + passes:
        store.wait()


def finish(summed, vec, activations, input_grad):
    rows, cols = summed.shape[1:]
    vmem = pl.BlockSpec(memory_space=pltpu.VMEM)
    hbm = pl.BlockSpec(memory_space=pl.ANY)

    def shape(high, across):
        return jax.ShapeDtypeStruct((rows * high, cols * across), F32)

    def like(array):
        return jax.ShapeDtypeStruct(array.shape, array.dtype)

    return pl.pallas_call(
        finish_kernel,
        out_shape=(like(activations), like(input_grad), shape(1, 3), shape(1, 1), shape(1, 4), shape(1, 4), shape(4, 1))
        + (jax.ShapeDtypeStruct((rows,), F32),) * 4,
        in_specs=[hbm, vmem, hbm, hbm],
        out_specs=(hbm,) * 7 + (vmem,) * 4,
        scratch_shapes=[
            pltpu.VMEM(summed.shape, BF16),
            pltpu.VMEM(summed.shape, F32),
            pltpu.VMEM(activations.shape, activations.dtype),
            pltpu.VMEM(input_grad.shape, input_grad.dtype),
            pltpu.SemaphoreType.DMA((CHUNKS,)),
            pltpu.SemaphoreType.DMA((CHUNKS + 6,)),
            pltpu.SemaphoreType.DMA((2,)),
        ],
        compiler_params=pltpu.CompilerParams(vmem_limit_bytes=62 << 20),
    )(summed, vec, activations, input_grad)


def shards(
    tokens,
    lengths,
    w_qkv,
    w_out,
    w_gate,
    w_up,
    w_down,
    norm1_gain,
    norm1_bias,
    norm2_gain,
    norm2_bias,
    cotangent,
):
    zero = jnp.zeros_like(norm1_gain)
    norms = jnp.stack([norm1_gain, norm1_bias, norm2_gain, norm2_bias, zero, zero, zero, zero]).astype(F32)
    weights = (w_qkv, w_out, w_gate, w_up, w_down)
    (q, k, v, context, features, low, unit, inv, slope_gate, slope_up, hidden, grad_second, mixed, activations,
     vec, norms, key_marks, cosines, sines, stream, *weights) = forward(tokens, cotangent, weights, norms, lengths)
    saved = (context, low, mixed, hidden, slope_gate, slope_up, grad_second, unit, inv, q, k, v, features)
    summed, input_grad, vec_sum = backward(
        stream, saved, norms, key_marks, cosines, sines, vec, weights, tokens.shape
    )
    groups = lax.axis_size("rep") // UNITS
    if groups > 1:
        alike = [[UNITS * g + n for g in range(groups)] for n in range(UNITS)]
        summed = lax.psum(summed, "rep", axis_index_groups=alike)
        vec_sum = lax.psum(vec_sum, "rep", axis_index_groups=alike)
    return finish(summed, vec_sum, activations, input_grad)


def solution(mesh):
    placed = (
        P("rep", "fsdp", None),
        P("rep", None),
        P("fsdp", None),
        P("fsdp", None),
        P("fsdp", None),
        P("fsdp", None),
        P("fsdp", None),
        P("fsdp"),
        P("fsdp"),
        P("fsdp"),
        P("fsdp"),
        P("rep", "fsdp", None),
    )
    return jax.shard_map(
        shards,
        mesh=mesh,
        in_specs=placed,
        out_specs=(
            P("rep", "fsdp", None),
            P("rep", "fsdp", None),
            P("fsdp", None),
            P("fsdp", None),
            P("fsdp", None),
            P("fsdp", None),
            P("fsdp", None),
            P("fsdp"),
            P("fsdp"),
            P("fsdp"),
            P("fsdp"),
        ),
        check_vma=False,
    )
```

```python
import functools

import jax
import jax.numpy as jnp
import numpy as np
from jax import lax
from jax.experimental import pallas as pl
from jax.experimental.pallas import tpu as pltpu
from jax.sharding import PartitionSpec as P

HEADS = 12
HEAD_DIM = 64


EPSILON = 1e-05


CHUNKS = 16
PARTS = 3
PART_ROWS = 128
UNITS = 16
STEPS = 4
HALVES_RING = 8
MESH = pl.DeviceIdType.MESH
BF16 = jnp.bfloat16
F32 = jnp.float32


def bit_of(value, weight):
    return lax.rem(lax.div(value, weight), 2)


def orders(chunk):
    rep = lax.axis_index("rep")
    odd = lax.rem(jnp.asarray(chunk, jnp.int32), 2)
    first, second = 1 + odd, 2 - odd
    bits = {1: bit_of(rep, 1), 2: bit_of(rep, 2), 4: bit_of(rep, 4), 8: bit_of(rep, 8)}
    first_bit = bits[1] * (1 - odd) + bits[2] * odd
    second_bit = bits[2] * (1 - odd) + bits[1] * odd
    return (
        ((1, bits[1]), (2, bits[2]), (4, bits[4]), (8, bits[8])),
        ((2, bits[2]), (1, bits[1]), (4, bits[4]), (8, bits[8])),
        ((4, bits[4]), (first, first_bit), (second, second_bit), (8, bits[8])),
    )


def partner_of(weight, bit):
    return (lax.axis_index("rep") + weight * (1 - 2 * bit), lax.axis_index("fsdp"))


def other_core():
    return (lax.axis_index("rep"), 1 - lax.axis_index("fsdp"))


def region(ref, chunk, part, order, level, flip):
    rows = PART_ROWS >> min(level, STEPS - 1)
    start = part * PART_ROWS
    for step in range(level):
        bit = order[step][1]
        if flip and step == level - 1:
            bit = 1 - bit
        if step < STEPS - 1:
            start = start + bit * (PART_ROWS >> (step + 1))
        else:
            column = bit * (ref.shape[2] // 2)
    start = pl.multiple_of(start, 16)
    if level < STEPS:
        return (chunk, pl.ds(start, rows), slice(None))
    half = ref.shape[2] // 2
    return (chunk, pl.ds(start, rows), pl.ds(pl.multiple_of(column, 128), half))


def ring_slot(chunk):
    return lax.rem(jnp.asarray(chunk, jnp.int32), HALVES_RING)


def landing(ref, chunk, part, step):
    start = part * PART_ROWS + PART_ROWS - (PART_ROWS >> step)
    chunk = ring_slot(chunk)
    if step < STEPS - 1:
        return (chunk, pl.ds(start, PART_ROWS >> (step + 1)), slice(None))
    return (chunk, pl.ds(start, PART_ROWS >> step), pl.ds(0, ref.shape[2] // 2))


def halving_copy(refs, chunk, part, order, step):
    grads, halves, _, send_sems, recv_sems = refs
    slot = ring_slot(chunk)
    return pltpu.make_async_remote_copy(
        src_ref=grads.at[region(grads, chunk, part, order, step + 1, True)],
        dst_ref=halves.at[landing(halves, chunk, part, step)],
        send_sem=send_sems.at[slot, step],
        recv_sem=recv_sems.at[slot, step],
        device_id=partner_of(*order[step]),
        device_id_type=MESH,
    )


def all_parts(ref, first, step):
    rows = PARTS * (PART_ROWS >> min(step + 1, STEPS - 1))
    columns = ref.shape[2] if step < STEPS - 1 else ref.shape[2] // 2
    return ref.at[first, pl.ds(0, rows), pl.ds(0, columns)]


def wait_parts(ref, first, step, send_sem, recv_sem):
    whole = all_parts(ref, first, step)
    pltpu.make_async_remote_copy(
        src_ref=whole,
        dst_ref=whole,
        send_sem=send_sem,
        recv_sem=recv_sem,
        device_id=other_core(),
        device_id_type=MESH,
    ).wait()


def halving_add(refs, chunk, part, order, step):
    grads, halves = refs[:2]
    kept = region(grads, chunk, part, order, step + 1, False)
    theirs = halves[landing(halves, chunk, part, step)]
    grads[kept] = (grads[kept].astype(F32) + theirs.astype(F32)).astype(BF16)


def settle_copy(refs, chunk, part, order):
    grads, _, out, send_sems, _ = refs
    mine = region(grads, chunk, part, order, STEPS, False)
    return pltpu.make_async_copy(grads.at[mine], out.at[mine], send_sems.at[ring_slot(chunk), 2 * STEPS])


def doubling_copy(refs, chunk, part, order, step):
    grads, _, out, send_sems, recv_sems = refs
    slot = ring_slot(chunk)
    mine = region(out, chunk, part, order, step + 1, False)
    return pltpu.make_async_remote_copy(
        src_ref=(grads if step == STEPS - 1 else out).at[mine],
        dst_ref=out.at[mine],
        send_sem=send_sems.at[slot, STEPS + step],
        recv_sem=recv_sems.at[slot, STEPS + step],
        device_id=partner_of(*order[step]),
        device_id_type=MESH,
    )


def halve(refs, chunk, stage):
    _, halves, _, send_sems, recv_sems = refs
    slot = ring_slot(chunk)
    if stage > 0:
        wait_parts(halves, slot, stage - 1, send_sems.at[slot, stage - 1], recv_sems.at[slot, stage - 1])
    for part, order in enumerate(orders(chunk)):
        if stage > 0:
            halving_add(refs, chunk, part, order, stage - 1)
        if stage < STEPS:
            halving_copy(refs, chunk, part, order, stage).start()
        else:
            settle_copy(refs, chunk, part, order).start()


def double(refs, chunk, stage):
    grads, _, out, send_sems, recv_sems = refs
    slot = ring_slot(chunk)
    if stage > 0:
        sems = send_sems.at[slot, 2 * STEPS - stage], recv_sems.at[slot, 2 * STEPS - stage]
        wait_parts(out, chunk, STEPS - stage, *sems)
    if stage == 1:
        sizes = [all_parts(ref, chunk, STEPS - 1) for ref in (grads, out)]
        pltpu.make_async_copy(*sizes, send_sems.at[slot, 2 * STEPS]).wait()
    if stage < STEPS:
        for part, order in enumerate(orders(chunk)):
            doubling_copy(refs, chunk, part, order, STEPS - 1 - stage).start()


def greet():
    rep = lax.axis_index("rep")
    barrier = pltpu.get_barrier_semaphore()
    pl.semaphore_signal(barrier, inc=1, device_id=other_core(), device_id_type=MESH)
    for weight in (1, 2, 4, 8):
        there = partner_of(weight, bit_of(rep, weight))
        pl.semaphore_signal(barrier, inc=1, device_id=there, device_id_type=MESH)
    pl.semaphore_wait(barrier, 5)


def vector_copy(vectors, send_sems, recv_sems, step):
    rep = lax.axis_index("rep")
    if step == 0:
        there = other_core()
    else:
        weight = 1 << (step - 1)
        there = partner_of(weight, bit_of(rep, weight))
    return pltpu.make_async_remote_copy(
        src_ref=vectors.at[2 * step],
        dst_ref=vectors.at[2 * step + 1],
        send_sem=send_sems.at[step],
        recv_sem=recv_sems.at[step],
        device_id=there,
        device_id_type=MESH,
    )


VECTOR_STEPS = 5


def vector_stage(vectors, send_sems, recv_sems, stage):
    if stage > 0:
        vector_copy(vectors, send_sems, recv_sems, stage - 1).wait()
        vectors[2 * stage] = vectors[2 * stage - 2] + vectors[2 * stage - 1]
    if stage < VECTOR_STEPS:
        vector_copy(vectors, send_sems, recv_sems, stage).start()


SEQ_ROWS = 512
NEG = -1e30
FEATURES = 128
SPLIT_LANE = 8


def nn(left, right):
    return jnp.dot(left, right, preferred_element_type=F32)


def nt(left, right):
    return lax.dot_general(left, right, (((1,), (1,)), ((), ())), preferred_element_type=F32)


def tn(left, right):
    return lax.dot_general(left, right, (((0,), (0,)), ((), ())), preferred_element_type=F32)


def aligned(start, size, multiple=None):
    return pl.ds(pl.multiple_of(start, multiple or size), size)


def lanes():
    return lax.broadcasted_iota(jnp.int32, (1, 128), 1)


def head_mask(values, first):
    low = lanes() < HEAD_DIM
    zero = jnp.zeros_like(values)
    return jnp.where(low, values, zero) if first else jnp.where(low, zero, values)


def turn(values, cosines, sines):
    first = lax.rem(lanes(), HEAD_DIM) < HEAD_DIM // 2
    swapped = jnp.where(first, pltpu.roll(values, 96, 1), pltpu.roll(values, 32, 1))
    return values * cosines + swapped * sines


def split_lanes(base, values):
    high = values.astype(BF16).astype(F32)
    middle = (values - high).astype(BF16).astype(F32)
    low = values - high - middle
    lane = lanes()
    out = jnp.where(lane == SPLIT_LANE, high, base)
    out = jnp.where(lane == SPLIT_LANE + 1, middle, out)
    return jnp.where(lane == SPLIT_LANE + 2, low, out).astype(BF16)


def row_mean(values):
    return jnp.mean(values, axis=1, keepdims=True)


def forward_kernel(
    tokens, cotangent, w_qkv, w_out, w_gate, w_up, w_down, norm_one, norm_two, norm_three, norm_four, lengths,
    frequencies,
    q_out, k_out, v_out, context_out, features_out, low_out, unit_out, inv_out, slope_gate_out, slope_up_out,
    hidden_out, grad_second_out, mixed_out, activations_out, vec_out,
    norms_out, key_marks, cosines, sines, x_out, wq_out, wo_out, wg_out, wu_out, wd_out,
    x, g, wq, wo, wg, wu, wd, nv, qs, ks, vs, ctx, total, key_aug, value_aug, pieces, seconds,
    norms, query_marks, marks, products, send_sems, recv_sems, own_sems, save_sems, act_sems, mark_sems,
):
    rep = lax.axis_index("rep")
    core = lax.axis_index("fsdp")
    there = (rep, 1 - core)
    seq, width = x.shape
    half = seq // 2

    barrier = pltpu.get_barrier_semaphore()
    pl.semaphore_signal(barrier, inc=1, device_id=there, device_id_type=MESH)
    pl.semaphore_wait(barrier, 1)

    norms[...] = jnp.zeros_like(norms)
    for n, ref in enumerate((norm_one, norm_two, norm_three, norm_four)):
        norms[n, :] = ref[...].astype(F32)

    def rows_of(ref, block):
        return ref.at[aligned(core * block, block)]

    exchanges = (
        (tokens.at[core], tokens.at[1 - core], rows_of(x, half)),
        (w_qkv, w_qkv, rows_of(wq, w_qkv.shape[0])),
        (w_out, w_out, rows_of(wo, w_out.shape[0])),
        (norms, norms, nv.at[core]),
        (w_gate, w_gate, rows_of(wg, w_gate.shape[0])),
        (w_up, w_up, rows_of(wu, w_up.shape[0])),
        (w_down, w_down, rows_of(wd, w_down.shape[0])),
        (cotangent.at[core], cotangent.at[1 - core], rows_of(g, half)),
    )

    def copies(number):
        mine, theirs, place = exchanges[number]
        return (
            pltpu.make_async_copy(mine, place, own_sems.at[number]),
            pltpu.make_async_remote_copy(
                src_ref=theirs,
                dst_ref=place,
                send_sem=send_sems.at[number],
                recv_sem=recv_sems.at[number],
                device_id=there,
                device_id_type=MESH,
            ),
        )

    for number in range(len(exchanges)):
        for copy in copies(number):
            copy.start()

    def arrived(number):
        for copy in copies(number):
            copy.wait()

    def save(source, target, number):
        copy = pltpu.make_async_copy(source, target, save_sems.at[number])
        copy.start()
        return copy

    places = lax.broadcasted_iota(jnp.int32, (seq, 128), 0)
    segment = jnp.zeros_like(places)
    begins = jnp.zeros_like(places)
    doc_end = jnp.int32(0)
    for doc in range(lengths.shape[1]):
        doc_end = doc_end + lengths[core, doc]
        past = places >= doc_end
        segment = segment + past.astype(jnp.int32)
        begins = jnp.where(past, doc_end, begins)
    same = segment == lanes()
    query_marks[...] = jnp.where(same, 1.0, 0.0).astype(BF16)
    key_marks[...] = jnp.where(same | (lanes() >= SPLIT_LANE), 0.0, NEG).astype(BF16)
    angles = (places - begins).astype(F32) * frequencies[0:1, :]
    cosines[...] = jnp.cos(angles)
    side = jnp.where(lax.rem(lanes(), HEAD_DIM) < HEAD_DIM // 2, -1.0, 1.0)
    sines[...] = jnp.sin(angles) * side

    arrived(0)
    arrived(1)
    tile = 512
    for n, out in enumerate((qs, ks, vs)):
        for r in range(seq // tile):
            rows = pl.ds(r * tile, tile)
            product_rows = nn(x[rows, :], wq[:, pl.ds(n * width, width)])
            if n == 2:
                out[rows, :] = product_rows.astype(BF16)
                continue
            for pair in range(width // 128):
                cols = slice(pair * 128, pair * 128 + 128)
                turned = turn(product_rows[:, cols], cosines[rows, :], sines[rows, :]).astype(BF16)
                if n == 0:
                    turned = turned * jnp.asarray(HEAD_DIM ** (-0.5), BF16)
                out[rows, cols] = turned
    saves = {12: save(x, x_out, 12), 0: save(qs, q_out, 0), 1: save(ks, k_out, 1), 2: save(vs, v_out, 2)}

    saves[7] = save(wq, wq_out, 7)

    block = 256
    steps = [(a, r) for r in range(seq // block) for a in range(2)]

    def mark_copy(pair):
        slot = lax.rem(pair, 2)
        return pltpu.make_async_copy(marks.at[slot], features_out.at[pl.ds(2 * pair, 2)], mark_sems.at[slot])

    weight_saves = [
        pltpu.make_async_copy(source, target, save_sems.at[8 + number])
        for number, (source, target) in enumerate(((wo, wo_out), (wg, wg_out), (wu, wu_out), (wd, wd_out)))
    ]

    def pair_step(pair, carry):
        for number, turn_number in enumerate((1, 2, 3, 4)):

            @pl.when(pair == turn_number)
            def _():
                arrived((2, 4, 5, 6)[number])
                weight_saves[number].start()

        cols = aligned(pair * 128, 128)
        mark_slot = lax.rem(pair, 2)

        @pl.when(pair >= 2)
        def _():
            mark_copy(pair - 2).wait()

        key_aug[:, :128] = ks[:, cols]
        key_aug[:, 128:] = key_marks[...]
        for a in range(2):
            value_aug[a, :, :128] = head_mask(vs[:, cols], a == 0)
            value_aug[a, :, 128:] = jnp.ones((seq, 128), BF16)

        def scores_of(a, r):
            rows = pl.ds(r * block, block)
            query = jnp.concatenate([head_mask(qs[rows, cols], a == 0), query_marks[rows, :]], axis=1)
            return nt(query, key_aug[...])

        scores = scores_of(*steps[0])
        parts = [None, None]
        for number, (a, r) in enumerate(steps):
            rows = pl.ds(r * block, block)
            upcoming = scores_of(*steps[number + 1]) if number + 1 < len(steps) else None
            row_max = jnp.max(scores, axis=1, keepdims=True)
            probs = jnp.exp(scores - row_max).astype(BF16)
            summed = nn(probs, value_aug[a])
            row_total = summed[:, 128:]
            parts[a] = summed[:, :128] / row_total
            lse = row_max + jnp.log(row_total)
            marks[mark_slot, a, rows, :] = split_lanes(query_marks[rows, :].astype(F32), -lse)
            if a == 1:
                ctx[rows, cols] = (parts[0] + parts[1]).astype(BF16)
            scores = upcoming
        mark_copy(pair).start()
        return carry

    lax.fori_loop(0, HEADS // 2, pair_step, 0)
    saves[3] = save(ctx, context_out, 3)

    low = qs
    saves[0].wait()
    arrived(3)

    def vector(n):
        return jnp.concatenate([nv[0, n : n + 1, :], nv[1, n : n + 1, :]], axis=1)

    for r in range(seq // block):
        rows = pl.ds(r * block, block)
        first_sum = x[rows, :].astype(F32) + nn(ctx[rows, :], wo[...])
        centre = first_sum - row_mean(first_sum)
        inv = lax.rsqrt(row_mean(centre * centre) + EPSILON)
        unit = centre * inv
        normed = unit * vector(0) + vector(1)
        seconds[rows, :] = unit
        inv_out[rows, :] = jnp.broadcast_to(inv, (block, 128))
        total[rows, :] = normed
        low[rows, :] = normed.astype(BF16)
    saves[4] = save(seconds, unit_out, 4)
    saves[5] = save(low, low_out, 5)

    slots, _, tile, columns = pieces.shape
    row_tiles = seq // tile
    count = row_tiles * (wg.shape[1] // columns)
    outs = (slope_gate_out, slope_up_out, hidden_out)

    def piece_copy(number, n):
        slot = lax.rem(number, slots)
        rows = aligned(lax.rem(number, row_tiles) * tile, tile)
        cols = aligned(lax.div(number, row_tiles) * columns, columns)
        return pltpu.make_async_copy(pieces.at[slot, n], outs[n].at[rows, cols], act_sems.at[slot, n])

    def multiply(number, slot):
        rows = aligned(lax.rem(number, row_tiles) * tile, tile)
        cols = aligned(lax.div(number, row_tiles) * columns, columns)
        products[slot, 0] = nn(low[rows, :], wg[:, cols])
        products[slot, 1] = nn(low[rows, :], wu[:, cols])

    def take(number, slot):
        rows = aligned(lax.rem(number, row_tiles) * tile, tile)
        cols = aligned(lax.div(number, row_tiles) * columns, columns)
        gate = products[slot, 0]
        up = products[slot, 1]
        gate_sig = 0.5 + 0.5 * jnp.tanh(0.5 * gate)
        gate_silu = gate * gate_sig
        place = lax.rem(number, slots)
        pieces[place, 0] = (up * (gate_sig + gate_silu * (1.0 - gate_sig))).astype(BF16)
        pieces[place, 1] = gate_silu.astype(BF16)
        hidden = (gate_silu * up).astype(BF16)
        pieces[place, 2] = hidden
        total[rows, :] += nn(hidden, wd[cols, :])

    def feed_step(turn_number, carry):
        number = 2 * turn_number

        @pl.when(number >= slots)
        def _():
            for n in range(3):
                piece_copy(number - slots, n).wait()
                piece_copy(number - slots + 1, n).wait()

        multiply(number + 1, 1)
        take(number, 0)
        multiply(jnp.minimum(number + 2, count - 1), 0)
        take(number + 1, 1)
        for n in range(3):
            piece_copy(number, n).start()
            piece_copy(number + 1, n).start()
        return carry

    multiply(jnp.int32(0), 0)
    lax.fori_loop(0, count // 2, feed_step, 0)

    acts = ctx
    saves[3].wait()
    arrived(7)
    saves[2].wait()
    saves[4].wait()
    gain_two, bias_two = vector(2), vector(3)
    bias_sum = jnp.zeros((1, width), F32)
    gain_sum = jnp.zeros((1, width), F32)
    for r in range(seq // block):
        rows = pl.ds(r * block, block)
        second_sum = total[rows, :]
        centre = second_sum - row_mean(second_sum)
        inv = lax.rsqrt(row_mean(centre * centre) + EPSILON)
        unit = centre * inv
        acts[rows, :] = (unit * gain_two + bias_two).astype(BF16)
        grad_out = g[rows, :].astype(F32)
        bias_sum += jnp.sum(grad_out, axis=0, keepdims=True)
        gain_sum += jnp.sum(grad_out * unit, axis=0, keepdims=True)
        scaled = grad_out * gain_two
        grad_second = inv * (scaled - row_mean(scaled) - unit * row_mean(scaled * unit))
        seconds[rows, :] = grad_second
        vs[rows, :] = grad_second.astype(BF16)
    norms_out[...] = nv[...]
    vec_out[...] = jnp.zeros_like(vec_out)
    vec_out[2:3, :] = gain_sum
    vec_out[3:4, :] = bias_sum
    del saves[0], saves[3]
    saves[4] = save(seconds, grad_second_out, 4)
    saves[2] = save(vs, mixed_out, 2)

    mine = pltpu.make_async_copy(rows_of(acts, half), activations_out.at[core], save_sems.at[6])
    mine.start()
    theirs = pltpu.make_async_remote_copy(
        src_ref=acts.at[aligned((1 - core) * half, half)],
        dst_ref=activations_out.at[core],
        send_sem=send_sems.at[len(exchanges)],
        recv_sem=recv_sems.at[len(exchanges)],
        device_id=there,
        device_id_type=MESH,
    )
    theirs.start()
    for copy in list(saves.values()) + weight_saves:
        copy.wait()
    for pair in range(HEADS // 2 - 2, HEADS // 2):
        mark_copy(pair).wait()
    for number in range(slots):
        for n in range(3):
            piece_copy(jnp.int32(count - slots + number), n).wait()
    mine.wait()
    theirs.wait()


def forward(tokens, cotangent, weights, norms, lengths):
    w_qkv, w_out, w_gate, w_up, w_down = weights
    seq, width = 2 * tokens.shape[1], tokens.shape[2]
    hidden_width = w_gate.shape[1]
    dma = pltpu.SemaphoreType.DMA
    vmem = pl.BlockSpec(memory_space=pltpu.VMEM)
    hbm = pl.BlockSpec(memory_space=pl.ANY)

    def shape(*dims, dtype=BF16):
        return jax.ShapeDtypeStruct(dims, dtype)

    lane = np.arange(128) % (HEAD_DIM // 2)
    frequencies = np.broadcast_to(1000.0 ** (-2.0 * lane / HEAD_DIM), (8, 128)).astype(np.float32)

    def full(shard):
        return pltpu.VMEM((2 * shard.shape[0], shard.shape[1]), BF16)

    rows = shape(seq, width)
    wide = shape(seq, hidden_width)
    return pl.pallas_call(
        forward_kernel,
        out_shape=(
            rows, rows, rows, rows, shape(HEADS, seq, FEATURES), rows, shape(seq, width, dtype=F32),
            shape(seq, 128, dtype=F32), wide, wide, wide, shape(seq, width, dtype=F32), rows,
            shape(*tokens.shape), shape(8, width, dtype=F32), shape(2, 8, *norms[0].shape, dtype=F32),
            shape(seq, FEATURES), shape(seq, 128, dtype=F32), shape(seq, 128, dtype=F32), rows,
        )
        + tuple(shape(2 * shard.shape[0], shard.shape[1]) for shard in weights),
        in_specs=[hbm] * 7 + [vmem] * 4 + [pl.BlockSpec(memory_space=pltpu.SMEM), vmem],
        out_specs=(hbm, hbm, hbm, hbm, hbm, hbm, hbm, vmem, hbm, hbm, hbm, hbm, hbm, hbm, vmem, vmem)
        + (vmem,) * 3
        + (hbm,) * 6,
        scratch_shapes=[
            pltpu.VMEM((seq, width), BF16),
            pltpu.VMEM((seq, width), BF16),
            full(w_qkv), full(w_out), full(w_gate), full(w_up), full(w_down),
            pltpu.VMEM((2, 8) + norms[0].shape, F32),
            pltpu.VMEM((seq, width), BF16),
            pltpu.VMEM((seq, width), BF16),
            pltpu.VMEM((seq, width), BF16),
            pltpu.VMEM((seq, width), BF16),
            pltpu.VMEM((seq, width), F32),
            pltpu.VMEM((seq, 256), BF16),
            pltpu.VMEM((2, seq, 256), BF16),
            pltpu.VMEM((4, 3, 256, 768), BF16),
            pltpu.VMEM((seq, width), F32),
            pltpu.VMEM((8,) + norms[0].shape, F32),
            pltpu.VMEM((seq, FEATURES), BF16),
            pltpu.VMEM((2, 2, seq, FEATURES), BF16),
            pltpu.VMEM((2, 2, 256, 768), F32),
            dma((9,)), dma((9,)), dma((8,)), dma((13,)), dma((4, 3)), dma((2,)),
        ],
        compiler_params=pltpu.CompilerParams(collective_id=1, has_side_effects=True, vmem_limit_bytes=63 << 20),
    )(tokens, cotangent, w_qkv, w_out, w_gate, w_up, w_down, *norms, lengths, jnp.asarray(frequencies))


RING = 4
FIRST_ATTENTION = 13
FIRST_DOUBLING = 13
LATE_SLOT = 17
LATE_EVERY = 5
HALVING_LAGS = (0, 3, 5, 8, 11)
LATE_LAGS = (0, 3, 5, 7, 10)
DOUBLING_LAGS = (0, 3, 5, 8, 10)
REMAINDER = (
    (double, 13, 0),
    (double, 4, 4),
    (double, 5, 4),
    (double, 6, 3),
    (halve, 14, 3),
    (double, 7, 3),
    (halve, 15, 1),
    (double, 8, 2),
    (double, 9, 2),
    (double, 13, 1),
    (double, 6, 4),
    (double, 10, 1),
    (double, 11, 1),
    (double, 12, 0),
    (halve, 14, 4),
    (halve, 15, 2),
    (double, 14, 0),
    (double, 7, 4),
    (double, 8, 3),
    (double, 13, 2),
    (double, 9, 3),
    (halve, 15, 3),
    (double, 10, 2),
    (double, 11, 2),
    (double, 13, 3),
    (double, 14, 1),
    (double, 8, 4),
    (double, 9, 4),
    (double, 10, 3),
    (halve, 15, 4),
    (double, 15, 0),
    (double, 11, 3),
    (double, 13, 4),
    (double, 12, 1),
    (double, 14, 2),
    (double, 10, 4),
    (double, 15, 1),
    (double, 11, 4),
    (double, 12, 2),
    (double, 14, 3),
    (double, 15, 2),
    (double, 12, 3),
    (double, 14, 4),
    (double, 15, 3),
    (double, 12, 4),
    (double, 15, 4),
)


def backward_kernel(
    tokens, context, low, mixed, hidden, slope_gate, slope_up, grad_second, unit_in, inv, norms, q_in, k_in, v_in,
    features, key_marks, cosines, sines, vec, wq, wo, wg, wu, wd,
    out, input_grad_out, vec_out,
    grads, halves, from_core, to_core, vectors, arena, total, unit, marks, key_aug, value_aug, probs_kept, scores_kept, turned_rows, dquery, dkey, dvalue,
    send_sems, recv_sems, core_send, core_recv, vec_send, vec_recv, load_sems, input_sems, extra_sems, wq_sems,
    feature_sems, unit_sems,
):
    rep = lax.axis_index("rep")
    core = lax.axis_index("fsdp")
    seq, width = total.shape
    shard = width // 2
    refs = (grads, halves, out, send_sems, recv_sems)

    def load(slot, source, target=None):
        return pltpu.make_async_copy(source, arena.at[slot] if target is None else target, load_sems.at[slot])

    def square(slot):
        return arena.at[slot, pl.ds(0, width), :]

    def sided(slot, source, first, second):
        return (
            pltpu.make_async_copy(
                source.at[:, aligned(first, shard, 128)], arena.at[slot, :, pl.ds(0, shard)], load_sems.at[slot]
            ),
            pltpu.make_async_copy(
                source.at[:, aligned(second, shard, 128)], arena.at[slot, :, pl.ds(shard, shard)], input_sems.at[slot]
            ),
        )

    def begin(loads):
        for one in loads if isinstance(loads, tuple) else (loads,):
            one.start()

    def finish(loads):
        for one in loads if isinstance(loads, tuple) else (loads,):
            one.wait()

    def core_copy(chunk):
        slot = lax.rem(chunk, RING)
        return pltpu.make_async_remote_copy(
            src_ref=to_core.at[lax.rem(chunk, 2)],
            dst_ref=from_core.at[slot],
            send_sem=core_send.at[slot],
            recv_sem=core_recv.at[slot],
            device_id=other_core(),
            device_id_type=MESH,
        )

    def emit(chunk, left, right):
        slot = lax.rem(chunk, 2)

        @pl.when(chunk >= 2)
        def _():
            core_copy(chunk - 2).wait_send()

        to_core[slot] = tn(arena[left, :, shard:], arena[right]).astype(BF16)
        grads[chunk] = tn(arena[left, :, :shard], arena[right]).astype(BF16)
        core_copy(chunk).start()

    def absorb(chunk):
        core_copy(chunk).wait_recv()
        slot = lax.rem(chunk, RING)
        grads[chunk] = (grads[chunk].astype(F32) + from_core[slot].astype(F32)).astype(BF16)

    def slot_work(slot, doubling):
        stages = range(STEPS, -1, -1)
        for stage in stages if doubling else ():
            wait = slot - FIRST_DOUBLING - DOUBLING_LAGS[stage]
            chunk = lax.div(4 * wait + 4, 5)

            @pl.when((wait >= 0) & (chunk <= fed) & (lax.div(5 * chunk, 4) == wait))
            def _():
                double(refs, chunk, stage)

        for stage in stages:
            chunk = slot - 1 - HALVING_LAGS[stage]

            @pl.when((chunk >= 0) & (chunk <= fed))
            def _():
                halve(refs, chunk, stage)

        for stage in stages if doubling else ():
            wait = slot - LATE_SLOT - LATE_LAGS[stage]

            @pl.when((wait >= 0) & (lax.rem(wait, LATE_EVERY) == 0))
            def _():
                halve(refs, fed + 1 + lax.div(wait, LATE_EVERY), stage)

    MIXED, LOW, SLOPE_GATE, SLOPE_UP, HIDDEN, GATE, UP, SIDED_CONTEXT, WD, WG, WU, WO, CONTEXT = range(13)
    ATTENDED, Q, K, V, GRAD_CONTEXT, PROJECTED, TOKENS = MIXED, SLOPE_GATE, SLOPE_UP, WD, HIDDEN, GATE, WG
    WQ = (WU, WO, LOW)
    blocks = wg.shape[1] // width
    fed = 3 * blocks

    def block_loads(j):
        cols = aligned(j * width, width)
        return {
            SLOPE_GATE: load(SLOPE_GATE, slope_gate.at[:, cols]),
            SLOPE_UP: load(SLOPE_UP, slope_up.at[:, cols]),
            WD: load(WD, wd.at[cols, :], square(WD)),
            WG: load(WG, wg.at[:, cols], square(WG)),
            WU: load(WU, wu.at[:, cols], square(WU)),
        }

    def hidden_load(j):
        rows = wd.shape[0] // 2
        return sided(HIDDEN + j, hidden, core * rows + j * shard, (1 - core) * rows + j * shard)

    def wq_loads(turn_number):
        part = width // 3
        return tuple(
            pltpu.make_async_copy(
                wq.at[:, aligned(n * width + turn_number * part, part)],
                arena.at[WQ[turn_number], pl.ds(0, width), pl.ds(n * part, part)],
                wq_sems.at[turn_number, n],
            )
            for n in range(3)
        )

    def feature_load(pair):
        slot = lax.rem(pair, 2)
        return pltpu.make_async_copy(
            features.at[pl.ds(2 * pair, 2)], marks.at[slot], feature_sems.at[slot]
        )

    first_loads = block_loads(0)
    mixed_load = load(MIXED, mixed)
    low_load = sided(LOW, low, core * shard, (1 - core) * shard)
    second_load = pltpu.make_async_copy(grad_second, total, extra_sems.at[0])
    block = 256

    def unit_load(r):
        return pltpu.make_async_copy(unit_in.at[pl.ds(r * block, block)], unit.at[r % 2], unit_sems.at[r % 2])

    context_load = load(CONTEXT, context)
    sided_load = sided(SIDED_CONTEXT, context, core * shard, (1 - core) * shard)
    wo_load = load(WO, wo, square(WO))
    late_loads = {
        Q: load(Q, q_in),
        K: load(K, k_in),
        V: load(V, v_in),
        TOKENS: sided(TOKENS, tokens, core * shard, (1 - core) * shard),
    }
    for one in (mixed_load, hidden_load(0), hidden_load(1), hidden_load(2), hidden_load(3), first_loads[WD],
                first_loads[SLOPE_GATE], first_loads[SLOPE_UP], low_load, first_loads[WG], second_load,
                first_loads[WU], wo_load, unit_load(0), unit_load(1), context_load, feature_load(0)):
        begin(one)
    vectors[0] = vec[...]
    greet()
    finish(mixed_load)

    tile = 512

    def down_step(j, carry):
        finish(hidden_load(j))
        emit(j, HIDDEN + j, MIXED)

        @pl.when(j > 0)
        def _():
            absorb(j - 1)
            slot_work(j, False)

        return carry

    lax.fori_loop(0, blocks, down_step, 0)
    begin(sided_load)
    finish(low_load)
    finish(second_load)

    def feed_step(j, carry):
        loads = block_loads(j)
        upcoming = block_loads(j + 1)
        more = j + 1 < blocks
        chunk = blocks + 2 * j

        def renew(*slots):
            @pl.when(more)
            def _():
                for slot in slots:
                    begin(upcoming[slot])

        def replace(*slots):
            @pl.when(jnp.logical_not(more))
            def _():
                for slot in slots:
                    begin(late_loads[slot])

        for slot in (WD, SLOPE_GATE, SLOPE_UP):
            finish(loads[slot])
        for r in range(seq // tile):
            rows = pl.ds(r * tile, tile)
            grad_hidden = nt(arena[MIXED, rows, :], arena[WD, :width, :])
            arena[GATE, rows, :] = (grad_hidden * arena[SLOPE_GATE, rows, :].astype(F32)).astype(BF16)
            arena[UP, rows, :] = (grad_hidden * arena[SLOPE_UP, rows, :].astype(F32)).astype(BF16)
        renew(WD, SLOPE_GATE, SLOPE_UP)
        replace(Q, K, V)
        emit(chunk, LOW, GATE)
        finish(loads[WG])
        for r in range(seq // tile):
            rows = pl.ds(r * tile, tile)
            total[rows, :] += nt(arena[GATE, rows, :], arena[WG, :width, :])
        renew(WG)
        replace(TOKENS)
        absorb(chunk - 1)
        slot_work(chunk, False)
        emit(chunk + 1, LOW, UP)
        finish(loads[WU])
        for r in range(seq // tile):
            rows = pl.ds(r * tile, tile)
            total[rows, :] += nt(arena[UP, rows, :], arena[WU, :width, :])
        renew(WU)
        absorb(chunk)
        slot_work(chunk + 1, False)
        return carry

    lax.fori_loop(0, blocks, feed_step, 0)

    begin(wq_loads(0))
    begin(wq_loads(2))
    gain_one = jnp.concatenate([norms[0, 0:1, :], norms[1, 0:1, :]], axis=1)
    bias_sum = jnp.zeros((1, width), F32)
    gain_sum = jnp.zeros((1, width), F32)
    for r in range(seq // block):
        rows = pl.ds(r * block, block)
        grad_normed = total[rows, :]
        unit_load(r).wait()
        unit_rows = unit[r % 2]
        bias_sum += jnp.sum(grad_normed, axis=0, keepdims=True)
        gain_sum += jnp.sum(grad_normed * unit_rows, axis=0, keepdims=True)
        scaled = grad_normed * gain_one
        grad_first = inv[rows, 0:1] * (scaled - row_mean(scaled) - unit_rows * row_mean(scaled * unit_rows))
        total[rows, :] = grad_first
        arena[ATTENDED, rows, :] = grad_first.astype(BF16)
        if r + 2 < seq // block:
            unit_load(r + 2).start()
    vectors[0, 0:1, :] = gain_sum
    vectors[0, 1:2, :] = bias_sum
    finish(sided_load)
    emit(fed, SIDED_CONTEXT, ATTENDED)
    finish(wo_load)
    absorb(fed - 1)
    slot_work(fed, False)
    for r in range(seq // tile):
        rows = pl.ds(r * tile, tile)
        arena[GRAD_CONTEXT, rows, :] = nt(arena[ATTENDED, rows, :], arena[WO, :width, :]).astype(BF16)
    begin(wq_loads(1))
    absorb(fed)
    for one in (context_load, late_loads[Q], late_loads[K], late_loads[V], late_loads[TOKENS]):
        finish(one)

    ones = jnp.where((lanes() >= SPLIT_LANE) & (lanes() < SPLIT_LANE + 3), 1.0, 0.0)
    part = width // 3
    block_count = seq // block

    def head_step(turn_number, number, carry):
        pair = 2 * turn_number + lax.div(number, 2)
        head = lax.rem(number, 2)
        place = lax.div(number, 2) * 128
        cols = aligned(pair * 128, 128)
        mark_slot = lax.rem(pair, 2)
        own_lanes = lax.div(lanes(), HEAD_DIM) == head

        def only(values):
            return jnp.where(own_lanes, values, jnp.zeros_like(values))

        @pl.when(head == 0)
        def _():
            feature_load(pair).wait()

            @pl.when(pair + 1 < HEADS // 2)
            def _():
                feature_load(pair + 1).start()

            key_aug[:, :128] = arena[K, :, cols]
            key_aug[:, 128:] = (key_marks[...].astype(F32) + ones).astype(BF16)
            value_aug[:, :128] = arena[V, :, cols]
            value_aug[:, 128:] = jnp.broadcast_to(ones, (seq, 128)).astype(BF16)
            turned_rows[0] = jnp.transpose(arena[Q, :, cols])
            turned_rows[1] = jnp.transpose(arena[GRAD_CONTEXT, :, cols])

        def products_of(r):
            rows = pl.ds(r * block, block)
            query = jnp.concatenate([only(arena[Q, rows, cols]), marks[mark_slot, head, rows, :]], axis=1)
            grads_here = only(arena[GRAD_CONTEXT, rows, cols])
            delta = jnp.sum(grads_here.astype(F32) * arena[CONTEXT, rows, cols].astype(F32), axis=1, keepdims=True)
            tail = split_lanes(jnp.zeros((block, 128), F32), -delta)
            return nt(query, key_aug[...]), nt(jnp.concatenate([grads_here, tail], axis=1), value_aug[...])

        key_only = only(key_aug[:, :128])
        upcoming = products_of(0)
        for r in range(block_count):
            rows = pl.ds(r * block, block)
            scores, grad_probs = upcoming
            upcoming = products_of(r + 1) if r + 1 < block_count else None
            probs = jnp.exp(scores)
            grad_scores = (probs * grad_probs).astype(BF16)
            probs_kept[rows, :] = probs.astype(BF16)
            scores_kept[rows, :] = grad_scores
            dquery_term = nn(grad_scores, key_only)

            dquery[rows, :] = jnp.where(head == 0, 0.0, dquery[rows, :]) + dquery_term

        own_rows = aligned(head * HEAD_DIM, HEAD_DIM)
        dkey[own_rows, :] = nn(turned_rows[0, own_rows, :], scores_kept[...])
        dvalue[own_rows, :] = nn(turned_rows[1, own_rows, :], probs_kept[...])

        @pl.when(head == 1)
        def _():
            turned = turn(dquery[...] * (HEAD_DIM ** (-0.5)), cosines[...], -sines[...])
            arena[PROJECTED + turn_number, :, aligned(place, 128)] = turned.astype(BF16)
            turned = turn(jnp.transpose(dkey[...]), cosines[...], -sines[...])
            arena[PROJECTED + turn_number, :, aligned(part + place, 128)] = turned.astype(BF16)
            arena[PROJECTED + turn_number, :, aligned(2 * part + place, 128)] = jnp.transpose(dvalue[...]).astype(BF16)

        slot_work(FIRST_ATTENTION + LATE_EVERY * turn_number + number, True)
        for stage in range(VECTOR_STEPS + 1):

            @pl.when(4 * turn_number + number == stage)
            def _():
                vector_stage(vectors, vec_send, vec_recv, stage)

        return carry

    def turn_step(turn_number, carry):
        lax.fori_loop(0, 4, functools.partial(head_step, turn_number), 0)
        chunk = fed + 1 + turn_number
        emit(chunk, TOKENS, PROJECTED + turn_number)
        absorb(chunk)
        slot_work(LATE_SLOT + LATE_EVERY * turn_number, True)
        return carry

    lax.fori_loop(0, 3, turn_step, 0)

    half = seq // 2
    mine = pltpu.make_async_copy(total.at[aligned(core * half, half)], input_grad_out.at[core], extra_sems.at[2])
    theirs = pltpu.make_async_remote_copy(
        src_ref=total.at[aligned((1 - core) * half, half)],
        dst_ref=input_grad_out.at[core],
        send_sem=core_send.at[RING],
        recv_sem=core_recv.at[RING],
        device_id=other_core(),
        device_id_type=MESH,
    )
    vec_out[...] = vectors[2 * VECTOR_STEPS]
    for number, (work, chunk, stage) in enumerate(REMAINDER):
        work(refs, chunk, stage)
        turn_number, odd = divmod(number, 3)
        if odd == 0 and turn_number < 3:
            finish(wq_loads(turn_number))
            for r in range(seq // tile):
                rows = pl.ds(r * tile, tile)
                total[rows, :] += nt(arena[PROJECTED + turn_number, rows, :], arena[WQ[turn_number], :width, :])
            if turn_number == 2:
                mine.start()
                theirs.start()
    mine.wait()
    theirs.wait()
    for number in range(2):
        core_copy(CHUNKS - 2 + number).wait_send()


def backward(tokens, saved, norms, key_marks, cosines, sines, vec, weights, outs):
    context, low, mixed, hidden, slope_gate, slope_up, grad_second, unit, inv, q, k, v, features = saved
    seq, width = tokens.shape
    dma = pltpu.SemaphoreType.DMA
    vmem = pl.BlockSpec(memory_space=pltpu.VMEM)
    hbm = pl.BlockSpec(memory_space=pl.ANY)
    chunks = (CHUNKS, width // 2, width)
    return pl.pallas_call(
        backward_kernel,
        out_shape=(
            jax.ShapeDtypeStruct(chunks, BF16),
            jax.ShapeDtypeStruct(outs, F32),
            jax.ShapeDtypeStruct(vec.shape, F32),
        ),
        in_specs=[hbm] * 9 + [vmem] * 2 + [hbm] * 4 + [vmem] * 4 + [hbm] * 5,
        out_specs=(hbm, hbm, vmem),
        scratch_shapes=[
            pltpu.VMEM(chunks, BF16),
            pltpu.VMEM((HALVES_RING,) + chunks[1:], BF16),
            pltpu.VMEM((RING,) + chunks[1:], BF16),
            pltpu.VMEM((2,) + chunks[1:], BF16),
            pltpu.VMEM((2 * VECTOR_STEPS + 1,) + vec.shape, F32),
            pltpu.VMEM((13, seq, width), BF16),
            pltpu.VMEM((seq, width), F32),
            pltpu.VMEM((2, 256, width), F32),
            pltpu.VMEM((2, 2, seq, FEATURES), BF16),
            pltpu.VMEM((seq, 256), BF16),
            pltpu.VMEM((seq, 256), BF16),
            pltpu.VMEM((seq, seq), BF16),
            pltpu.VMEM((seq, seq), BF16),
            pltpu.VMEM((2, 128, seq), BF16),
            pltpu.VMEM((seq, 128), F32),
            pltpu.VMEM((128, seq), F32),
            pltpu.VMEM((128, seq), F32),
            dma((HALVES_RING, 2 * STEPS + 1)),
            dma((HALVES_RING, 2 * STEPS)),
            dma((RING + 1,)),
            dma((RING + 1,)),
            dma((VECTOR_STEPS,)),
            dma((VECTOR_STEPS,)),
            dma((13,)),
            dma((13,)),
            dma((3,)),
            dma((3, 3)),
            dma((2,)),
            dma((2,)),
        ],
        compiler_params=pltpu.CompilerParams(collective_id=0, has_side_effects=True, vmem_limit_bytes=63 << 20),
    )(tokens, context, low, mixed, hidden, slope_gate, slope_up, grad_second, unit, inv, norms, q, k, v,
      features, key_marks, cosines, sines, vec, *weights)


def finish_kernel(
    summed, vec, activations, input_grad,
    activations_out, input_grad_out, qkv, out, gate, up, down, gain_one, bias_one, gain_two, bias_two,
    narrow, wide, acts, inputs, in_sems, out_sems, pass_sems,
):
    rows, width = narrow.shape[1:]
    part = width // 3
    fed = CHUNKS - 4
    held = ((activations, acts, activations_out), (input_grad, inputs, input_grad_out))
    fetches = [pltpu.make_async_copy(source, place, pass_sems.at[n]) for n, (source, place, _) in enumerate(held)]
    passes = [pltpu.make_async_copy(place, target, pass_sems.at[n]) for n, (_, place, target) in enumerate(held)]
    loads = [pltpu.make_async_copy(summed.at[n], narrow.at[n], in_sems.at[n]) for n in range(CHUNKS)]
    for load in loads + fetches:
        load.start()
    core = lax.axis_index("fsdp")
    for n, ref in enumerate((gain_one, bias_one, gain_two, bias_two)):
        ref[...] = vec[n, aligned(core * rows, rows, 128)]
    stores = []
    for n in range(CHUNKS):
        loads[n].wait()
        wide[n] = narrow[n].astype(F32)
        if n < 4:
            parts = [(wide.at[n], down.at[pl.ds(rows * n, rows)])]
        elif n < fed:
            parts = [(wide.at[n], (gate, up)[n % 2].at[:, pl.ds(width * ((n - 4) // 2), width)])]
        elif n == fed:
            parts = [(wide.at[n], out)]
        else:
            parts = [
                (wide.at[n, :, pl.ds(m * part, part)], qkv.at[:, pl.ds(m * width + (n - fed - 1) * part, part)])
                for m in range(3)
            ]
        for source, target in parts:
            stores.append(pltpu.make_async_copy(source, target, out_sems.at[len(stores)]))
            stores[-1].start()
    for fetch, store in zip(fetches, passes):
        fetch.wait()
        store.start()
    for store in stores + passes:
        store.wait()


def finish(summed, vec, activations, input_grad):
    rows, cols = summed.shape[1:]
    vmem = pl.BlockSpec(memory_space=pltpu.VMEM)
    hbm = pl.BlockSpec(memory_space=pl.ANY)

    def shape(high, across):
        return jax.ShapeDtypeStruct((rows * high, cols * across), F32)

    def like(array):
        return jax.ShapeDtypeStruct(array.shape, array.dtype)

    return pl.pallas_call(
        finish_kernel,
        out_shape=(like(activations), like(input_grad), shape(1, 3), shape(1, 1), shape(1, 4), shape(1, 4), shape(4, 1))
        + (jax.ShapeDtypeStruct((rows,), F32),) * 4,
        in_specs=[hbm, vmem, hbm, hbm],
        out_specs=(hbm,) * 7 + (vmem,) * 4,
        scratch_shapes=[
            pltpu.VMEM(summed.shape, BF16),
            pltpu.VMEM(summed.shape, F32),
            pltpu.VMEM(activations.shape, activations.dtype),
            pltpu.VMEM(input_grad.shape, input_grad.dtype),
            pltpu.SemaphoreType.DMA((CHUNKS,)),
            pltpu.SemaphoreType.DMA((CHUNKS + 6,)),
            pltpu.SemaphoreType.DMA((2,)),
        ],
        compiler_params=pltpu.CompilerParams(vmem_limit_bytes=62 << 20),
    )(summed, vec, activations, input_grad)


def shards(
    tokens,
    lengths,
    w_qkv,
    w_out,
    w_gate,
    w_up,
    w_down,
    norm1_gain,
    norm1_bias,
    norm2_gain,
    norm2_bias,
    cotangent,
):
    norms = (norm1_gain, norm1_bias, norm2_gain, norm2_bias)
    weights = (w_qkv, w_out, w_gate, w_up, w_down)
    (q, k, v, context, features, low, unit, inv, slope_gate, slope_up, hidden, grad_second, mixed, activations,
     vec, norms, key_marks, cosines, sines, stream, *weights) = forward(tokens, cotangent, weights, norms, lengths)
    saved = (context, low, mixed, hidden, slope_gate, slope_up, grad_second, unit, inv, q, k, v, features)
    summed, input_grad, vec_sum = backward(
        stream, saved, norms, key_marks, cosines, sines, vec, weights, tokens.shape
    )
    groups = lax.axis_size("rep") // UNITS
    if groups > 1:
        alike = [[UNITS * g + n for g in range(groups)] for n in range(UNITS)]
        summed = lax.psum(summed, "rep", axis_index_groups=alike)
        vec_sum = lax.psum(vec_sum, "rep", axis_index_groups=alike)
    return finish(summed, vec_sum, activations, input_grad)


def solution(mesh):
    placed = (
        P("rep", "fsdp", None),
        P("rep", None),
        P("fsdp", None),
        P("fsdp", None),
        P("fsdp", None),
        P("fsdp", None),
        P("fsdp", None),
        P("fsdp"),
        P("fsdp"),
        P("fsdp"),
        P("fsdp"),
        P("rep", "fsdp", None),
    )
    return jax.shard_map(
        shards,
        mesh=mesh,
        in_specs=placed,
        out_specs=(
            P("rep", "fsdp", None),
            P("rep", "fsdp", None),
            P("fsdp", None),
            P("fsdp", None),
            P("fsdp", None),
            P("fsdp", None),
            P("fsdp", None),
            P("fsdp"),
            P("fsdp"),
            P("fsdp"),
            P("fsdp"),
        ),
        check_vma=False,
    )
```

```python
import functools

import jax
import jax.numpy as jnp
import numpy as np
from jax import lax
from jax.experimental import pallas as pl
from jax.experimental.pallas import tpu as pltpu
from jax.sharding import PartitionSpec as P

HEADS = 12
HEAD_DIM = 64


EPSILON = 1e-05


CHUNKS = 16
PARTS = 3
PART_ROWS = 128
UNITS = 16
STEPS = 4
HALVES_RING = 8
MESH = pl.DeviceIdType.MESH
BF16 = jnp.bfloat16
F32 = jnp.float32


def bit_of(value, weight):
    return lax.rem(lax.div(value, weight), 2)


ORDERS = ((1, 2, 4, 8), (2, 1, 4, 8), (4, 1, 2, 8), (4, 2, 1, 8))


def partner_of(weight, bit):
    return (lax.axis_index("rep") + weight * (1 - 2 * bit), lax.axis_index("fsdp"))


def transfer_plan():
    rep = lax.axis_index("rep")
    bits = {weight: bit_of(rep, weight) for weight in ORDERS[0]}
    partners = {weight: partner_of(weight, bits[weight])[0] for weight in ORDERS[0]}
    kept, sent = [], []
    for number, order in enumerate(ORDERS):
        starts = [min(number, PARTS - 1) * PART_ROWS]
        others = [None]
        for step in range(STEPS - 1):
            half = PART_ROWS >> (step + 1)
            others.append(starts[-1] + (1 - bits[order[step]]) * half)
            starts.append(starts[-1] + bits[order[step]] * half)
        kept.append(starts)
        sent.append(others)
    return kept, sent, partners, bits[ORDERS[0][-1]]


def choose(part, odd, values):
    if part < PARTS - 1:
        return values(part)
    return values(part) + odd * (values(part + 1) - values(part))


def other_core():
    return (lax.axis_index("rep"), 1 - lax.axis_index("fsdp"))


def region(refs, ref, chunk, part, level, flip):
    kept, sent, _, bit = refs[5]
    rows = PART_ROWS >> min(level, STEPS - 1)
    table = sent if flip and level < STEPS else kept
    start = choose(part, last_bit(chunk), lambda number: table[number][min(level, STEPS - 1)])
    if level < STEPS:
        return (chunk, pl.ds(pl.multiple_of(start, 16), rows), slice(None))
    half = ref.shape[2] // 2
    column = (1 - bit if flip else bit) * half
    return (chunk, pl.ds(pl.multiple_of(start, 16), rows), pl.ds(pl.multiple_of(column, 128), half))


def last_bit(chunk):
    return chunk % 2 if isinstance(chunk, int) else lax.rem(chunk, 2)


def rep_partner(refs, chunk, part, step):
    partners = refs[5][2]
    there = choose(part, last_bit(chunk), lambda number: partners[ORDERS[number][step]])
    return (there, lax.axis_index("fsdp"))


def ring_slot(chunk):
    return chunk % HALVES_RING if isinstance(chunk, int) else lax.rem(chunk, HALVES_RING)


def landing(ref, chunk, part, step):
    start = part * PART_ROWS + PART_ROWS - (PART_ROWS >> step)
    chunk = ring_slot(chunk)
    if step < STEPS - 1:
        return (chunk, pl.ds(start, PART_ROWS >> (step + 1)), slice(None))
    return (chunk, pl.ds(start, PART_ROWS >> step), pl.ds(0, ref.shape[2] // 2))


def halving_copy(refs, chunk, part, step):
    grads, halves, _, send_sems, recv_sems = refs[:5]
    slot = ring_slot(chunk)
    return pltpu.make_async_remote_copy(
        src_ref=grads.at[region(refs, grads, chunk, part, step + 1, True)],
        dst_ref=halves.at[landing(halves, chunk, part, step)],
        send_sem=send_sems.at[slot, step],
        recv_sem=recv_sems.at[slot, step],
        device_id=rep_partner(refs, chunk, part, step),
        device_id_type=MESH,
    )


def all_parts(ref, first, step):
    rows = PARTS * (PART_ROWS >> min(step + 1, STEPS - 1))
    columns = ref.shape[2] if step < STEPS - 1 else ref.shape[2] // 2
    return ref.at[first, pl.ds(0, rows), pl.ds(0, columns)]


def wait_parts(ref, first, step, send_sem, recv_sem):
    whole = all_parts(ref, first, step)
    pltpu.make_async_remote_copy(
        src_ref=whole,
        dst_ref=whole,
        send_sem=send_sem,
        recv_sem=recv_sem,
        device_id=other_core(),
        device_id_type=MESH,
    ).wait()


def halving_add(refs, chunk, part, step):
    grads, halves = refs[:2]
    kept = region(refs, grads, chunk, part, step + 1, False)
    theirs = halves[landing(halves, chunk, part, step)]
    grads[kept] = (grads[kept].astype(F32) + theirs.astype(F32)).astype(BF16)


def settle_copy(refs, chunk, part):
    grads, _, out, send_sems, _ = refs[:5]
    mine = region(refs, grads, chunk, part, STEPS, False)
    return pltpu.make_async_copy(grads.at[mine], out.at[mine], send_sems.at[ring_slot(chunk), 2 * STEPS])


def doubling_copy(refs, chunk, part, step):
    grads, _, out, send_sems, recv_sems = refs[:5]
    slot = ring_slot(chunk)
    mine = region(refs, out, chunk, part, step + 1, False)
    return pltpu.make_async_remote_copy(
        src_ref=(grads if step == STEPS - 1 else out).at[mine],
        dst_ref=out.at[mine],
        send_sem=send_sems.at[slot, STEPS + step],
        recv_sem=recv_sems.at[slot, STEPS + step],
        device_id=rep_partner(refs, chunk, part, step),
        device_id_type=MESH,
    )


def halve(refs, chunk, stage):
    _, halves, _, send_sems, recv_sems = refs[:5]
    slot = ring_slot(chunk)
    if stage > 0:
        wait_parts(halves, slot, stage - 1, send_sems.at[slot, stage - 1], recv_sems.at[slot, stage - 1])
    for part in range(PARTS):
        if stage > 0:
            halving_add(refs, chunk, part, stage - 1)
        if stage < STEPS:
            halving_copy(refs, chunk, part, stage).start()
        else:
            settle_copy(refs, chunk, part).start()


def double(refs, chunk, stage):
    grads, _, out, send_sems, recv_sems = refs[:5]
    slot = ring_slot(chunk)
    if stage > 0:
        sems = send_sems.at[slot, 2 * STEPS - stage], recv_sems.at[slot, 2 * STEPS - stage]
        wait_parts(out, chunk, STEPS - stage, *sems)
    if stage == 1:
        sizes = [all_parts(ref, chunk, STEPS - 1) for ref in (grads, out)]
        pltpu.make_async_copy(*sizes, send_sems.at[slot, 2 * STEPS]).wait()
    if stage < STEPS:
        for part in range(PARTS):
            doubling_copy(refs, chunk, part, STEPS - 1 - stage).start()


def greet():
    rep = lax.axis_index("rep")
    barrier = pltpu.get_barrier_semaphore()
    pl.semaphore_signal(barrier, inc=1, device_id=other_core(), device_id_type=MESH)
    for weight in (1, 2, 4, 8):
        there = partner_of(weight, bit_of(rep, weight))
        pl.semaphore_signal(barrier, inc=1, device_id=there, device_id_type=MESH)
    pl.semaphore_wait(barrier, 5)


def vector_copy(vectors, send_sems, recv_sems, step):
    rep = lax.axis_index("rep")
    if step == 0:
        there = other_core()
    else:
        weight = 1 << (step - 1)
        there = partner_of(weight, bit_of(rep, weight))
    return pltpu.make_async_remote_copy(
        src_ref=vectors.at[2 * step],
        dst_ref=vectors.at[2 * step + 1],
        send_sem=send_sems.at[step],
        recv_sem=recv_sems.at[step],
        device_id=there,
        device_id_type=MESH,
    )


VECTOR_STEPS = 5


def vector_stage(vectors, send_sems, recv_sems, stage):
    if stage > 0:
        vector_copy(vectors, send_sems, recv_sems, stage - 1).wait()
        vectors[2 * stage] = vectors[2 * stage - 2] + vectors[2 * stage - 1]
    if stage < VECTOR_STEPS:
        vector_copy(vectors, send_sems, recv_sems, stage).start()


SEQ_ROWS = 512
NEG = -1e30
FEATURES = 128
SPLIT_LANE = 8


def nn(left, right):
    return jnp.dot(left, right, preferred_element_type=F32)


def nt(left, right):
    return lax.dot_general(left, right, (((1,), (1,)), ((), ())), preferred_element_type=F32)


def tn(left, right):
    return lax.dot_general(left, right, (((0,), (0,)), ((), ())), preferred_element_type=F32)


def aligned(start, size, multiple=None):
    return pl.ds(pl.multiple_of(start, multiple or size), size)


def lanes():
    return lax.broadcasted_iota(jnp.int32, (1, 128), 1)


def head_mask(values, first):
    low = lanes() < HEAD_DIM
    zero = jnp.zeros_like(values)
    return jnp.where(low, values, zero) if first else jnp.where(low, zero, values)


def turn(values, cosines, sines):
    first = lax.rem(lanes(), HEAD_DIM) < HEAD_DIM // 2
    swapped = jnp.where(first, pltpu.roll(values, 96, 1), pltpu.roll(values, 32, 1))
    return values * cosines + swapped * sines


def split_lanes(base, values):
    high = values.astype(BF16).astype(F32)
    middle = (values - high).astype(BF16).astype(F32)
    low = values - high - middle
    lane = lanes()
    out = jnp.where(lane == SPLIT_LANE, high, base)
    out = jnp.where(lane == SPLIT_LANE + 1, middle, out)
    return jnp.where(lane == SPLIT_LANE + 2, low, out).astype(BF16)


def row_mean(values):
    return jnp.mean(values, axis=1, keepdims=True)


def forward_kernel(
    tokens, cotangent, w_qkv, w_out, w_gate, w_up, w_down, norm_one, norm_two, norm_three, norm_four, lengths,
    frequencies,
    q_out, k_out, v_out, context_out, features_out, low_out, unit_out, inv_out, slope_gate_out, slope_up_out,
    hidden_out, grad_second_out, mixed_out, activations_out, vec_out,
    norms_out, key_marks, cosines, sines, x_out, wq_out, wo_out, wg_out, wu_out, wd_out,
    x, g, wq, wo, wg, wu, wd, nv, qs, ks, vs, ctx, total, key_aug, value_aug, pieces, seconds,
    norms, query_marks, marks, products, send_sems, recv_sems, own_sems, save_sems, act_sems, mark_sems,
):
    rep = lax.axis_index("rep")
    core = lax.axis_index("fsdp")
    there = (rep, 1 - core)
    seq, width = x.shape
    half = seq // 2

    barrier = pltpu.get_barrier_semaphore()
    pl.semaphore_signal(barrier, inc=1, device_id=there, device_id_type=MESH)
    pl.semaphore_wait(barrier, 1)

    norms[...] = jnp.zeros_like(norms)
    for n, ref in enumerate((norm_one, norm_two, norm_three, norm_four)):
        norms[n, :] = ref[...].astype(F32)

    def rows_of(ref, block):
        return ref.at[aligned(core * block, block)]

    exchanges = (
        (tokens.at[core], tokens.at[1 - core], rows_of(x, half)),
        (w_qkv, w_qkv, rows_of(wq, w_qkv.shape[0])),
        (w_out, w_out, rows_of(wo, w_out.shape[0])),
        (norms, norms, nv.at[core]),
        (w_gate, w_gate, rows_of(wg, w_gate.shape[0])),
        (w_up, w_up, rows_of(wu, w_up.shape[0])),
        (w_down, w_down, rows_of(wd, w_down.shape[0])),
        (cotangent.at[core], cotangent.at[1 - core], rows_of(g, half)),
    )

    def copies(number):
        mine, theirs, place = exchanges[number]
        return (
            pltpu.make_async_copy(mine, place, own_sems.at[number]),
            pltpu.make_async_remote_copy(
                src_ref=theirs,
                dst_ref=place,
                send_sem=send_sems.at[number],
                recv_sem=recv_sems.at[number],
                device_id=there,
                device_id_type=MESH,
            ),
        )

    for number in range(len(exchanges)):
        for copy in copies(number):
            copy.start()

    def arrived(number):
        for copy in copies(number):
            copy.wait()

    def save(source, target, number):
        copy = pltpu.make_async_copy(source, target, save_sems.at[number])
        copy.start()
        return copy

    places = lax.broadcasted_iota(jnp.int32, (seq, 128), 0)
    segment = jnp.zeros_like(places)
    begins = jnp.zeros_like(places)
    doc_end = jnp.int32(0)
    for doc in range(lengths.shape[1]):
        doc_end = doc_end + lengths[core, doc]
        past = places >= doc_end
        segment = segment + past.astype(jnp.int32)
        begins = jnp.where(past, doc_end, begins)
    same = segment == lanes()
    query_marks[...] = jnp.where(same, 1.0, 0.0).astype(BF16)
    key_marks[...] = jnp.where(same | (lanes() >= SPLIT_LANE), 0.0, NEG).astype(BF16)
    angles = (places - begins).astype(F32) * frequencies[0:1, :]
    cosines[...] = jnp.cos(angles)
    side = jnp.where(lax.rem(lanes(), HEAD_DIM) < HEAD_DIM // 2, -1.0, 1.0)
    sines[...] = jnp.sin(angles) * side

    arrived(0)
    arrived(1)
    tile = 512
    for n, out in enumerate((qs, ks, vs)):
        for r in range(seq // tile):
            rows = pl.ds(r * tile, tile)
            product_rows = nn(x[rows, :], wq[:, pl.ds(n * width, width)])
            if n == 2:
                out[rows, :] = product_rows.astype(BF16)
                continue
            for pair in range(width // 128):
                cols = slice(pair * 128, pair * 128 + 128)
                turned = turn(product_rows[:, cols], cosines[rows, :], sines[rows, :]).astype(BF16)
                if n == 0:
                    turned = turned * jnp.asarray(HEAD_DIM ** (-0.5), BF16)
                out[rows, cols] = turned
    saves = {12: save(x, x_out, 12), 0: save(qs, q_out, 0), 1: save(ks, k_out, 1), 2: save(vs, v_out, 2)}

    saves[7] = save(wq, wq_out, 7)

    block = 256
    steps = [(a, r) for r in range(seq // block) for a in range(2)]

    def mark_copy(pair):
        slot = lax.rem(pair, 2)
        return pltpu.make_async_copy(marks.at[slot], features_out.at[pl.ds(2 * pair, 2)], mark_sems.at[slot])

    weight_saves = [
        pltpu.make_async_copy(source, target, save_sems.at[8 + number])
        for number, (source, target) in enumerate(((wo, wo_out), (wg, wg_out), (wu, wu_out), (wd, wd_out)))
    ]

    def pair_step(pair, carry):
        for number, turn_number in enumerate((1, 2, 3, 4)):

            @pl.when(pair == turn_number)
            def _():
                arrived((2, 4, 5, 6)[number])
                weight_saves[number].start()

        cols = aligned(pair * 128, 128)
        mark_slot = lax.rem(pair, 2)

        @pl.when(pair >= 2)
        def _():
            mark_copy(pair - 2).wait()

        key_aug[:, :128] = ks[:, cols]
        key_aug[:, 128:] = key_marks[...]
        for a in range(2):
            value_aug[a, :, :128] = head_mask(vs[:, cols], a == 0)
            value_aug[a, :, 128:] = jnp.ones((seq, 128), BF16)

        def scores_of(a, r):
            rows = pl.ds(r * block, block)
            query = jnp.concatenate([head_mask(qs[rows, cols], a == 0), query_marks[rows, :]], axis=1)
            return nt(query, key_aug[...])

        scores = scores_of(*steps[0])
        parts = [None, None]
        for number, (a, r) in enumerate(steps):
            rows = pl.ds(r * block, block)
            upcoming = scores_of(*steps[number + 1]) if number + 1 < len(steps) else None
            row_max = jnp.max(scores, axis=1, keepdims=True)
            probs = jnp.exp(scores - row_max).astype(BF16)
            summed = nn(probs, value_aug[a])
            row_total = summed[:, 128:]
            parts[a] = summed[:, :128] / row_total
            lse = row_max + jnp.log(row_total)
            marks[mark_slot, a, rows, :] = split_lanes(query_marks[rows, :].astype(F32), -lse)
            if a == 1:
                ctx[rows, cols] = (parts[0] + parts[1]).astype(BF16)
            scores = upcoming
        mark_copy(pair).start()
        return carry

    lax.fori_loop(0, HEADS // 2, pair_step, 0)
    saves[3] = save(ctx, context_out, 3)

    low = qs
    saves[0].wait()
    arrived(3)

    def vector(n):
        return jnp.concatenate([nv[0, n : n + 1, :], nv[1, n : n + 1, :]], axis=1)

    for r in range(seq // block):
        rows = pl.ds(r * block, block)
        first_sum = x[rows, :].astype(F32) + nn(ctx[rows, :], wo[...])
        centre = first_sum - row_mean(first_sum)
        inv = lax.rsqrt(row_mean(centre * centre) + EPSILON)
        unit = centre * inv
        normed = unit * vector(0) + vector(1)
        seconds[rows, :] = unit
        inv_out[rows, :] = jnp.broadcast_to(inv, (block, 128))
        total[rows, :] = normed
        low[rows, :] = normed.astype(BF16)
    saves[4] = save(seconds, unit_out, 4)
    saves[5] = save(low, low_out, 5)

    slots, _, tile, columns = pieces.shape
    row_tiles = seq // tile
    count = row_tiles * (wg.shape[1] // columns)
    outs = (slope_gate_out, slope_up_out, hidden_out)

    def piece_copy(number, n):
        slot = lax.rem(number, slots)
        rows = aligned(lax.rem(number, row_tiles) * tile, tile)
        cols = aligned(lax.div(number, row_tiles) * columns, columns)
        return pltpu.make_async_copy(pieces.at[slot, n], outs[n].at[rows, cols], act_sems.at[slot, n])

    def multiply(number, slot):
        rows = aligned(lax.rem(number, row_tiles) * tile, tile)
        cols = aligned(lax.div(number, row_tiles) * columns, columns)
        products[slot, 0] = nn(low[rows, :], wg[:, cols])
        products[slot, 1] = nn(low[rows, :], wu[:, cols])

    def take(number, slot):
        rows = aligned(lax.rem(number, row_tiles) * tile, tile)
        cols = aligned(lax.div(number, row_tiles) * columns, columns)
        gate = products[slot, 0]
        up = products[slot, 1]
        gate_sig = 0.5 + 0.5 * jnp.tanh(0.5 * gate)
        gate_silu = gate * gate_sig
        place = lax.rem(number, slots)
        pieces[place, 0] = (up * (gate_sig + gate_silu * (1.0 - gate_sig))).astype(BF16)
        pieces[place, 1] = gate_silu.astype(BF16)
        hidden = (gate_silu * up).astype(BF16)
        pieces[place, 2] = hidden
        total[rows, :] += nn(hidden, wd[cols, :])

    def feed_step(turn_number, carry):
        number = 2 * turn_number

        @pl.when(number >= slots)
        def _():
            for n in range(3):
                piece_copy(number - slots, n).wait()
                piece_copy(number - slots + 1, n).wait()

        multiply(number + 1, 1)
        take(number, 0)
        multiply(jnp.minimum(number + 2, count - 1), 0)
        take(number + 1, 1)
        for n in range(3):
            piece_copy(number, n).start()
            piece_copy(number + 1, n).start()
        return carry

    multiply(jnp.int32(0), 0)
    lax.fori_loop(0, count // 2, feed_step, 0)

    acts = ctx
    saves[3].wait()
    arrived(7)
    saves[2].wait()
    saves[4].wait()
    gain_two, bias_two = vector(2), vector(3)
    bias_sum = jnp.zeros((1, width), F32)
    gain_sum = jnp.zeros((1, width), F32)
    for r in range(seq // block):
        rows = pl.ds(r * block, block)
        second_sum = total[rows, :]
        centre = second_sum - row_mean(second_sum)
        inv = lax.rsqrt(row_mean(centre * centre) + EPSILON)
        unit = centre * inv
        acts[rows, :] = (unit * gain_two + bias_two).astype(BF16)
        grad_out = g[rows, :].astype(F32)
        bias_sum += jnp.sum(grad_out, axis=0, keepdims=True)
        gain_sum += jnp.sum(grad_out * unit, axis=0, keepdims=True)
        scaled = grad_out * gain_two
        grad_second = inv * (scaled - row_mean(scaled) - unit * row_mean(scaled * unit))
        seconds[rows, :] = grad_second
        vs[rows, :] = grad_second.astype(BF16)
        pltpu.make_async_copy(seconds.at[rows], grad_second_out.at[rows], save_sems.at[4]).start()
        pltpu.make_async_copy(vs.at[rows], mixed_out.at[rows], save_sems.at[2]).start()
    norms_out[...] = nv[...]
    vec_out[...] = jnp.zeros_like(vec_out)
    vec_out[2:3, :] = gain_sum
    vec_out[3:4, :] = bias_sum
    del saves[0], saves[3]
    saves[4] = pltpu.make_async_copy(seconds, grad_second_out, save_sems.at[4])
    saves[2] = pltpu.make_async_copy(vs, mixed_out, save_sems.at[2])

    mine = pltpu.make_async_copy(rows_of(acts, half), activations_out.at[core], save_sems.at[6])
    mine.start()
    theirs = pltpu.make_async_remote_copy(
        src_ref=acts.at[aligned((1 - core) * half, half)],
        dst_ref=activations_out.at[core],
        send_sem=send_sems.at[len(exchanges)],
        recv_sem=recv_sems.at[len(exchanges)],
        device_id=there,
        device_id_type=MESH,
    )
    theirs.start()
    for copy in list(saves.values()) + weight_saves:
        copy.wait()
    for pair in range(HEADS // 2 - 2, HEADS // 2):
        mark_copy(pair).wait()
    for number in range(slots):
        for n in range(3):
            piece_copy(jnp.int32(count - slots + number), n).wait()
    mine.wait()
    theirs.wait()


def forward(tokens, cotangent, weights, norms, lengths):
    w_qkv, w_out, w_gate, w_up, w_down = weights
    seq, width = 2 * tokens.shape[1], tokens.shape[2]
    hidden_width = w_gate.shape[1]
    dma = pltpu.SemaphoreType.DMA
    vmem = pl.BlockSpec(memory_space=pltpu.VMEM)
    hbm = pl.BlockSpec(memory_space=pl.ANY)

    def shape(*dims, dtype=BF16):
        return jax.ShapeDtypeStruct(dims, dtype)

    lane = np.arange(128) % (HEAD_DIM // 2)
    frequencies = np.broadcast_to(1000.0 ** (-2.0 * lane / HEAD_DIM), (8, 128)).astype(np.float32)

    def full(shard):
        return pltpu.VMEM((2 * shard.shape[0], shard.shape[1]), BF16)

    rows = shape(seq, width)
    wide = shape(seq, hidden_width)
    return pl.pallas_call(
        forward_kernel,
        out_shape=(
            rows, rows, rows, rows, shape(HEADS, seq, FEATURES), rows, shape(seq, width, dtype=F32),
            shape(seq, 128, dtype=F32), wide, wide, wide, shape(seq, width, dtype=F32), rows,
            shape(*tokens.shape), shape(8, width, dtype=F32), shape(2, 8, *norms[0].shape, dtype=F32),
            shape(seq, FEATURES), shape(seq, 128, dtype=F32), shape(seq, 128, dtype=F32), rows,
        )
        + tuple(shape(2 * shard.shape[0], shard.shape[1]) for shard in weights),
        in_specs=[hbm] * 7 + [vmem] * 4 + [pl.BlockSpec(memory_space=pltpu.SMEM), vmem],
        out_specs=(hbm, hbm, hbm, hbm, hbm, hbm, hbm, vmem, hbm, hbm, hbm, hbm, hbm, hbm, vmem, vmem)
        + (vmem,) * 3
        + (hbm,) * 6,
        scratch_shapes=[
            pltpu.VMEM((seq, width), BF16),
            pltpu.VMEM((seq, width), BF16),
            full(w_qkv), full(w_out), full(w_gate), full(w_up), full(w_down),
            pltpu.VMEM((2, 8) + norms[0].shape, F32),
            pltpu.VMEM((seq, width), BF16),
            pltpu.VMEM((seq, width), BF16),
            pltpu.VMEM((seq, width), BF16),
            pltpu.VMEM((seq, width), BF16),
            pltpu.VMEM((seq, width), F32),
            pltpu.VMEM((seq, 256), BF16),
            pltpu.VMEM((2, seq, 256), BF16),
            pltpu.VMEM((4, 3, 256, 768), BF16),
            pltpu.VMEM((seq, width), F32),
            pltpu.VMEM((8,) + norms[0].shape, F32),
            pltpu.VMEM((seq, FEATURES), BF16),
            pltpu.VMEM((2, 2, seq, FEATURES), BF16),
            pltpu.VMEM((2, 2, 256, 768), F32),
            dma((9,)), dma((9,)), dma((8,)), dma((13,)), dma((4, 3)), dma((2,)),
        ],
        compiler_params=pltpu.CompilerParams(collective_id=1, has_side_effects=True, vmem_limit_bytes=63 << 20),
    )(tokens, cotangent, w_qkv, w_out, w_gate, w_up, w_down, *norms, lengths, jnp.asarray(frequencies))


RING = 4
FIRST_ATTENTION = 13
FIRST_DOUBLING = 13
LATE_SLOT = 17
LATE_EVERY = 5
HALVING_LAGS = (0, 3, 5, 8, 11)
LATE_LAGS = (0, 3, 5, 7, 10)
DOUBLING_LAGS = (0, 3, 5, 8, 10)
REMAINDER = (
    (double, 13, 0),
    (double, 4, 4),
    (double, 5, 4),
    (double, 6, 3),
    (halve, 14, 3),
    (double, 7, 3),
    (halve, 15, 1),
    (double, 8, 2),
    (double, 9, 2),
    (double, 13, 1),
    (double, 6, 4),
    (double, 10, 1),
    (double, 11, 1),
    (double, 12, 0),
    (halve, 14, 4),
    (halve, 15, 2),
    (double, 14, 0),
    (double, 7, 4),
    (double, 8, 3),
    (double, 13, 2),
    (double, 9, 3),
    (halve, 15, 3),
    (double, 10, 2),
    (double, 11, 2),
    (double, 13, 3),
    (double, 14, 1),
    (double, 8, 4),
    (double, 9, 4),
    (double, 10, 3),
    (halve, 15, 4),
    (double, 15, 0),
    (double, 11, 3),
    (double, 13, 4),
    (double, 12, 1),
    (double, 14, 2),
    (double, 10, 4),
    (double, 15, 1),
    (double, 11, 4),
    (double, 12, 2),
    (double, 14, 3),
    (double, 15, 2),
    (double, 12, 3),
    (double, 14, 4),
    (double, 15, 3),
    (double, 12, 4),
    (double, 15, 4),
)


def backward_kernel(
    tokens, context, low, mixed, hidden, slope_gate, slope_up, grad_second, unit_in, inv_in, norms, q_in, k_in, v_in,
    features, key_marks, cosines_in, sines_in, vec, wq, wo, wg, wu, wd,
    out, input_grad_out, vec_out,
    grads, halves, from_core, to_core, vectors, arena, total, unit, marks, key_aug, value_aug, probs_kept, scores_kept, turned_rows, dquery, dkey, dvalue, inv, cosines,
    sines,
    send_sems, recv_sems, core_send, core_recv, vec_send, vec_recv, load_sems, input_sems, extra_sems, wq_sems,
    feature_sems, unit_sems, table_sems,
):
    rep = lax.axis_index("rep")
    core = lax.axis_index("fsdp")
    seq, width = total.shape
    shard = width // 2
    refs = (grads, halves, out, send_sems, recv_sems, transfer_plan())

    def load(slot, source, target=None):
        return pltpu.make_async_copy(source, arena.at[slot] if target is None else target, load_sems.at[slot])

    def square(slot):
        return arena.at[slot, pl.ds(0, width), :]

    def sided(slot, source, first, second):
        return (
            pltpu.make_async_copy(
                source.at[:, aligned(first, shard, 128)], arena.at[slot, :, pl.ds(0, shard)], load_sems.at[slot]
            ),
            pltpu.make_async_copy(
                source.at[:, aligned(second, shard, 128)], arena.at[slot, :, pl.ds(shard, shard)], input_sems.at[slot]
            ),
        )

    def begin(loads):
        for one in loads if isinstance(loads, tuple) else (loads,):
            one.start()

    def finish(loads):
        for one in loads if isinstance(loads, tuple) else (loads,):
            one.wait()

    def core_copy(chunk):
        slot = lax.rem(chunk, RING)
        return pltpu.make_async_remote_copy(
            src_ref=to_core.at[lax.rem(chunk, 2)],
            dst_ref=from_core.at[slot],
            send_sem=core_send.at[slot],
            recv_sem=core_recv.at[slot],
            device_id=other_core(),
            device_id_type=MESH,
        )

    def emit(chunk, left, right):
        slot = lax.rem(chunk, 2)

        @pl.when(chunk >= 2)
        def _():
            core_copy(chunk - 2).wait_send()

        to_core[slot] = tn(arena[left, :, shard:], arena[right]).astype(BF16)
        grads[chunk] = tn(arena[left, :, :shard], arena[right]).astype(BF16)
        core_copy(chunk).start()

    def absorb(chunk):
        core_copy(chunk).wait_recv()
        slot = lax.rem(chunk, RING)
        grads[chunk] = (grads[chunk].astype(F32) + from_core[slot].astype(F32)).astype(BF16)

    def slot_work(slot, doubling):
        stages = range(STEPS, -1, -1)
        for stage in stages if doubling else ():
            wait = slot - FIRST_DOUBLING - DOUBLING_LAGS[stage]
            chunk = lax.div(4 * wait + 4, 5)

            @pl.when((wait >= 0) & (chunk <= fed) & (lax.div(5 * chunk, 4) == wait))
            def _():
                double(refs, chunk, stage)

        for stage in stages:
            chunk = slot - 1 - HALVING_LAGS[stage]

            @pl.when((chunk >= 0) & (chunk <= fed))
            def _():
                halve(refs, chunk, stage)

        for stage in stages if doubling else ():
            wait = slot - LATE_SLOT - LATE_LAGS[stage]

            @pl.when((wait >= 0) & (lax.rem(wait, LATE_EVERY) == 0))
            def _():
                halve(refs, fed + 1 + lax.div(wait, LATE_EVERY), stage)

    MIXED, LOW, SLOPE_GATE, SLOPE_UP, HIDDEN, GATE, UP, SIDED_CONTEXT, WD, WG, WU, WO, CONTEXT = range(13)
    ATTENDED, Q, K, V, GRAD_CONTEXT, PROJECTED, TOKENS = MIXED, SLOPE_GATE, SLOPE_UP, WD, HIDDEN, GATE, WG
    WQ = (WU, WO, LOW)
    blocks = wg.shape[1] // width
    fed = 3 * blocks

    def block_loads(j):
        cols = aligned(j * width, width)
        return {
            SLOPE_GATE: load(SLOPE_GATE, slope_gate.at[:, cols]),
            SLOPE_UP: load(SLOPE_UP, slope_up.at[:, cols]),
            WD: load(WD, wd.at[cols, :], square(WD)),
            WG: load(WG, wg.at[:, cols], square(WG)),
            WU: load(WU, wu.at[:, cols], square(WU)),
        }

    def hidden_load(j):
        rows = wd.shape[0] // 2
        return sided(HIDDEN + j, hidden, core * rows + j * shard, (1 - core) * rows + j * shard)

    def wq_loads(turn_number):
        part = width // 3
        return tuple(
            pltpu.make_async_copy(
                wq.at[:, aligned(n * width + turn_number * part, part)],
                arena.at[WQ[turn_number], pl.ds(0, width), pl.ds(n * part, part)],
                wq_sems.at[turn_number, n],
            )
            for n in range(3)
        )

    def feature_load(pair):
        slot = lax.rem(pair, 2)
        return pltpu.make_async_copy(
            features.at[pl.ds(2 * pair, 2)], marks.at[slot], feature_sems.at[slot]
        )

    first_loads = block_loads(0)
    mixed_load = load(MIXED, mixed)
    low_load = sided(LOW, low, core * shard, (1 - core) * shard)
    second_load = pltpu.make_async_copy(grad_second, total, extra_sems.at[0])
    block = 256

    def unit_load(r):
        return pltpu.make_async_copy(unit_in.at[pl.ds(r * block, block)], unit.at[r % 2], unit_sems.at[r % 2])

    table_loads = [
        pltpu.make_async_copy(source, target, table_sems.at[n])
        for n, (source, target) in enumerate(((inv_in, inv), (cosines_in, cosines), (sines_in, sines)))
    ]
    context_load = load(CONTEXT, context)
    sided_load = sided(SIDED_CONTEXT, context, core * shard, (1 - core) * shard)
    wo_load = load(WO, wo, square(WO))
    late_loads = {
        Q: load(Q, q_in),
        K: load(K, k_in),
        V: load(V, v_in),
        TOKENS: sided(TOKENS, tokens, core * shard, (1 - core) * shard),
    }
    for one in (mixed_load, hidden_load(0), hidden_load(1), hidden_load(2), hidden_load(3), first_loads[WD],
                first_loads[SLOPE_GATE], first_loads[SLOPE_UP], low_load, first_loads[WG], second_load,
                first_loads[WU], wo_load, unit_load(0), unit_load(1), context_load, feature_load(0),
                *table_loads):
        begin(one)
    vectors[0] = vec[...]
    greet()
    finish(mixed_load)

    tile = 512

    def down_step(j, carry):
        finish(hidden_load(j))
        emit(j, HIDDEN + j, MIXED)

        @pl.when(j > 0)
        def _():
            absorb(j - 1)
            slot_work(j, False)

        return carry

    lax.fori_loop(0, blocks, down_step, 0)
    begin(sided_load)
    finish(low_load)
    finish(second_load)

    def feed_step(j, carry):
        loads = block_loads(j)
        upcoming = block_loads(j + 1)
        more = j + 1 < blocks
        chunk = blocks + 2 * j

        def renew(*slots):
            @pl.when(more)
            def _():
                for slot in slots:
                    begin(upcoming[slot])

        def replace(*slots):
            @pl.when(jnp.logical_not(more))
            def _():
                for slot in slots:
                    begin(late_loads[slot])

        for slot in (WD, SLOPE_GATE, SLOPE_UP):
            finish(loads[slot])
        for r in range(seq // tile):
            rows = pl.ds(r * tile, tile)
            grad_hidden = nt(arena[MIXED, rows, :], arena[WD, :width, :])
            arena[GATE, rows, :] = (grad_hidden * arena[SLOPE_GATE, rows, :].astype(F32)).astype(BF16)
            arena[UP, rows, :] = (grad_hidden * arena[SLOPE_UP, rows, :].astype(F32)).astype(BF16)
        renew(WD, SLOPE_GATE, SLOPE_UP)
        replace(Q, K, V)
        emit(chunk, LOW, GATE)
        finish(loads[WG])
        for r in range(seq // tile):
            rows = pl.ds(r * tile, tile)
            total[rows, :] += nt(arena[GATE, rows, :], arena[WG, :width, :])
        renew(WG)
        replace(TOKENS)
        absorb(chunk - 1)
        slot_work(chunk, False)
        emit(chunk + 1, LOW, UP)
        finish(loads[WU])
        for r in range(seq // tile):
            rows = pl.ds(r * tile, tile)
            total[rows, :] += nt(arena[UP, rows, :], arena[WU, :width, :])
        renew(WU)
        absorb(chunk)
        slot_work(chunk + 1, False)
        return carry

    lax.fori_loop(0, blocks, feed_step, 0)

    begin(wq_loads(0))
    begin(wq_loads(2))
    gain_one = jnp.concatenate([norms[0, 0:1, :], norms[1, 0:1, :]], axis=1)
    for one in table_loads:
        one.wait()
    bias_sum = jnp.zeros((1, width), F32)
    gain_sum = jnp.zeros((1, width), F32)
    for r in range(seq // block):
        rows = pl.ds(r * block, block)
        grad_normed = total[rows, :]
        unit_load(r).wait()
        unit_rows = unit[r % 2]
        bias_sum += jnp.sum(grad_normed, axis=0, keepdims=True)
        gain_sum += jnp.sum(grad_normed * unit_rows, axis=0, keepdims=True)
        scaled = grad_normed * gain_one
        grad_first = inv[rows, 0:1] * (scaled - row_mean(scaled) - unit_rows * row_mean(scaled * unit_rows))
        total[rows, :] = grad_first
        arena[ATTENDED, rows, :] = grad_first.astype(BF16)
        if r + 2 < seq // block:
            unit_load(r + 2).start()
    vectors[0, 0:1, :] = gain_sum
    vectors[0, 1:2, :] = bias_sum
    finish(sided_load)
    emit(fed, SIDED_CONTEXT, ATTENDED)
    finish(wo_load)
    absorb(fed - 1)
    slot_work(fed, False)
    for r in range(seq // tile):
        rows = pl.ds(r * tile, tile)
        arena[GRAD_CONTEXT, rows, :] = nt(arena[ATTENDED, rows, :], arena[WO, :width, :]).astype(BF16)
    begin(wq_loads(1))
    absorb(fed)
    for one in (context_load, late_loads[Q], late_loads[K], late_loads[V], late_loads[TOKENS]):
        finish(one)

    ones = jnp.where((lanes() >= SPLIT_LANE) & (lanes() < SPLIT_LANE + 3), 1.0, 0.0)
    part = width // 3
    block_count = seq // block

    def head_step(turn_number, number, carry):
        pair = 2 * turn_number + lax.div(number, 2)
        head = lax.rem(number, 2)
        place = lax.div(number, 2) * 128
        cols = aligned(pair * 128, 128)
        mark_slot = lax.rem(pair, 2)
        own_lanes = lax.div(lanes(), HEAD_DIM) == head

        def only(values):
            return jnp.where(own_lanes, values, jnp.zeros_like(values))

        @pl.when(head == 0)
        def _():
            feature_load(pair).wait()

            @pl.when(pair + 1 < HEADS // 2)
            def _():
                feature_load(pair + 1).start()

            key_aug[:, :128] = arena[K, :, cols]
            key_aug[:, 128:] = (key_marks[...].astype(F32) + ones).astype(BF16)
            value_aug[:, :128] = arena[V, :, cols]
            value_aug[:, 128:] = jnp.broadcast_to(ones, (seq, 128)).astype(BF16)
            turned_rows[0] = jnp.transpose(arena[Q, :, cols])
            turned_rows[1] = jnp.transpose(arena[GRAD_CONTEXT, :, cols])

        def products_of(r):
            rows = pl.ds(r * block, block)
            query = jnp.concatenate([only(arena[Q, rows, cols]), marks[mark_slot, head, rows, :]], axis=1)
            grads_here = only(arena[GRAD_CONTEXT, rows, cols])
            delta = jnp.sum(grads_here.astype(F32) * arena[CONTEXT, rows, cols].astype(F32), axis=1, keepdims=True)
            tail = split_lanes(jnp.zeros((block, 128), F32), -delta)
            return nt(query, key_aug[...]), nt(jnp.concatenate([grads_here, tail], axis=1), value_aug[...])

        key_only = only(key_aug[:, :128])
        upcoming = products_of(0)
        for r in range(block_count):
            rows = pl.ds(r * block, block)
            scores, grad_probs = upcoming
            upcoming = products_of(r + 1) if r + 1 < block_count else None
            probs = jnp.exp(scores)
            grad_scores = (probs * grad_probs).astype(BF16)
            probs_kept[rows, :] = probs.astype(BF16)
            scores_kept[rows, :] = grad_scores
            dquery_term = nn(grad_scores, key_only)

            dquery[rows, :] = jnp.where(head == 0, 0.0, dquery[rows, :]) + dquery_term

        own_rows = aligned(head * HEAD_DIM, HEAD_DIM)
        dkey[own_rows, :] = nn(turned_rows[0, own_rows, :], scores_kept[...])
        dvalue[own_rows, :] = nn(turned_rows[1, own_rows, :], probs_kept[...])

        @pl.when(head == 1)
        def _():
            turned = turn(dquery[...] * (HEAD_DIM ** (-0.5)), cosines[...], -sines[...])
            arena[PROJECTED + turn_number, :, aligned(place, 128)] = turned.astype(BF16)
            turned = turn(jnp.transpose(dkey[...]), cosines[...], -sines[...])
            arena[PROJECTED + turn_number, :, aligned(part + place, 128)] = turned.astype(BF16)
            arena[PROJECTED + turn_number, :, aligned(2 * part + place, 128)] = jnp.transpose(dvalue[...]).astype(BF16)

        slot_work(FIRST_ATTENTION + LATE_EVERY * turn_number + number, True)
        for stage in range(VECTOR_STEPS + 1):

            @pl.when(4 * turn_number + number == stage)
            def _():
                vector_stage(vectors, vec_send, vec_recv, stage)

        return carry

    def turn_step(turn_number, carry):
        lax.fori_loop(0, 4, functools.partial(head_step, turn_number), 0)
        chunk = fed + 1 + turn_number
        emit(chunk, TOKENS, PROJECTED + turn_number)
        absorb(chunk)
        slot_work(LATE_SLOT + LATE_EVERY * turn_number, True)
        return carry

    lax.fori_loop(0, 3, turn_step, 0)

    half = seq // 2
    mine = pltpu.make_async_copy(total.at[aligned(core * half, half)], input_grad_out.at[core], extra_sems.at[2])
    theirs = pltpu.make_async_remote_copy(
        src_ref=total.at[aligned((1 - core) * half, half)],
        dst_ref=input_grad_out.at[core],
        send_sem=core_send.at[RING],
        recv_sem=core_recv.at[RING],
        device_id=other_core(),
        device_id_type=MESH,
    )
    vec_out[...] = vectors[2 * VECTOR_STEPS]
    for number, (work, chunk, stage) in enumerate(REMAINDER):
        work(refs, chunk, stage)
        turn_number, odd = divmod(number, 3)
        if odd == 0 and turn_number < 3:
            finish(wq_loads(turn_number))
            for r in range(seq // tile):
                rows = pl.ds(r * tile, tile)
                total[rows, :] += nt(arena[PROJECTED + turn_number, rows, :], arena[WQ[turn_number], :width, :])
            if turn_number == 2:
                mine.start()
                theirs.start()
    mine.wait()
    theirs.wait()
    for number in range(2):
        core_copy(CHUNKS - 2 + number).wait_send()


def backward(tokens, saved, norms, key_marks, cosines, sines, vec, weights, outs):
    context, low, mixed, hidden, slope_gate, slope_up, grad_second, unit, inv, q, k, v, features = saved
    seq, width = tokens.shape
    dma = pltpu.SemaphoreType.DMA
    vmem = pl.BlockSpec(memory_space=pltpu.VMEM)
    hbm = pl.BlockSpec(memory_space=pl.ANY)
    chunks = (CHUNKS, width // 2, width)
    return pl.pallas_call(
        backward_kernel,
        out_shape=(
            jax.ShapeDtypeStruct(chunks, BF16),
            jax.ShapeDtypeStruct(outs, F32),
            jax.ShapeDtypeStruct(vec.shape, F32),
        ),
        in_specs=[hbm] * 10 + [vmem] + [hbm] * 4 + [vmem] + [hbm] * 2 + [vmem] + [hbm] * 5,
        out_specs=(hbm, hbm, vmem),
        scratch_shapes=[
            pltpu.VMEM(chunks, BF16),
            pltpu.VMEM((HALVES_RING,) + chunks[1:], BF16),
            pltpu.VMEM((RING,) + chunks[1:], BF16),
            pltpu.VMEM((2,) + chunks[1:], BF16),
            pltpu.VMEM((2 * VECTOR_STEPS + 1,) + vec.shape, F32),
            pltpu.VMEM((13, seq, width), BF16),
            pltpu.VMEM((seq, width), F32),
            pltpu.VMEM((2, 256, width), F32),
            pltpu.VMEM((2, 2, seq, FEATURES), BF16),
            pltpu.VMEM((seq, 256), BF16),
            pltpu.VMEM((seq, 256), BF16),
            pltpu.VMEM((seq, seq), BF16),
            pltpu.VMEM((seq, seq), BF16),
            pltpu.VMEM((2, 128, seq), BF16),
            pltpu.VMEM((seq, 128), F32),
            pltpu.VMEM((128, seq), F32),
            pltpu.VMEM((128, seq), F32),
            pltpu.VMEM((seq, 128), F32),
            pltpu.VMEM((seq, 128), F32),
            pltpu.VMEM((seq, 128), F32),
            dma((HALVES_RING, 2 * STEPS + 1)),
            dma((HALVES_RING, 2 * STEPS)),
            dma((RING + 1,)),
            dma((RING + 1,)),
            dma((VECTOR_STEPS,)),
            dma((VECTOR_STEPS,)),
            dma((13,)),
            dma((13,)),
            dma((3,)),
            dma((3, 3)),
            dma((2,)),
            dma((2,)),
            dma((3,)),
        ],
        compiler_params=pltpu.CompilerParams(collective_id=0, has_side_effects=True, vmem_limit_bytes=63 << 20),
    )(tokens, context, low, mixed, hidden, slope_gate, slope_up, grad_second, unit, inv, norms, q, k, v,
      features, key_marks, cosines, sines, vec, *weights)


def finish_kernel(
    summed, vec, activations, input_grad,
    activations_out, input_grad_out, qkv, out, gate, up, down, gain_one, bias_one, gain_two, bias_two,
    narrow, wide, acts, inputs, in_sems, out_sems, pass_sems,
):
    rows, width = narrow.shape[1:]
    part = width // 3
    fed = CHUNKS - 4
    held = ((activations, acts, activations_out), (input_grad, inputs, input_grad_out))
    fetches = [pltpu.make_async_copy(source, place, pass_sems.at[n]) for n, (source, place, _) in enumerate(held)]
    passes = [pltpu.make_async_copy(place, target, pass_sems.at[n]) for n, (_, place, target) in enumerate(held)]
    loads = [pltpu.make_async_copy(summed.at[n], narrow.at[n], in_sems.at[n]) for n in range(CHUNKS)]
    for load in loads[:4] + fetches + loads[4:]:
        load.start()
    core = lax.axis_index("fsdp")
    for n, ref in enumerate((gain_one, bias_one, gain_two, bias_two)):
        ref[...] = vec[n, aligned(core * rows, rows, 128)]
    stores = []
    for n in range(CHUNKS):
        if n == 4:
            for fetch, store in zip(fetches, passes):
                fetch.wait()
                store.start()
        loads[n].wait()
        wide[n] = narrow[n].astype(F32)
        if n < 4:
            parts = [(wide.at[n], down.at[pl.ds(rows * n, rows)])]
        elif n < fed:
            parts = [(wide.at[n], (gate, up)[n % 2].at[:, pl.ds(width * ((n - 4) // 2), width)])]
        elif n == fed:
            parts = [(wide.at[n], out)]
        else:
            parts = [
                (wide.at[n, :, pl.ds(m * part, part)], qkv.at[:, pl.ds(m * width + (n - fed - 1) * part, part)])
                for m in range(3)
            ]
        for source, target in parts:
            stores.append(pltpu.make_async_copy(source, target, out_sems.at[len(stores)]))
            stores[-1].start()
    for store in stores + passes:
        store.wait()


def finish(summed, vec, activations, input_grad):
    rows, cols = summed.shape[1:]
    vmem = pl.BlockSpec(memory_space=pltpu.VMEM)
    hbm = pl.BlockSpec(memory_space=pl.ANY)

    def shape(high, across):
        return jax.ShapeDtypeStruct((rows * high, cols * across), F32)

    def like(array):
        return jax.ShapeDtypeStruct(array.shape, array.dtype)

    return pl.pallas_call(
        finish_kernel,
        out_shape=(like(activations), like(input_grad), shape(1, 3), shape(1, 1), shape(1, 4), shape(1, 4), shape(4, 1))
        + (jax.ShapeDtypeStruct((rows,), F32),) * 4,
        in_specs=[hbm, vmem, hbm, hbm],
        out_specs=(hbm,) * 7 + (vmem,) * 4,
        scratch_shapes=[
            pltpu.VMEM(summed.shape, BF16),
            pltpu.VMEM(summed.shape, F32),
            pltpu.VMEM(activations.shape, activations.dtype),
            pltpu.VMEM(input_grad.shape, input_grad.dtype),
            pltpu.SemaphoreType.DMA((CHUNKS,)),
            pltpu.SemaphoreType.DMA((CHUNKS + 6,)),
            pltpu.SemaphoreType.DMA((2,)),
        ],
        compiler_params=pltpu.CompilerParams(vmem_limit_bytes=62 << 20),
    )(summed, vec, activations, input_grad)


def shards(
    tokens,
    lengths,
    w_qkv,
    w_out,
    w_gate,
    w_up,
    w_down,
    norm1_gain,
    norm1_bias,
    norm2_gain,
    norm2_bias,
    cotangent,
):
    norms = (norm1_gain, norm1_bias, norm2_gain, norm2_bias)
    weights = (w_qkv, w_out, w_gate, w_up, w_down)
    (q, k, v, context, features, low, unit, inv, slope_gate, slope_up, hidden, grad_second, mixed, activations,
     vec, norms, key_marks, cosines, sines, stream, *weights) = forward(tokens, cotangent, weights, norms, lengths)
    saved = (context, low, mixed, hidden, slope_gate, slope_up, grad_second, unit, inv, q, k, v, features)
    summed, input_grad, vec_sum = backward(
        stream, saved, norms, key_marks, cosines, sines, vec, weights, tokens.shape
    )
    groups = lax.axis_size("rep") // UNITS
    if groups > 1:
        alike = [[UNITS * g + n for g in range(groups)] for n in range(UNITS)]
        summed = lax.psum(summed, "rep", axis_index_groups=alike)
        vec_sum = lax.psum(vec_sum, "rep", axis_index_groups=alike)
    return finish(summed, vec_sum, activations, input_grad)


def solution(mesh):
    placed = (
        P("rep", "fsdp", None),
        P("rep", None),
        P("fsdp", None),
        P("fsdp", None),
        P("fsdp", None),
        P("fsdp", None),
        P("fsdp", None),
        P("fsdp"),
        P("fsdp"),
        P("fsdp"),
        P("fsdp"),
        P("rep", "fsdp", None),
    )
    return jax.shard_map(
        shards,
        mesh=mesh,
        in_specs=placed,
        out_specs=(
            P("rep", "fsdp", None),
            P("rep", "fsdp", None),
            P("fsdp", None),
            P("fsdp", None),
            P("fsdp", None),
            P("fsdp", None),
            P("fsdp", None),
            P("fsdp"),
            P("fsdp"),
            P("fsdp"),
            P("fsdp"),
        ),
        check_vma=False,
    )
```
